256 devices in a mesh: gz: 16 (over z, core), gy: 4 (over y), gx: 4 (over x).
Axes of the slice: x: 4, y: 4, z: 8, core: 2. Of those that a mesh axis runs over, the one named last changes fastest.
Arguments:
- forward: float32 [6, 256, 64, 512], P(None, 'gz', 'gy', 'gx'), may hold values from -26 to 26
- adjoint_prev: float32 [6, 256, 64, 512], P(None, 'gz', 'gy', 'gx'), may hold values from -6 to 6
- density: float32 [256, 64, 512], P('gz', 'gy', 'gx'), may hold values from 0.05 to 1
- labels: int32 [256, 64, 512], P('gz', 'gy', 'gx'), may hold values from 0 to 2
- ports: int32 [256, 64, 512], P('gz', 'gy', 'gx'), may hold values 0 or 1
- z_target: float32 [2], replicated, may hold values from -4 to 4
- radius_z: int32 [256], replicated, may hold values from 8 to 16, as said below
- radius_y: int32 [64], replicated, may hold values from 8 to 16, as said below
- radius_x: int32 [512], replicated, may hold values from 8 to 16, as said below
Outputs:
- adjoint: float32 [6, 256, 64, 512], P(None, 'gz', 'gy', 'gx')
- gradient: float32 [256, 64, 512], P('gz', 'gy', 'gx')
- impedance: float32 [2], replicated
The draws below stay inside these ranges and needn't reach their ends.
Inputs may be any that keep to these rules, and one draw needn't show every extreme that they name: `labels`: 0 air, 1 coil, 2 design. `ports`: 1 marks a port cell. `radius_z`: both ends of the range occur along the axis. `radius_y`: both ends of the range occur along the axis. `radius_x`: both ends of the range occur along the axis.
All inputs are finite; a program needn't handle non-finite values. No bound on the sum of `ports` on one device may be relied on, other than what follows from the above.
Results may differ from the reference program's by a relative error of at most 0.0001.
Values sent between devices are 32-bit elements; how exact they have to be, the bound alone decides.
A program may use at most 64 MiB of HBM per device.

```python
import math
import jax
import jax.numpy as jnp
from jax import lax

SWEEPS = 2
RADIUS = 16
NZ = 256
NY = 64
NX = 512


def draw_forward(key, part):
    noise_key = jax.random.fold_in(key, 101)
    depth_frac = jnp.arange(NZ).astype(jnp.float32) / NZ
    envelope = jnp.exp(depth_frac * math.log(3.0))
    noise = jnp.clip(jax.random.normal(noise_key, (6, NZ, NY, NX), jnp.float32), -5.0, 5.0)
    offsets = jnp.array([0.0, 0.0, 1.0, 0.0, 0.0, 0.5], jnp.float32)
    return (offsets[:, None, None, None] + noise) * envelope[None, :, None, None]


def radius_line(key, count):
    values = jax.random.randint(key, (count,), RADIUS // 2, RADIUS + 1)
    positions = jax.random.permutation(jax.random.fold_in(key, 7), count)
    values = values.at[positions[0]].set(RADIUS)
    return values.at[positions[1]].set(RADIUS // 2)


def draw_radius_z(key, part):
    return radius_line(jax.random.fold_in(key, 211), NZ)


def draw_radius_y(key, part):
    return radius_line(jax.random.fold_in(key, 223), NY)


def draw_radius_x(key, part):
    return radius_line(jax.random.fold_in(key, 227), NX)


def place_ends(drawn, rng, least, largest):
    index_at = [jax.random.randint(jax.random.fold_in(rng, axis), (), 0, length) for axis, length in enumerate(drawn.shape)]
    main_axis = drawn.shape.index(max(drawn.shape))
    beside = index_at[:main_axis] + [(index_at[main_axis] + 1) % drawn.shape[main_axis]] + index_at[main_axis + 1:]
    return drawn.at[tuple(index_at)].set(least).at[tuple(beside)].set(largest)


def block_scale(stream_key, dims, shards, least, top_value):
    def one(position, parts):
        heights = jax.random.uniform(jax.random.fold_in(jax.random.fold_in(stream_key, 6), position), (parts,), jnp.float32, least / len(shards), top_value / len(shards))
        return jnp.repeat(jnp.exp(heights), dims[position] // parts).reshape((-1,) + (1,) * (len(dims) - position - 1))

    gain = one(*shards[0])
    for cut in shards[1:]:
        gain = gain * one(*cut)
    return gain


def bell_draw(key, extent, deviation, reach, cuts=(), held_as=jnp.bfloat16):
    values = deviation * jax.random.normal(key, extent, jnp.float32)
    if cuts:
        values = values * block_scale(key, extent, cuts, -0.22, 0.18)
    return jnp.clip(values, -reach, reach).astype(held_as)


def setup_inputs(seed: int = 0) -> dict:
    seeds = jax.random.split(jax.random.key(seed), 10)
    forward = draw_forward(jax.random.fold_in(seeds[9], 71), 0)
    adjoint_prev = bell_draw(seeds[1], (6, NZ, NY, NX), 1.0, 6.0, ((1, 16), (2, 4), (3, 4)), jnp.float32)
    density = jnp.clip(0.05 + 0.95 * jax.random.uniform(seeds[2], (NZ, NY, NX), jnp.float32) ** block_scale(seeds[2], (NZ, NY, NX), ((0, 16), (1, 4), (2, 4)), -0.2, 0.2), 0.05, 1.0)
    labels = place_ends(jax.random.randint(seeds[3], (NZ, NY, NX), 0, 3), jax.random.fold_in(seeds[3], 1), 0, 2).astype(jnp.int32)
    ports = place_ends((jax.random.randint(seeds[4], (NZ, NY, NX), 0, 4) < 1).astype(jnp.int32), jax.random.fold_in(seeds[4], 1), 0, 1)
    z_target = bell_draw(seeds[5], (2,), 1.0, 4.0, (), jnp.float32)
    radius_z = draw_radius_z(jax.random.fold_in(seeds[9], 71), 0)
    radius_y = draw_radius_y(jax.random.fold_in(seeds[9], 71), 0)
    radius_x = draw_radius_x(jax.random.fold_in(seeds[9], 71), 0)
    return dict(forward=forward, adjoint_prev=adjoint_prev, density=density, labels=labels, ports=ports, z_target=z_target, radius_z=radius_z, radius_y=radius_y, radius_x=radius_x)


MU_GAIN = 19.0
KAPPA_GAIN = 2.0
RELAX = 0.8
SENS_GAIN = 0.1


def material(labels, density):
    design = (labels == 2).astype(jnp.float32)
    square = density * density
    density_cube = square * density
    nu_design = 1.0 / (1.0 + MU_GAIN * density_cube)
    nu_cell = 1.0 - design + design * nu_design
    kappa_sigma = design * KAPPA_GAIN * density_cube
    nu_slope = -3.0 * MU_GAIN * design * square * nu_design * nu_design
    sigma_slope = 3.0 * KAPPA_GAIN * design * square
    return nu_cell, kappa_sigma, nu_slope, sigma_slope


def neighbours(padded):
    return [padded[..., 2:, 1:-1, 1:-1], padded[..., :-2, 1:-1, 1:-1],
            padded[..., 1:-1, 2:, 1:-1], padded[..., 1:-1, :-2, 1:-1],
            padded[..., 1:-1, 1:-1, 2:], padded[..., 1:-1, 1:-1, :-2]]


def relax_step(current, padded, face_nu, diag_re, kappa_sigma, source):
    applied = diag_re * current
    for nu_face, beside in zip(face_nu, neighbours(padded)):
        applied = applied - nu_face * beside
    image_re = applied[:3] - kappa_sigma * current[3:]
    image_im = applied[3:] + kappa_sigma * current[:3]
    rest_re = source[:3] - image_re
    rest_im = source[3:] - image_im
    denominator = diag_re * diag_re + kappa_sigma * kappa_sigma
    step_re = (rest_re * diag_re + rest_im * kappa_sigma) / denominator
    step_im = (rest_im * diag_re - rest_re * kappa_sigma) / denominator
    return current + RELAX * jnp.concatenate([step_re, step_im], axis=0)


def sensitivity(adjoint, padded_adj, forward, padded_fwd, nu_slope, sigma_slope):
    energy = jnp.zeros(forward.shape[1:], jnp.float32)
    for adj_near, fwd_near in zip(neighbours(padded_adj), neighbours(padded_fwd)):
        diff_adj = adjoint - adj_near
        diff_fwd = forward - fwd_near
        energy = energy + jnp.sum(diff_adj[:3] * diff_fwd[:3] - diff_adj[3:] * diff_fwd[3:], axis=0)
    cross_term = jnp.sum(adjoint[:3] * forward[3:] + adjoint[3:] * forward[:3], axis=0)
    power_term = jnp.sum(forward * forward, axis=0)
    return SENS_GAIN * (-nu_slope * 0.5 * energy + sigma_slope * (cross_term + power_term))


def band_matrix(radius_rows, count, shift):
    row_count = radius_rows.shape[0]
    source_pos = lax.broadcasted_iota(jnp.int32, (row_count, count), 0)
    target_pos = lax.broadcasted_iota(jnp.int32, (row_count, count), 1)
    distance = jnp.abs(source_pos - shift - target_pos)
    return jnp.maximum(radius_rows[:, None] + 1 - distance, 0).astype(jnp.float32)


def port_pattern(port_mask, coef_re, coef_im):
    zeros_plane = jnp.zeros_like(port_mask)
    return jnp.stack([zeros_plane, zeros_plane, coef_re * port_mask, zeros_plane, zeros_plane, coef_im * port_mask], axis=0)


def reference(forward, adjoint_prev, density, labels, ports, z_target, radius_z, radius_y, radius_x):
    nu_cell, kappa_sigma, nu_slope, sigma_slope = material(labels, density)
    padded_nu = jnp.pad(nu_cell, 1, constant_values=1.0)
    face_nu = [0.5 * (nu_cell + beside) for beside in neighbours(padded_nu)]
    diag_re = face_nu[0]
    for nu_face in face_nu[1:]:
        diag_re = diag_re + nu_face
    port_mask = ports.astype(jnp.float32)
    link_scale = 4.0 / (NX * NY * NZ)
    link_re = link_scale * jnp.sum(port_mask * forward[2])
    link_im = link_scale * jnp.sum(port_mask * forward[5])
    coef_re = 2.0 * (link_re - z_target[0])
    coef_im = -2.0 * (link_im - z_target[1])
    source = kappa_sigma * forward + port_pattern(port_mask, coef_re, coef_im)
    widths = ((0, 0), (1, 1), (1, 1), (1, 1))
    adjoint = adjoint_prev
    for sweep_index in range(SWEEPS):
        adjoint = relax_step(adjoint, jnp.pad(adjoint, widths), face_nu, diag_re, kappa_sigma, source)
    sens_field = sensitivity(adjoint, jnp.pad(adjoint, widths), forward, jnp.pad(forward, widths), nu_slope, sigma_slope)
    band_z = band_matrix(radius_z, NZ, 0)
    band_y = band_matrix(radius_y, NY, 0)
    band_x = band_matrix(radius_x, NX, 0)
    norm_z = jnp.sum(band_z, axis=1)
    norm_y = jnp.sum(band_y, axis=1)
    norm_x = jnp.sum(band_x, axis=1)
    scaled = sens_field / (norm_z[:, None, None] * norm_y[None, :, None] * norm_x[None, None, :])
    highest = lax.Precision.HIGHEST
    filtered = jnp.einsum("ayx,aj->jyx", scaled, band_z, precision=highest)
    filtered = jnp.einsum("zbx,bk->zkx", filtered, band_y, precision=highest)
    filtered = jnp.einsum("zya,aj->zyj", filtered, band_x, precision=highest)
    return adjoint, filtered, jnp.stack([link_re, link_im])
```

```python
import jax
import jax.numpy as jnp
from jax import lax
from jax.experimental import pallas as pl
from jax.experimental.pallas import tpu as pltpu
from jax.sharding import PartitionSpec as P

MU_GAIN = 19.0
KAPPA_GAIN = 2.0
RELAX = 0.8
SENS_GAIN = 0.1
REACH = 16
MESH = pl.DeviceIdType.MESH
AXES = ("gz", "gy", "gx")
F32 = jnp.float32
BF16 = jnp.bfloat16
D = 16
H = 16
L = 128


def plane(index):
    return pl.ds(pl.multiple_of(index * H, H), H)


def tri(value):
    value = jnp.maximum(value, 0)
    return value * (value + 1) // 2


def norm_of(radius, position, length):
    whole = (radius + 1) * (radius + 1)
    return whole - tri(radius - position) - tri(radius - (length - 1 - position))


def make_kernel(sizes):
    nz, ny, nx = sizes["gz"], sizes["gy"], sizes["gx"]
    total = {"gz": nz * D, "gy": ny * H, "gx": nx * L}
    scale = 4.0 / (total["gz"] * total["gy"] * total["gx"])
    flat = ny * nx

    def kernel(fwd_h, adj_h, den_h, lab_h, prt_h, zt, rz, ry, rx,
               adj_o, grad_o, imp_o,
               f, a0, den, lab, prt, a1, a2, t,
               nu, kap, wzm, wzp, wym, wyp, wxm, wxp, al, be, hx, kk, qq, s,
               zs0, ys0, xs0, zr0, yr0, xr0,
               zsf, ysf, xsf, zrf, yrf, xrf,
               zs1, ys1, xs1, zr1, yr1, xr1,
               zs2, ys2, xs2, zr2, yr2, xr2,
               ky, kz, bx, pb, ysF, yrF, zsF, zrF, st, sr, vb, xin,
               ar1, ar2, in_sem, out_sem,
               ss, rs, as1, ar_s1, as2, ar_s2):
        gz, gy, gx = (lax.axis_index(a) for a in AXES)
        pos = {"gz": gz, "gy": gy, "gx": gx}
        here = gy * nx + gx

        def plane_peer(d):
            q = lax.rem(here + d, flat)
            return {"gy": q // nx, "gx": lax.rem(q, nx)}

        def line_peer(d):
            return {"gz": lax.rem(gz + d, nz)}

        barrier = pltpu.get_barrier_semaphore()

        def greet_plane(d, _):
            pl.semaphore_signal(barrier, inc=1, device_id=plane_peer(d), device_id_type=MESH)
            return 0

        def greet_line(d, _):
            pl.semaphore_signal(barrier, inc=1, device_id=line_peer(d), device_id_type=MESH)
            return 0

        lax.fori_loop(1, flat, greet_plane, 0)
        lax.fori_loop(1, nz, greet_line, 0)
        diagonals = [(dz, dx) for dz in (-1, 1) for dx in (-1, 1)]

        def inside(axis, d):
            size = {"gz": nz, "gy": ny, "gx": nx}[axis]
            return pos[axis] < size - 1 if d > 0 else pos[axis] > 0

        for dz, dx in diagonals:
            @pl.when(jnp.logical_and(inside("gz", dz), inside("gx", dx)))
            def _():
                pl.semaphore_signal(barrier, inc=1, device_id={"gz": gz + dz, "gx": gx + dx}, device_id_type=MESH)

        loads = [
            pltpu.make_async_copy(src, dst, in_sem.at[k])
            for k, (src, dst) in enumerate(((den_h, den), (lab_h, lab), (adj_h, a0), (fwd_h, f), (prt_h, prt)))
        ]
        for load in loads:
            load.start()

        def remote(src, dst, slot, where):
            return pltpu.make_async_remote_copy(
                src_ref=src, dst_ref=dst, send_sem=ss.at[slot], recv_sem=rs.at[slot],
                device_id=where, device_id_type=MESH)

        sent = []

        def beside(axis, d, src, dst, slot):
            copy = remote(src, dst, slot, {axis: pos[axis] + d})
            pl.when(inside(axis, d))(copy.start)
            sent.append((inside(axis, d), copy))
            return (inside(axis, -d), copy)

        def arrive(copies):
            for cond, copy in copies:
                pl.when(cond)(copy.wait_recv)

        def exchange(base, zs, zr, ys, yr, xs, xr):
            copies = []
            for axis, src, dst, k in (("gy", ys, yr, 2), ("gx", xs, xr, 4), ("gz", zs, zr, 0)):
                for d in (-1, 1):
                    side = 0 if d < 0 else 1
                    piece = src if axis == "gx" else src.at[side]
                    copies.append(beside(axis, d, piece, dst.at[1 - side], base + k + side))
            return copies

        edges = {axis: (pos[axis] == 0, pos[axis] == {"gz": nz, "gy": ny, "gx": nx}[axis] - 1) for axis in AXES}
        for axis, bufs in (("gz", (zr0, zrf, zr1, zr2, zrF)), ("gy", (yr0, yrf, yr1, yr2, yrF)),
                           ("gx", (xr0, xrf, xr1, xr2, sr))):
            for side in (0, 1):
                @pl.when(edges[axis][side])
                def _():
                    for buf in bufs:
                        buf[side] = jnp.zeros(buf.shape[1:], F32)
                    if axis == "gx":
                        column = lax.rem(lax.broadcasted_iota(jnp.int32, (H, L), 1), 8)
                        xr0[side, 1] = jnp.where(column // 2 == 2, 1.0, 0.0).astype(F32)
                    else:
                        buf = zr0 if axis == "gz" else yr0
                        buf[side, pl.ds(6 * H, H), :] = jnp.ones((H, L), F32)
        for side, dz_ in ((0, 1), (1, 1)):
            for low in (0, 1):
                @pl.when(edges["gz"][low])
                def _():
                    sr[side, 1 + low] = jnp.zeros(sr.shape[2:], F32)

        lane = lax.broadcasted_iota(jnp.int32, (H, L), 1)
        row = lax.broadcasted_iota(jnp.int32, (H, L), 0)

        lane2 = lax.broadcasted_iota(jnp.int32, (H, 2 * L), 1)
        row2 = lax.broadcasted_iota(jnp.int32, (H, 2 * L), 0)
        low4 = lax.rem(lane2, H)
        high4 = lane2 // H
        ry_l = jnp.zeros((H, 2 * L), jnp.int32)
        rz_l = jnp.zeros((H, 2 * L), jnp.int32)
        ry_r = jnp.zeros((H, L), jnp.int32)
        for b in range(H):
            ry_b = ry[gy * H + b]
            rz_b = rz[gz * D + b]
            ry_l = jnp.where(low4 == b, ry_b, ry_l)
            rz_l = jnp.where(high4 == b, rz_b, rz_l)
            ry_r = jnp.where(row == b, ry_b, ry_r)

        def build(k, _):
            shift = (k // D - 1) * D
            p = lax.rem(k, D)
            band_y = jnp.maximum(ry_l + 1 - jnp.abs(low4 - (row2 + shift)), 0)
            ky[plane(k), :] = jnp.where(high4 == p, band_y, 0).astype(F32).astype(BF16)
            band_z = jnp.maximum(rz_l + 1 - jnp.abs(high4 - (p + shift)), 0)
            kz[plane(k), :] = jnp.where(low4 == row2, band_z, 0).astype(F32).astype(BF16)
            return 0

        lax.fori_loop(0, 3 * D, build, 0)
        rx_own = jnp.broadcast_to(rx[pl.ds(gx, 1), :], (H, L))
        rx_low = jnp.broadcast_to(rx[pl.ds(jnp.maximum(gx - 1, 0), 1), :], (H, L))
        rx_high = jnp.broadcast_to(rx[pl.ds(jnp.minimum(gx + 1, nx - 1), 1), :], (H, L))

        def build_x(k, _):
            target = row + k * H
            own = jnp.maximum(rx_own + 1 - jnp.abs(lane - target), 0)
            low = jnp.maximum(rx_low + 1 - jnp.abs(lane - L - target), 0)
            high = jnp.maximum(rx_high + 1 - jnp.abs(lane + L - target), 0)
            bx[plane(k), pl.ds(0, L)] = own.astype(F32).astype(BF16)
            bx[plane(k), pl.ds(L, L)] = jnp.where(lane < L // 2, high, low).astype(F32).astype(BF16)
            return 0

        lax.fori_loop(0, L // H, build_x, 0)
        norm_yx = (norm_of(ry_r, gy * H + row, total["gy"]) * norm_of(rx_own, gx * L + lane, total["gx"])).astype(F32)

        loads[0].wait()
        loads[1].wait()

        def material(z, _):
            density = den[plane(z), :]
            design = jnp.where(lab[plane(z), :] == 2, 1.0, 0.0).astype(F32)
            square = density * density
            cube = square * density
            nu_design = 1.0 / (1.0 + MU_GAIN * cube)
            nu[plane(z), :] = 1.0 - design + design * nu_design
            kap[plane(z), :] = design * KAPPA_GAIN * cube
            gz_i = gz * D + z
            norm_z = norm_of(rz[gz_i], gz_i, total["gz"]).astype(F32)
            inverse = SENS_GAIN / (norm_yx * norm_z)
            nu_slope = -3.0 * MU_GAIN * design * square * nu_design * nu_design
            kk[plane(z), :] = -0.5 * nu_slope * inverse
            qq[plane(z), :] = 3.0 * KAPPA_GAIN * design * square * inverse
            return 0

        lax.fori_loop(0, D, material, 0)

        def faces(z, _):
            v = nu[plane(z), :]
            below = nu[plane(jnp.maximum(z - 1, 0)), :]
            above = nu[plane(jnp.minimum(z + 1, D - 1)), :]
            wzm[plane(z), :] = jnp.where(z > 0, 0.5 * (v + below), 0.0)
            wzp[plane(z), :] = jnp.where(z < D - 1, 0.5 * (v + above), 0.0)
            wym[plane(z), :] = jnp.where(row > 0, 0.5 * (v + pltpu.roll(v, 1, 0)), 0.0)
            wyp[plane(z), :] = jnp.where(row < H - 1, 0.5 * (v + pltpu.roll(v, H - 1, 0)), 0.0)
            wxm[plane(z), :] = jnp.where(lane > 0, 0.5 * (v + pltpu.roll(v, 1, 1)), 0.0)
            wxp[plane(z), :] = jnp.where(lane < L - 1, 0.5 * (v + pltpu.roll(v, L - 1, 1)), 0.0)
            return 0

        lax.fori_loop(0, D, faces, 0)

        def pack(z, tiles, values):
            out = []
            for n, tile in enumerate(tiles):
                group = None
                for c, v in enumerate(values[4 * n:4 * n + 4]):
                    moved = pltpu.roll(v, 2 * c + 1, 1)
                    group = moved if group is None else jnp.where(lane // 2 == c, moved, group)
                group = pltpu.roll(group, z * 8, 1)
                out.append(jnp.where(lane // 8 == z, group, tile))
            return tuple(out)

        def pair(xr, n):
            below = pltpu.roll(xr[0, n], 1, 1)
            above = pltpu.roll(xr[1, n], L - 1, 1)
            return jnp.where(lax.rem(lane, 2) == 0, above, below)

        def unpack(tile, z, count):
            group = pltpu.roll(tile, lax.rem(L - z * 8, L), 1)
            return [pltpu.roll(group, L - 2 * c - 1, 1) for c in range(count)]

        zero = jnp.zeros((H, L), F32)

        def cell_rows(ref, count, first):
            return ref[pl.ds(first, count * D, stride=H), :]

        loads[2].wait()
        for side, z in ((0, 0), (1, D - 1)):
            for c in range(6):
                zs0[side, pl.ds(c * H, H), :] = a0[pl.ds((c * D + z) * H, H), :]
            zs0[side, pl.ds(6 * H, H), :] = nu[pl.ds(z * H, H), :]
            ys0[side, pl.ds(0, 6 * D), :] = cell_rows(a0, 6, side * (H - 1))
            ys0[side, pl.ds(6 * D, D), :] = cell_rows(nu, 1, side * (H - 1))

        def pack0(z, tiles):
            return pack(z, tiles, [a0[plane(c * D + z), :] for c in range(6)] + [nu[plane(z), :]])

        tiles = lax.fori_loop(0, D, pack0, (zero, zero))
        xs0[0] = tiles[0]
        xs0[1] = tiles[1]

        loads[3].wait()
        loads[4].wait()
        for side, z in ((0, 0), (1, D - 1)):
            for c in range(6):
                zsf[side, pl.ds(c * H, H), :] = f[pl.ds((c * D + z) * H, H), :]
            ysf[side] = cell_rows(f, 6, side * (H - 1))

        def packf(z, carry):
            tiles, re, im = carry
            values = [f[plane(c * D + z), :] for c in range(6)]
            mask = prt[plane(z), :].astype(F32)
            return (pack(z, tiles, values), re + mask * values[2], im + mask * values[5])

        tiles, port_re, port_im = lax.fori_loop(0, D, packf, ((zero, zero), zero, zero))
        xsf[0] = tiles[0]
        xsf[1] = tiles[1]
        ar1[here, pl.ds(0, 8), :] = port_re[:8] + port_re[8:]
        ar1[here, pl.ds(8, 8), :] = port_im[:8] + port_im[8:]

        has_diag = [jnp.logical_and(inside("gz", dz), inside("gx", dx)) for dz, dx in diagonals]
        count = flat - 1 + nz - 1
        for cond in has_diag:
            count = count + cond.astype(jnp.int32)
        pl.semaphore_wait(barrier, count)

        got0 = exchange(0, zs0, zr0, ys0, yr0, xs0, xr0)

        def ar1_copy(d):
            return pltpu.make_async_remote_copy(
                src_ref=ar1.at[here], dst_ref=ar1.at[here], send_sem=as1.at[d],
                recv_sem=ar_s1.at[here], device_id=plane_peer(d), device_id_type=MESH)

        def ar1_from(d):
            q = lax.rem(here + d, flat)
            return pltpu.make_async_remote_copy(
                src_ref=ar1.at[q], dst_ref=ar1.at[q], send_sem=as1.at[d],
                recv_sem=ar_s1.at[q], device_id=plane_peer(d), device_id_type=MESH)

        def ar2_copy(d):
            return pltpu.make_async_remote_copy(
                src_ref=ar2.at[gz], dst_ref=ar2.at[gz], send_sem=as2.at[d],
                recv_sem=ar_s2.at[gz], device_id=line_peer(d), device_id_type=MESH)

        def ar2_from(d):
            q = lax.rem(gz + d, nz)
            return pltpu.make_async_remote_copy(
                src_ref=ar2.at[q], dst_ref=ar2.at[q], send_sem=as2.at[d],
                recv_sem=ar_s2.at[q], device_id=line_peer(d), device_id_type=MESH)

        def loop(first, last, action):
            def step(d, _):
                action(d)
                return 0
            lax.fori_loop(first, last, step, 0)

        loop(1, flat, lambda d: ar1_copy(d).start())
        gotf = exchange(6, zsf, zrf, ysf, yrf, xsf, xrf)

        def inner(a, count, z, begin):
            zm = jnp.maximum(z - 1, 0)
            zp = jnp.minimum(z + 1, D - 1)
            w = [ref[plane(z), :] for ref in (wzm, wzp, wym, wyp, wxm, wxp)]
            for c in range(count):
                v = a[plane(c * D + z), :]
                total_ = w[0] * a[plane(c * D + zm), :] + w[1] * a[plane(c * D + zp), :]
                total_ += w[2] * pltpu.roll(v, 1, 0) + w[3] * pltpu.roll(v, H - 1, 0)
                total_ += w[4] * pltpu.roll(v, 1, 1) + w[5] * pltpu.roll(v, L - 1, 1)
                first = begin(c)
                t[plane(c * D + z), :] = total_ if first is None else total_ + first

        def inner1(z, _):
            kappa = kap[plane(z), :]
            inner(a0, 6, z, lambda c: kappa * f[plane(c * D + z), :])
            return 0

        lax.fori_loop(0, D, inner1, 0)

        arrive(got0)
        x0 = [pair(xr0, 0), pair(xr0, 1)]
        outer_x = jnp.logical_or(lane == 0, lane == L - 1)

        hz = []
        hy = []
        for side, z in ((0, 0), (1, D - 1)):
            hz.append(0.5 * (nu[pl.ds(z * H, H), :] + zr0[side, pl.ds(6 * H, H), :]))
            hy.append(0.5 * (cell_rows(nu, 1, side * (H - 1)) + yr0[side, pl.ds(6 * D, D), :]))

        def add_outer(zr, yr, count):
            for side, z in ((0, 0), (1, D - 1)):
                for c in range(count):
                    t[pl.ds((c * D + z) * H, H), :] += hz[side] * zr[side, pl.ds(c * H, H), :]
                for c in range(count):
                    at = pl.ds(c * D * H + side * (H - 1), D, stride=H)
                    t[at, :] = t[at, :] + hy[side] * yr[side, pl.ds(c * D, D), :]

        add_outer(zr0, yr0, 6)
        def diagonal(z, _):
            total_ = wzm[plane(z), :] + wzp[plane(z), :] + wym[plane(z), :] + wyp[plane(z), :]
            v = nu[plane(z), :]
            outside = unpack(x0[1], z, 3)[2]
            face = jnp.where(outer_x, 0.5 * (v + outside), 0.0)
            hx[plane(z), :] = face
            al[plane(z), :] = total_ + wxm[plane(z), :] + wxp[plane(z), :] + face
            return 0

        lax.fori_loop(0, D, diagonal, 0)
        for side, z in ((0, 0), (1, D - 1)):
            al[pl.ds(z * H, H), :] += hz[side]
            at = pl.ds(side * (H - 1), D, stride=H)
            al[at, :] = al[at, :] + hy[side]

        def finish(z, a, tiles_in, count):
            alpha = al[plane(z), :]
            beta = be[plane(z), :]
            face = hx[plane(z), :]
            outside = unpack(tiles_in[0], z, 4) + unpack(tiles_in[1], z, count - 4)
            tt = [t[plane(c * D + z), :] + face * outside[c] for c in range(count)]
            out = [None] * count
            pairs = [(0, 3), (1, 4), (2, 5)] + ([(6, 7)] if count == 8 else [])
            for re, im in pairs:
                out[re] = (1.0 - RELAX) * a[plane(re * D + z), :] + (tt[re] * alpha + tt[im] * beta)
                out[im] = (1.0 - RELAX) * a[plane(im * D + z), :] + (tt[im] * alpha - tt[re] * beta)
            return out

        def sweep1(z, tiles):
            d = al[plane(z), :]
            kappa = kap[plane(z), :]
            weight = RELAX / (d * d + kappa * kappa)
            al[plane(z), :] = d * weight
            be[plane(z), :] = kappa * weight
            out = finish(z, a0, x0, 6)
            mask = prt[plane(z), :].astype(F32)
            out.append(mask * (d * weight))
            out.append(-mask * (kappa * weight))
            for c in range(8):
                a1[plane(c * D + z), :] = out[c]
            return pack(z, tiles, out)

        tiles = lax.fori_loop(0, D, sweep1, (zero, zero))
        xs1[0] = tiles[0]
        xs1[1] = tiles[1]
        for side, z in ((0, 0), (1, D - 1)):
            for c in range(8):
                zs1[side, pl.ds(c * H, H), :] = a1[pl.ds((c * D + z) * H, H), :]
            ys1[side] = cell_rows(a1, 8, side * (H - 1))
        got1 = exchange(12, zs1, zr1, ys1, yr1, xs1, xr1)

        loop(1, flat, lambda d: ar1_from(d).wait_recv())
        part = ar1[0]
        for q in range(1, flat):
            part = part + ar1[q]
        ar2[gz] = part
        loop(1, nz, lambda d: ar2_copy(d).start())

        def inner2(z, _):
            kappa = kap[plane(z), :]

            def begin(c):
                if c < 6:
                    return kappa * f[plane(c * D + z), :]
                return prt[plane(z), :].astype(F32) if c == 6 else None

            inner(a1, 8, z, begin)
            return 0

        lax.fori_loop(0, D, inner2, 0)
        arrive(gotf)
        xf = [pair(xrf, 0), pair(xrf, 1)]
        arrive(got1)
        loop(1, nz, lambda d: ar2_from(d).wait_recv())
        part = ar2[0]
        for q in range(1, nz):
            part = part + ar2[q]
        link_re = scale * jnp.sum(part[:8])
        link_im = scale * jnp.sum(part[8:])
        imp_o[0] = link_re
        imp_o[1] = link_im
        coef_re = 2.0 * (link_re - zt[0])
        coef_im = -2.0 * (link_im - zt[1])
        add_outer(zr1, yr1, 8)
        x1 = [pair(xr1, 0), pair(xr1, 1)]

        def sweep2(z, tile):
            out = finish(z, a1, x1, 8)
            out[2] = out[2] + (coef_re * out[6] - coef_im * out[7])
            out[5] = out[5] + (coef_re * out[7] + coef_im * out[6])
            for c in range(6):
                a2[plane(c * D + z), :] = out[c]
            outside = unpack(xf[0], z, 4) + unpack(xf[1], z, 2)
            share = zero
            for c in range(6):
                term = out[c] * (f[plane(c * D + z), :] - outside[c])
                share = share + term if c < 3 else share - term
            share = jnp.where(outer_x, share, 0.0)
            t[plane(z), :] = share
            return pack(z, (tile,), [share])[0]

        xs2[...] = lax.fori_loop(0, D, sweep2, zero)
        adj_copy = pltpu.make_async_copy(a2, adj_o, out_sem)
        adj_copy.start()
        hz2 = []
        hy2 = []
        for side, z in ((0, 0), (1, D - 1)):
            share = zero
            for c in range(6):
                here_ = pl.ds((c * D + z) * H, H)
                term = a2[here_, :] * (f[here_, :] - zrf[side, pl.ds(c * H, H), :])
                share = share + term if c < 3 else share - term
            zs2[side] = share
            hz2.append(share)
            share = zero
            for c in range(6):
                at = pl.ds(c * D * H + side * (H - 1), D, stride=H)
                term = a2[at, :] * (f[at, :] - yrf[side, pl.ds(c * D, D), :])
                share = share + term if c < 3 else share - term
            ys2[side] = share
            hy2.append(share)
        got2 = exchange(18, zs2, zr2, ys2, yr2, xs2, xr2)

        def sens(z, last):
            zp = jnp.minimum(z + 1, D - 1)
            ez = zero
            ey = zero
            ex = zero
            more = zero
            av = [a2[plane(c * D + z), :] for c in range(6)]
            fv = [f[plane(c * D + z), :] for c in range(6)]
            for c in range(6):
                a, g = av[c], fv[c]
                tz = (a - a2[plane(c * D + zp), :]) * (g - f[plane(c * D + zp), :])
                ty = (a - pltpu.roll(a, H - 1, 0)) * (g - pltpu.roll(g, H - 1, 0))
                tx = (a - pltpu.roll(a, L - 1, 1)) * (g - pltpu.roll(g, L - 1, 1))
                ez = ez + tz if c < 3 else ez - tz
                ey = ey + ty if c < 3 else ey - ty
                ex = ex + tx if c < 3 else ex - tx
                more = more + g * (g + av[(c + 3) % 6])
            ey = jnp.where(row < H - 1, ey, 0.0)
            ex = jnp.where(lane < L - 1, ex, 0.0)
            energy = ez + last + ey + pltpu.roll(ey, 1, 0) + ex + pltpu.roll(ex, 1, 1) + t[plane(z), :]
            s[plane(z), :] = kk[plane(z), :] * energy + qq[plane(z), :] * more
            return ez

        lax.fori_loop(0, D, sens, zero)
        arrive(got2)
        for side, z in ((0, 0), (1, D - 1)):
            at = pl.ds(z * H, H)
            s[at, :] += kk[at, :] * (hz2[side] + zr2[side])
            at = pl.ds(side * (H - 1), D, stride=H)
            s[at, :] = s[at, :] + kk[at, :] * (hy2[side] + yr2[side])
        below = pltpu.roll(xr2[0], 1, 1)
        above = pltpu.roll(xr2[1], L - 1, 1)
        x2 = jnp.where(lax.rem(lane, 2) == 0, above, below)

        def split(v):
            high = v.astype(BF16)
            return high, (v - high.astype(F32)).astype(BF16)

        def add_x(z, _):
            outside = unpack(x2, z, 1)[0]
            v = s[plane(z), :] + kk[plane(z), :] * jnp.where(outer_x, outside, 0.0)
            high, low = split(v)
            vb[plane(z), pl.ds(0, L)] = high
            vb[plane(z), pl.ds(L, L)] = low
            return 0

        lax.fori_loop(0, D, add_x, 0)

        def band(matrix, dst_low, dst_own, dst_high):
            for n, dst in ((0, dst_low), (2, dst_high), (1, dst_own)):
                both = jnp.dot(matrix[pl.ds(n * D * H, D * H), :], vb[...], preferred_element_type=F32)
                dst[...] = both[:, :L] + both[:, L:]

        band(ky, ysF.at[0], pb, ysF.at[1])
        gotF = []
        for side, d in ((0, -1), (1, 1)):
            gotF.append(beside("gy", d, ysF.at[side], yrF.at[1 - side], 24 + side))
        arrive(gotF)

        def add_y(z, _):
            v = pb[plane(z), :] + yrF[0, plane(z), :] + yrF[1, plane(z), :]
            high, low = split(v)
            vb[plane(z), pl.ds(0, L)] = high
            vb[plane(z), pl.ds(L, L)] = low
            return 0

        lax.fori_loop(0, D, add_y, 0)

        band(kz, zsF.at[0], pb, zsF.at[1])
        gotZ = []
        for side, d in ((0, -1), (1, 1)):
            gotZ.append(beside("gz", d, zsF.at[side], zrF.at[1 - side], 26 + side))

        def strips(src, n):
            for half in range(2):
                def step(p, tiles):
                    v = src[plane(p + 8 * half), :]
                    out = []
                    for side in (0, 1):
                        moved = pltpu.roll(v, lax.rem(p * REACH + side * REACH, L), 1)
                        out.append(jnp.where(lane // REACH == p, moved, tiles[side]))
                    return tuple(out)
                tiles = lax.fori_loop(0, 8, step, (zero, zero))
                for side in (0, 1):
                    st[side, n, half] = tiles[side]

        strips(zsF.at[0], 1)
        strips(zsF.at[1], 2)
        strips(pb, 0)
        gotX = []
        for side, dx in ((0, -1), (1, 1)):
            for n, dz in ((1, -1), (2, 1)):
                go = jnp.logical_and(inside("gx", dx), inside("gz", dz))
                come = jnp.logical_and(inside("gx", -dx), inside("gz", -dz))
                copy = remote(st.at[side, n], sr.at[1 - side, 3 - n], 28 + side * 3 + n,
                              {"gz": gz + dz, "gx": gx + dx})
                pl.when(go)(copy.start)
                sent.append((go, copy))
                gotX.append((come, copy))
            gotX.append(beside("gx", dx, st.at[side, 0], sr.at[1 - side, 0], 28 + side * 3))
        arrive(gotZ)
        arrive(gotX)
        cols = [[sr[side, 0, half] + sr[side, 1, half] + sr[side, 2, half] for half in range(2)] for side in (0, 1)]
        for half in range(2):
            def add_z(p, _):
                at = plane(p + 8 * half)
                v = pb[at, :] + zrF[0, at, :] + zrF[1, at, :]
                back = lax.rem(L - p * REACH, L)
                low = pltpu.roll(cols[0][half], lax.rem(back + L - REACH, L), 1)
                high = pltpu.roll(cols[1][half], back, 1)
                for k, part_ in enumerate((v, jnp.where(lane < L // 2, high, low))):
                    big, small = split(part_)
                    xin[at, pl.ds(k * L, L)] = big
                    xin[plane(p + 8 * half + D), pl.ds(k * L, L)] = small
                return 0
            lax.fori_loop(0, 8, add_z, 0)
        both = lax.dot_general(xin[...], bx[...], (((1,), (1,)), ((), ())), preferred_element_type=F32)
        grad_o[...] = both[:D * H] + both[D * H:]

        for cond, copy in sent:
            pl.when(cond)(copy.wait_send)
        loop(1, flat, lambda d: ar1_copy(d).wait_send())
        loop(1, nz, lambda d: ar2_copy(d).wait_send())
        adj_copy.wait()

    return kernel


def solution(mesh):
    sizes = dict(mesh.shape)
    nz, ny, nx = (sizes[a] for a in AXES)
    rows = D * H
    vm = lambda *shape: pltpu.VMEM(shape, F32)
    field = vm(rows, L)

    def halo(planes, tiles):
        y = vm(2, planes * D, L)
        z = vm(2, planes * H, L)
        return [z, y, vm(tiles, H, L), z, y, vm(2, tiles, H, L)]

    scratch = [
        vm(6 * rows, L), vm(6 * rows, L), field, pltpu.VMEM((rows, L), jnp.int32), pltpu.VMEM((rows, L), jnp.int32),
        vm(8 * rows, L), vm(6 * rows, L), vm(8 * rows, L),
    ] + [field] * 14 + halo(7, 2) + halo(6, 2) + halo(8, 2) + [
        vm(2, H, L), vm(2, D, L), vm(H, L), vm(2, H, L), vm(2, D, L), vm(2, H, L),
        pltpu.VMEM((3 * rows, 2 * L), BF16), pltpu.VMEM((3 * rows, 2 * L), BF16), pltpu.VMEM((L, 2 * L), BF16),
        field, vm(2, rows, L), vm(2, rows, L), vm(2, rows, L), vm(2, rows, L),
        vm(2, 3, 2, H, L), vm(2, 3, 2, H, L),
        pltpu.VMEM((rows, 2 * L), BF16), pltpu.VMEM((2 * rows, 2 * L), BF16),
        vm(ny * nx, H, L), vm(nz, H, L),
        pltpu.SemaphoreType.DMA((5,)), pltpu.SemaphoreType.DMA,
        pltpu.SemaphoreType.DMA((34,)), pltpu.SemaphoreType.DMA((34,)),
        pltpu.SemaphoreType.DMA((ny * nx,)), pltpu.SemaphoreType.DMA((ny * nx,)),
        pltpu.SemaphoreType.DMA((nz,)), pltpu.SemaphoreType.DMA((nz,)),
    ]
    hbm = pl.BlockSpec(memory_space=pl.ANY)
    smem = pl.BlockSpec(memory_space=pltpu.SMEM)
    vmem = pl.BlockSpec(memory_space=pltpu.VMEM)
    call = pl.pallas_call(
        make_kernel(sizes),
        out_shape=(
            jax.ShapeDtypeStruct((6 * rows, L), F32),
            jax.ShapeDtypeStruct((rows, L), F32),
            jax.ShapeDtypeStruct((2,), F32),
        ),
        in_specs=[hbm] * 5 + [smem] * 3 + [vmem],
        out_specs=(hbm, vmem, smem),
        scratch_shapes=scratch,
        compiler_params=pltpu.CompilerParams(
            collective_id=0, has_side_effects=True, vmem_limit_bytes=48 * 2**20),
    )

    def body(forward, adjoint_prev, density, labels, ports, z_target, radius_z, radius_y, radius_x):
        adjoint, gradient, impedance = call(
            forward.reshape(6 * rows, L), adjoint_prev.reshape(6 * rows, L), density.reshape(rows, L),
            labels.reshape(rows, L), ports.reshape(rows, L), z_target, radius_z, radius_y,
            radius_x.reshape(nx, L))
        return adjoint.reshape(6, D, H, L), gradient.reshape(D, H, L), impedance

    in_specs = (P(None, *AXES),) * 2 + (P(*AXES),) * 3 + (P(),) * 4
    out_specs = (P(None, *AXES), P(*AXES), P())
    return jax.shard_map(body, mesh=mesh, in_specs=in_specs, out_specs=out_specs, check_vma=False)
```

```python
import jax
import jax.numpy as jnp
from jax import lax
from jax.experimental import pallas as pl
from jax.experimental.pallas import tpu as pltpu
from jax.sharding import PartitionSpec as P

MU_GAIN = 19.0
KAPPA_GAIN = 2.0
RELAX = 0.8
SENS_GAIN = 0.1
REACH = 16
CORES = 2
WIDTH = dict(add_x=16, add_y=16, add_z=8, build=4, build_x=4, diagonal=16, faces=16, inner1=16, inner2=16, material=16, pack0=16, packf=16, sens=16, step=8, sweep1=16, sweep2=16, join=16, answer=16)
MESH = pl.DeviceIdType.MESH
AXES = ("gz", "gy", "gx")
F32 = jnp.float32
BF16 = jnp.bfloat16
D = 16
H = 16
L = 128


def plane(index):
    if isinstance(index, int):
        return pl.ds(index * H, H)
    return pl.ds(pl.multiple_of(index * H, H), H)


def each(count, step, carry, width):
    if width == count:
        for k in range(count):
            carry = step(k, carry)
        return carry

    def group(g, carry):
        for k in range(width):
            carry = step(g * width + k, carry)
        return carry

    return lax.fori_loop(0, count // width, group, carry)


def mod(a, b):
    return a % b if isinstance(a, int) else lax.rem(a, b)


def clamp(value):
    if isinstance(value, int):
        return min(max(value, 0), D - 1)
    return jnp.clip(value, 0, D - 1)


def tri(value):
    value = jnp.maximum(value, 0)
    return value * (value + 1) // 2


def norm_of(radius, position, length):
    whole = (radius + 1) * (radius + 1)
    return whole - tri(radius - position) - tri(radius - (length - 1 - position))


def make_kernel(sizes):
    nz, ny, nx = sizes["gz"], sizes["gy"], sizes["gx"]
    total = {"gz": nz * D, "gy": ny * H, "gx": nx * L}
    scale = 4.0 / (total["gz"] * total["gy"] * total["gx"])

    def kernel(fwd_h, adj_h, den_h, lab_h, prt_h, zt, rz, ry, rx,
               adj_o, grad_o, imp_o,
               f, a0, den, lab, prt, a1, a2, t,
               nu, kap, wzm, wzp, wym, wyp, wxm, wxp, al, be, hx, kk, qq, s,
               zs0, ys0, xs0, zr0, yr0, xr0,
               zsf, ysf, xsf, zrf, yrf, xrf,
               zs1, ys1, xs1, zr1, yr1, xr1,
               zs2, ys2, xs2, zr2, yr2, xr2,
               ky, kz, bx, pb, ysF, yrF, zsF, zrF, st, sr, vb, xin,
               sum_core, sum_x, sum_y, sum_z, in_sem, out_sem, ss, rs,
               ss_core, rs_core, ss_x, rs_x, ss_y, rs_y, ss_z, rs_z):
        sums = {"core": sum_core, "gx": sum_x, "gy": sum_y, "gz": sum_z}
        sum_ss = {"core": ss_core, "gx": ss_x, "gy": ss_y, "gz": ss_z}
        sum_rs = {"core": rs_core, "gx": rs_x, "gy": rs_y, "gz": rs_z}
        gz, gy, gx = (lax.axis_index(a) for a in AXES)
        pos = {"gz": gz, "gy": gy, "gx": gx}
        core = lax.rem(gz, CORES)

        def inside(axis, d):
            size = {"gz": nz, "gy": ny, "gx": nx}[axis]
            return pos[axis] < size - 1 if d > 0 else pos[axis] > 0

        stages = {
            "core": (CORES, lambda d: {"gz": gz - core + lax.rem(core + d, CORES)}, core),
            "gx": (nx, lambda d: {"gx": lax.rem(gx + d, nx)}, gx),
            "gy": (ny, lambda d: {"gy": lax.rem(gy + d, ny)}, gy),
            "gz": (nz // CORES, lambda d: {"gz": lax.rem(gz + CORES * d, nz)}, gz // CORES),
        }
        barrier = pltpu.get_barrier_semaphore()
        others = [(dz, dx, jnp.logical_and(inside("gz", dz), inside("gx", dx))) for dz in (-1, 1) for dx in (-1, 1)]
        others += [(dz, 0, jnp.logical_and(inside("gz", dz), (core == 0) if dz < 0 else (core == CORES - 1)))
                   for dz in (-1, 1)]
        expected = 0
        for members, peer, _ in stages.values():
            for d in range(1, members):
                pl.semaphore_signal(barrier, inc=1, device_id=peer(d), device_id_type=MESH)
                expected += 1
        for dz, dx, cond in others:
            @pl.when(cond)
            def _():
                pl.semaphore_signal(barrier, inc=1, device_id={"gz": gz + dz, "gx": gx + dx}, device_id_type=MESH)
            expected = expected + cond.astype(jnp.int32)

        loads = [
            pltpu.make_async_copy(src, dst, in_sem.at[k])
            for k, (src, dst) in enumerate(((den_h, den), (lab_h, lab), (adj_h, a0), (fwd_h, f), (prt_h, prt)))
        ]
        for load in loads:
            load.start()

        def remote(src, dst, slot, where):
            return pltpu.make_async_remote_copy(
                src_ref=src, dst_ref=dst, send_sem=ss.at[slot], recv_sem=rs.at[slot],
                device_id=where, device_id_type=MESH)

        sent = []

        def beside(axis, d, src, dst, slot):
            copy = remote(src, dst, slot, {axis: pos[axis] + d})
            pl.when(inside(axis, d))(copy.start)
            sent.append((inside(axis, d), copy))
            return (inside(axis, -d), copy)

        def arrive(copies):
            for cond, copy in copies:
                pl.when(cond)(copy.wait_recv)

        def exchange(base, zs, zr, ys, yr, xs, xr):
            copies = []
            for axis, src, dst, k in (("gy", ys, yr, 2), ("gx", xs, xr, 4), ("gz", zs, zr, 0)):
                for d in (-1, 1):
                    side = 0 if d < 0 else 1
                    piece = src if axis == "gx" else src.at[side]
                    copies.append(beside(axis, d, piece, dst.at[1 - side], base + k + side))
            return copies

        edges = {axis: (pos[axis] == 0, pos[axis] == {"gz": nz, "gy": ny, "gx": nx}[axis] - 1) for axis in AXES}
        for axis, bufs in (("gz", (zr0, zrf, zr1, zr2, zrF)), ("gy", (yr0, yrf, yr1, yr2, yrF)),
                           ("gx", (xr0, xrf, xr1, xr2, sr))):
            for side in (0, 1):
                @pl.when(edges[axis][side])
                def _():
                    for buf in bufs:
                        buf[side] = jnp.zeros(buf.shape[1:], F32)
                    if axis == "gx":
                        column = lax.rem(lax.broadcasted_iota(jnp.int32, (H, L), 1), 8)
                        xr0[side, 1] = jnp.where(column // 2 == 2, 1.0, 0.0).astype(F32)
                    else:
                        buf = zr0 if axis == "gz" else yr0
                        buf[side, pl.ds(6 * H, H), :] = jnp.ones((H, L), F32)
        for side, dz_ in ((0, 1), (1, 1)):
            for low in (0, 1):
                @pl.when(edges["gz"][low])
                def _():
                    sr[side, 1 + low] = jnp.zeros(sr.shape[2:], F32)

        lane = lax.broadcasted_iota(jnp.int32, (H, L), 1)
        row = lax.broadcasted_iota(jnp.int32, (H, L), 0)

        lane2 = lax.broadcasted_iota(jnp.int32, (H, 2 * L), 1)
        row2 = lax.broadcasted_iota(jnp.int32, (H, 2 * L), 0)
        low4 = lax.rem(lane2, H)
        high4 = lane2 // H
        ry_l = jnp.zeros((H, 2 * L), jnp.int32)
        rz_l = jnp.zeros((H, 2 * L), jnp.int32)
        ry_r = jnp.zeros((H, L), jnp.int32)
        for b in range(H):
            ry_b = ry[gy * H + b]
            rz_b = rz[gz * D + b]
            ry_l = jnp.where(low4 == b, ry_b, ry_l)
            rz_l = jnp.where(high4 == b, rz_b, rz_l)
            ry_r = jnp.where(row == b, ry_b, ry_r)

        def build(k, _):
            shift = (k // D - 1) * D
            p = lax.rem(k, D)
            band_y = jnp.maximum(ry_l + 1 - jnp.abs(low4 - (row2 + shift)), 0)
            ky[plane(k), :] = jnp.where(high4 == p, band_y, 0).astype(F32).astype(BF16)
            band_z = jnp.maximum(rz_l + 1 - jnp.abs(high4 - (p + shift)), 0)
            kz[plane(k), :] = jnp.where(low4 == row2, band_z, 0).astype(F32).astype(BF16)
            return 0

        each(3 * D, build, 0, WIDTH['build'])
        rx_own = jnp.broadcast_to(rx[pl.ds(gx, 1), :], (H, L))
        rx_low = jnp.broadcast_to(rx[pl.ds(jnp.maximum(gx - 1, 0), 1), :], (H, L))
        rx_high = jnp.broadcast_to(rx[pl.ds(jnp.minimum(gx + 1, nx - 1), 1), :], (H, L))

        def build_x(k, _):
            target = row + k * H
            own = jnp.maximum(rx_own + 1 - jnp.abs(lane - target), 0)
            low = jnp.maximum(rx_low + 1 - jnp.abs(lane - L - target), 0)
            high = jnp.maximum(rx_high + 1 - jnp.abs(lane + L - target), 0)
            bx[plane(k), pl.ds(0, L)] = own.astype(F32).astype(BF16)
            bx[plane(k), pl.ds(L, L)] = jnp.where(lane < L // 2, high, low).astype(F32).astype(BF16)
            return 0

        each(L // H, build_x, 0, WIDTH['build_x'])
        norm_yx = (norm_of(ry_r, gy * H + row, total["gy"]) * norm_of(rx_own, gx * L + lane, total["gx"])).astype(F32)

        loads[0].wait()
        loads[1].wait()

        def material(z, _):
            density = den[plane(z), :]
            design = jnp.where(lab[plane(z), :] == 2, 1.0, 0.0).astype(F32)
            square = density * density
            cube = square * density
            nu_design = 1.0 / (1.0 + MU_GAIN * cube)
            nu[plane(z), :] = 1.0 - design + design * nu_design
            kap[plane(z), :] = design * KAPPA_GAIN * cube
            gz_i = gz * D + z
            norm_z = norm_of(rz[gz_i], gz_i, total["gz"]).astype(F32)
            inverse = SENS_GAIN / (norm_yx * norm_z)
            nu_slope = -3.0 * MU_GAIN * design * square * nu_design * nu_design
            kk[plane(z), :] = -0.5 * nu_slope * inverse
            qq[plane(z), :] = 3.0 * KAPPA_GAIN * design * square * inverse
            return 0

        each(D, material, 0, WIDTH['material'])

        def faces(z, _):
            v = nu[plane(z), :]
            below = nu[plane(clamp(z - 1)), :]
            above = nu[plane(clamp(z + 1)), :]
            wzm[plane(z), :] = jnp.where(z > 0, 0.5 * (v + below), 0.0)
            wzp[plane(z), :] = jnp.where(z < D - 1, 0.5 * (v + above), 0.0)
            wym[plane(z), :] = jnp.where(row > 0, 0.5 * (v + pltpu.roll(v, 1, 0)), 0.0)
            wyp[plane(z), :] = jnp.where(row < H - 1, 0.5 * (v + pltpu.roll(v, H - 1, 0)), 0.0)
            wxm[plane(z), :] = jnp.where(lane > 0, 0.5 * (v + pltpu.roll(v, 1, 1)), 0.0)
            wxp[plane(z), :] = jnp.where(lane < L - 1, 0.5 * (v + pltpu.roll(v, L - 1, 1)), 0.0)
            return 0

        each(D, faces, 0, WIDTH['faces'])

        def pack(z, tiles, values):
            out = list(tiles)
            for c, v in enumerate(values):
                moved = pltpu.roll(v, (z * 8 + 2 * (c % 4) + 1) % L, 1)
                out[c // 4] = jnp.where(lane // 2 == z * 4 + c % 4, moved, out[c // 4])
            return tuple(out)

        def pair(xr, n):
            below = pltpu.roll(xr[0, n], 1, 1)
            above = pltpu.roll(xr[1, n], L - 1, 1)
            return jnp.where(lax.rem(lane, 2) == 0, above, below)

        def unpack(tile, z, count, first=0):
            return [pltpu.roll(tile, (-z * 8 - 2 * c - 1) % L, 1) for c in range(first, first + count)]

        zero = jnp.zeros((H, L), F32)

        def cell_rows(ref, count, first):
            return ref[pl.ds(first, count * D, stride=H), :]

        loads[2].wait()
        for side, z in ((0, 0), (1, D - 1)):
            for c in range(6):
                zs0[side, pl.ds(c * H, H), :] = a0[pl.ds((c * D + z) * H, H), :]
            zs0[side, pl.ds(6 * H, H), :] = nu[pl.ds(z * H, H), :]
            ys0[side, pl.ds(0, 6 * D), :] = cell_rows(a0, 6, side * (H - 1))
            ys0[side, pl.ds(6 * D, D), :] = cell_rows(nu, 1, side * (H - 1))

        def pack0(z, tiles):
            return pack(z, tiles, [a0[plane(c * D + z), :] for c in range(6)] + [nu[plane(z), :]])

        tiles = each(D, pack0, (zero, zero), WIDTH['pack0'])
        xs0[0] = tiles[0]
        xs0[1] = tiles[1]

        loads[3].wait()
        loads[4].wait()
        for side, z in ((0, 0), (1, D - 1)):
            for c in range(6):
                zsf[side, pl.ds(c * H, H), :] = f[pl.ds((c * D + z) * H, H), :]
            ysf[side] = cell_rows(f, 6, side * (H - 1))

        def packf(z, carry):
            tiles, re, im = carry
            values = [f[plane(c * D + z), :] for c in range(6)]
            mask = prt[plane(z), :].astype(F32)
            return (pack(z, tiles, values), re + mask * values[2], im + mask * values[5])

        tiles, port_re, port_im = each(D, packf, ((zero, zero), zero, zero), WIDTH['packf'])
        xsf[0] = tiles[0]
        xsf[1] = tiles[1]
        port_sum = jnp.concatenate(
            [jnp.sum(port_re, axis=0, keepdims=True), jnp.sum(port_im, axis=0, keepdims=True)], axis=0)

        pl.semaphore_wait(barrier, expected)
        got0 = exchange(0, zs0, zr0, ys0, yr0, xs0, xr0)

        def sum_copy(stage, d, arriving):
            members, peer, slot = stages[stage]
            at = lax.rem(slot + d, members) if arriving else slot
            ref = sums[stage].at[at]
            return pltpu.make_async_remote_copy(
                src_ref=ref, dst_ref=ref, send_sem=sum_ss[stage].at[d], recv_sem=sum_rs[stage].at[at],
                device_id=peer(d), device_id_type=MESH)

        def sum_start(stage, value):
            members, _, slot = stages[stage]
            sums[stage][slot] = value
            for d in range(1, members):
                sum_copy(stage, d, False).start()

        def sum_finish(stage):
            members = stages[stage][0]
            for d in range(1, members):
                sum_copy(stage, d, True).wait_recv()
            value = sums[stage][0]
            for q in range(1, members):
                value = value + sums[stage][q]
            return value

        sum_start("core", port_sum)

        def inner(a, count, z, begin):
            zm = clamp(z - 1)
            zp = clamp(z + 1)
            w = [ref[plane(z), :] for ref in (wzm, wzp, wym, wyp, wxm, wxp)]
            for c in range(count):
                v = a[plane(c * D + z), :]
                total_ = w[0] * a[plane(c * D + zm), :] + w[1] * a[plane(c * D + zp), :]
                total_ += w[2] * pltpu.roll(v, 1, 0) + w[3] * pltpu.roll(v, H - 1, 0)
                total_ += w[4] * pltpu.roll(v, 1, 1) + w[5] * pltpu.roll(v, L - 1, 1)
                first = begin(c)
                t[plane(c * D + z), :] = total_ if first is None else total_ + first

        def inner1(z, _):
            kappa = kap[plane(z), :]
            inner(a0, 6, z, lambda c: kappa * f[plane(c * D + z), :])
            return 0

        each(D, inner1, 0, WIDTH['inner1'])
        sum_start("gx", sum_finish("core"))
        gotf = exchange(6, zsf, zrf, ysf, yrf, xsf, xrf)

        arrive(got0)
        x0 = [pair(xr0, 0), pair(xr0, 1)]
        outer_x = jnp.logical_or(lane == 0, lane == L - 1)

        hz = []
        hy = []
        for side, z in ((0, 0), (1, D - 1)):
            hz.append(0.5 * (nu[pl.ds(z * H, H), :] + zr0[side, pl.ds(6 * H, H), :]))
            hy.append(0.5 * (cell_rows(nu, 1, side * (H - 1)) + yr0[side, pl.ds(6 * D, D), :]))

        def add_outer(zr, yr, count):
            for side, z in ((0, 0), (1, D - 1)):
                for c in range(count):
                    t[pl.ds((c * D + z) * H, H), :] += hz[side] * zr[side, pl.ds(c * H, H), :]
                for c in range(count):
                    at = pl.ds(c * D * H + side * (H - 1), D, stride=H)
                    t[at, :] = t[at, :] + hy[side] * yr[side, pl.ds(c * D, D), :]

        add_outer(zr0, yr0, 6)
        def diagonal(z, _):
            total_ = wzm[plane(z), :] + wzp[plane(z), :] + wym[plane(z), :] + wyp[plane(z), :]
            v = nu[plane(z), :]
            outside = unpack(x0[1], z, 1, 2)[0]
            face = jnp.where(outer_x, 0.5 * (v + outside), 0.0)
            hx[plane(z), :] = face
            al[plane(z), :] = total_ + wxm[plane(z), :] + wxp[plane(z), :] + face
            return 0

        each(D, diagonal, 0, WIDTH['diagonal'])
        for side, z in ((0, 0), (1, D - 1)):
            al[pl.ds(z * H, H), :] += hz[side]
            at = pl.ds(side * (H - 1), D, stride=H)
            al[at, :] = al[at, :] + hy[side]

        def finish(z, a, tiles_in, count):
            alpha = al[plane(z), :]
            beta = be[plane(z), :]
            face = hx[plane(z), :]
            outside = unpack(tiles_in[0], z, 4) + unpack(tiles_in[1], z, count - 4)
            tt = [t[plane(c * D + z), :] + face * outside[c] for c in range(count)]
            out = [None] * count
            pairs = [(0, 3), (1, 4), (2, 5)] + ([(6, 7)] if count == 8 else [])
            for re, im in pairs:
                out[re] = (1.0 - RELAX) * a[plane(re * D + z), :] + (tt[re] * alpha + tt[im] * beta)
                out[im] = (1.0 - RELAX) * a[plane(im * D + z), :] + (tt[im] * alpha - tt[re] * beta)
            return out

        def sweep1(z, tiles):
            d = al[plane(z), :]
            kappa = kap[plane(z), :]
            weight = RELAX / (d * d + kappa * kappa)
            al[plane(z), :] = d * weight
            be[plane(z), :] = kappa * weight
            out = finish(z, a0, x0, 6)
            mask = prt[plane(z), :].astype(F32)
            out.append(mask * (d * weight))
            out.append(-mask * (kappa * weight))
            for c in range(8):
                a1[plane(c * D + z), :] = out[c]
            return pack(z, tiles, out)

        tiles = each(D, sweep1, (zero, zero), WIDTH['sweep1'])
        xs1[0] = tiles[0]
        xs1[1] = tiles[1]
        for side, z in ((0, 0), (1, D - 1)):
            for c in range(8):
                zs1[side, pl.ds(c * H, H), :] = a1[pl.ds((c * D + z) * H, H), :]
            ys1[side] = cell_rows(a1, 8, side * (H - 1))
        got1 = exchange(12, zs1, zr1, ys1, yr1, xs1, xr1)

        sum_start("gy", sum_finish("gx"))

        def inner2(z, _):
            kappa = kap[plane(z), :]

            def begin(c):
                if c < 6:
                    return kappa * f[plane(c * D + z), :]
                return prt[plane(z), :].astype(F32) if c == 6 else None

            inner(a1, 8, z, begin)
            return 0

        each(D, inner2, 0, WIDTH['inner2'])
        sum_start("gz", sum_finish("gy"))
        arrive(gotf)
        xf = [pair(xrf, 0), pair(xrf, 1)]
        arrive(got1)
        add_outer(zr1, yr1, 8)
        x1 = [pair(xr1, 0), pair(xr1, 1)]

        def shares(answers, near):
            main = None
            for c in range(6):
                term = answers[c] * near[c]
                main = term if c == 0 else main + term if c < 3 else main - term
            return [main, answers[6] * near[2] - answers[7] * near[5], -(answers[7] * near[2]) - answers[6] * near[5]]

        def sweep2(z, tile):
            out = finish(z, a1, x1, 8)
            for c in range(8):
                a2[plane(c * D + z), :] = out[c]
            outside = unpack(xf[0], z, 4) + unpack(xf[1], z, 2)
            near = [f[plane(c * D + z), :] - outside[c] for c in range(6)]
            share = [jnp.where(outer_x, v, 0.0) for v in shares(out, near)]
            for k in range(3):
                t[plane(k * D + z), :] = share[k]
            return pack(z, (tile,), share)[0]

        xs2[0] = each(D, sweep2, zero, WIDTH['sweep2'])
        hz2 = []
        hy2 = []
        for side, z in ((0, 0), (1, D - 1)):
            at = [pl.ds((c * D + z) * H, H) for c in range(8)]
            near = [f[at[c], :] - zrf[side, pl.ds(c * H, H), :] for c in range(6)]
            share = shares([a2[where, :] for where in at], near)
            for k in range(3):
                zs2[side, pl.ds(k * H, H), :] = share[k]
            hz2.append(share)
            at = [pl.ds(c * D * H + side * (H - 1), D, stride=H) for c in range(8)]
            near = [f[at[c], :] - yrf[side, pl.ds(c * D, D), :] for c in range(6)]
            share = shares([a2[where, :] for where in at], near)
            for k in range(3):
                ys2[side, pl.ds(k * D, D), :] = share[k]
            hy2.append(share)
        got2 = exchange(18, zs2, zr2, ys2, yr2, xs2, xr2)

        def sens(z, last):
            zp = clamp(z + 1)
            av = [a2[plane(c * D + z), :] for c in range(8)]
            fv = [f[plane(c * D + z), :] for c in range(6)]
            above = [a2[plane(c * D + zp), :] for c in range(8)], [f[plane(c * D + zp), :] for c in range(6)]
            ez = shares([v - w for v, w in zip(av, above[0])], [v - w for v, w in zip(fv, above[1])])
            ey = shares([v - pltpu.roll(v, H - 1, 0) for v in av], [v - pltpu.roll(v, H - 1, 0) for v in fv])
            ex = shares([v - pltpu.roll(v, L - 1, 1) for v in av], [v - pltpu.roll(v, L - 1, 1) for v in fv])
            more = [zero, av[6] * fv[5] + av[7] * fv[2], av[6] * fv[2] - av[7] * fv[5]]
            for c in range(6):
                more[0] = more[0] + fv[c] * (fv[c] + av[(c + 3) % 6])
            for k in range(3):
                along_y = jnp.where(row < H - 1, ey[k], 0.0)
                along_x = jnp.where(lane < L - 1, ex[k], 0.0)
                energy = ez[k] + last[k] + along_y + pltpu.roll(along_y, 1, 0)
                energy = energy + along_x + pltpu.roll(along_x, 1, 1) + t[plane(k * D + z), :]
                s[plane(k * D + z), :] = kk[plane(z), :] * energy + qq[plane(z), :] * more[k]
            return ez

        each(D, sens, [zero] * 3, WIDTH['sens'])
        total_ports = sum_finish("gz")
        link_re = scale * jnp.sum(total_ports[0:1])
        link_im = scale * jnp.sum(total_ports[1:2])
        imp_o[0] = link_re
        imp_o[1] = link_im
        coef_re = 2.0 * (link_re - zt[0])
        coef_im = -2.0 * (link_im - zt[1])

        def joined(parts):
            return parts[0] + (coef_re * parts[1] + coef_im * parts[2])

        def join(z, _):
            s[plane(z), :] = joined([s[plane(k * D + z), :] for k in range(3)])
            return 0

        each(D, join, 0, WIDTH['join'])
        for side, z in ((0, 0), (1, D - 1)):
            at = pl.ds(z * H, H)
            s[at, :] += kk[at, :] * joined(hz2[side])
            at = pl.ds(side * (H - 1), D, stride=H)
            s[at, :] = s[at, :] + kk[at, :] * joined(hy2[side])
        arrive(got2)
        for side, z in ((0, 0), (1, D - 1)):
            at = pl.ds(z * H, H)
            s[at, :] += kk[at, :] * joined([zr2[side, pl.ds(k * H, H), :] for k in range(3)])
            at = pl.ds(side * (H - 1), D, stride=H)
            s[at, :] = s[at, :] + kk[at, :] * joined([yr2[side, pl.ds(k * D, D), :] for k in range(3)])
        tile2 = pair(xr2, 0)
        tile2 = joined([tile2, pltpu.roll(tile2, L - 2, 1), pltpu.roll(tile2, L - 4, 1)])

        def split(v):
            high = v.astype(BF16)
            return high, (v - high.astype(F32)).astype(BF16)

        def add_x(z, _):
            outside = unpack(tile2, z, 1)[0]
            v = s[plane(z), :] + kk[plane(z), :] * jnp.where(outer_x, outside, 0.0)
            high, low = split(v)
            vb[plane(z), pl.ds(0, L)] = high
            vb[plane(z), pl.ds(L, L)] = low
            return 0

        each(D, add_x, 0, WIDTH['add_x'])

        def band(matrix, dst_low, dst_own, dst_high):
            for n, dst in ((0, dst_low), (2, dst_high), (1, dst_own)):
                both = jnp.dot(matrix[pl.ds(n * D * H, D * H), :], vb[...], preferred_element_type=F32)
                dst[...] = both[:, :L] + both[:, L:]

        band(ky, ysF.at[0], pb, ysF.at[1])
        gotF = []
        for side, d in ((0, -1), (1, 1)):
            gotF.append(beside("gy", d, ysF.at[side], yrF.at[1 - side], 24 + side))

        def answer(z, _):
            re, im = a2[plane(6 * D + z), :], a2[plane(7 * D + z), :]
            a2[plane(2 * D + z), :] += coef_re * re - coef_im * im
            a2[plane(5 * D + z), :] += coef_re * im + coef_im * re
            return 0

        each(D, answer, 0, WIDTH['answer'])
        adj_copy = pltpu.make_async_copy(a2.at[pl.ds(0, 6 * D * H), :], adj_o, out_sem)
        adj_copy.start()
        arrive(gotF)

        def add_y(z, _):
            v = pb[plane(z), :] + yrF[0, plane(z), :] + yrF[1, plane(z), :]
            high, low = split(v)
            vb[plane(z), pl.ds(0, L)] = high
            vb[plane(z), pl.ds(L, L)] = low
            return 0

        each(D, add_y, 0, WIDTH['add_y'])

        band(kz, zsF.at[0], pb, zsF.at[1])
        gotZ = []
        for side, d in ((0, -1), (1, 1)):
            gotZ.append(beside("gz", d, zsF.at[side], zrF.at[1 - side], 26 + side))

        def strips(src, n):
            for half in range(2):
                def step(p, tiles):
                    v = src[plane(p + 8 * half), :]
                    out = []
                    for side in (0, 1):
                        moved = pltpu.roll(v, mod(p * REACH + side * REACH, L), 1)
                        out.append(jnp.where(lane // REACH == p, moved, tiles[side]))
                    return tuple(out)
                tiles = each(8, step, (zero, zero), WIDTH['step'])
                for side in (0, 1):
                    st[side, n, half] = tiles[side]

        strips(zsF.at[0], 1)
        strips(zsF.at[1], 2)
        strips(pb, 0)
        gotX = []
        for side, dx in ((0, -1), (1, 1)):
            for n, dz in ((1, -1), (2, 1)):
                go = jnp.logical_and(inside("gx", dx), inside("gz", dz))
                come = jnp.logical_and(inside("gx", -dx), inside("gz", -dz))
                copy = remote(st.at[side, n], sr.at[1 - side, 3 - n], 28 + side * 3 + n,
                              {"gz": gz + dz, "gx": gx + dx})
                pl.when(go)(copy.start)
                sent.append((go, copy))
                gotX.append((come, copy))
            gotX.append(beside("gx", dx, st.at[side, 0], sr.at[1 - side, 0], 28 + side * 3))
        arrive(gotZ)
        arrive(gotX)
        cols = [[sr[side, 0, half] + sr[side, 1, half] + sr[side, 2, half] for half in range(2)] for side in (0, 1)]
        for half in range(2):
            def add_z(p, _):
                at = plane(p + 8 * half)
                v = pb[at, :] + zrF[0, at, :] + zrF[1, at, :]
                back = mod(L - p * REACH, L)
                low = pltpu.roll(cols[0][half], mod(back + L - REACH, L), 1)
                high = pltpu.roll(cols[1][half], back, 1)
                for k, part_ in enumerate((v, jnp.where(lane < L // 2, high, low))):
                    big, small = split(part_)
                    xin[at, pl.ds(k * L, L)] = big
                    xin[plane(p + 8 * half + D), pl.ds(k * L, L)] = small
                return 0
            each(8, add_z, 0, WIDTH['add_z'])
        both = lax.dot_general(xin[...], bx[...], (((1,), (1,)), ((), ())), preferred_element_type=F32)
        grad_o[...] = both[:D * H] + both[D * H:]

        for cond, copy in sent:
            pl.when(cond)(copy.wait_send)
        for stage in stages:
            for d in range(1, stages[stage][0]):
                sum_copy(stage, d, False).wait_send()
        adj_copy.wait()

    return kernel


def solution(mesh):
    sizes = dict(mesh.shape)
    nz, ny, nx = (sizes[a] for a in AXES)
    rows = D * H
    vm = lambda *shape: pltpu.VMEM(shape, F32)
    field = vm(rows, L)

    def halo(planes, tiles):
        y = vm(2, planes * D, L)
        z = vm(2, planes * H, L)
        return [z, y, vm(tiles, H, L), z, y, vm(2, tiles, H, L)]

    scratch = [
        vm(6 * rows, L), vm(6 * rows, L), field, pltpu.VMEM((rows, L), jnp.int32), pltpu.VMEM((rows, L), jnp.int32),
        vm(8 * rows, L), vm(8 * rows, L), vm(8 * rows, L),
    ] + [field] * 13 + [vm(3 * rows, L)] + halo(7, 2) + halo(6, 2) + halo(8, 2) + [
        vm(2, 3 * H, L), vm(2, 3 * D, L), vm(1, H, L), vm(2, 3 * H, L), vm(2, 3 * D, L), vm(2, 1, H, L),
        pltpu.VMEM((3 * rows, 2 * L), BF16), pltpu.VMEM((3 * rows, 2 * L), BF16), pltpu.VMEM((L, 2 * L), BF16),
        field, vm(2, rows, L), vm(2, rows, L), vm(2, rows, L), vm(2, rows, L),
        vm(2, 3, 2, H, L), vm(2, 3, 2, H, L),
        pltpu.VMEM((rows, 2 * L), BF16), pltpu.VMEM((2 * rows, 2 * L), BF16),
    ] + [vm(n, 2, L) for n in (CORES, nx, ny, nz // CORES)] + [
        pltpu.SemaphoreType.DMA((5,)), pltpu.SemaphoreType.DMA,
        pltpu.SemaphoreType.DMA((34,)), pltpu.SemaphoreType.DMA((34,)),
    ] + [pltpu.SemaphoreType.DMA((n,)) for n in (CORES, nx, ny, nz // CORES) for _ in range(2)]
    hbm = pl.BlockSpec(memory_space=pl.ANY)
    smem = pl.BlockSpec(memory_space=pltpu.SMEM)
    vmem = pl.BlockSpec(memory_space=pltpu.VMEM)
    call = pl.pallas_call(
        make_kernel(sizes),
        out_shape=(
            jax.ShapeDtypeStruct((6 * rows, L), F32),
            jax.ShapeDtypeStruct((rows, L), F32),
            jax.ShapeDtypeStruct((2,), F32),
        ),
        in_specs=[hbm] * 5 + [smem] * 3 + [vmem],
        out_specs=(hbm, vmem, smem),
        scratch_shapes=scratch,
        compiler_params=pltpu.CompilerParams(
            collective_id=0, has_side_effects=True, vmem_limit_bytes=62 * 2**20),
    )

    def body(forward, adjoint_prev, density, labels, ports, z_target, radius_z, radius_y, radius_x):
        adjoint, gradient, impedance = call(
            forward.reshape(6 * rows, L), adjoint_prev.reshape(6 * rows, L), density.reshape(rows, L),
            labels.reshape(rows, L), ports.reshape(rows, L), z_target, radius_z, radius_y,
            radius_x.reshape(nx, L))
        return adjoint.reshape(6, D, H, L), gradient.reshape(D, H, L), impedance

    in_specs = (P(None, *AXES),) * 2 + (P(*AXES),) * 3 + (P(),) * 4
    out_specs = (P(None, *AXES), P(*AXES), P())
    return jax.shard_map(body, mesh=mesh, in_specs=in_specs, out_specs=out_specs, check_vma=False)
```

```python
import jax
import jax.numpy as jnp
from jax import lax
from jax.experimental import pallas as pl
from jax.experimental.pallas import tpu as pltpu
from jax.sharding import PartitionSpec as P

MU_GAIN = 19.0
KAPPA_GAIN = 2.0
RELAX = 0.8
SENS_GAIN = 0.1
REACH = 16
CORES = 2
WIDTH = dict(add_x=16, add_y=16, add_z=8, build=4, build_x=4, diagonal=16, faces=16, inner1=16, inner2=16, material=16, pack0=16, packf=16, sens=16, step=8, sweep1=16, sweep2=16, reluctivity=16, join=16, answer=16)
MESH = pl.DeviceIdType.MESH
AXES = ("gz", "gy", "gx")
F32 = jnp.float32
BF16 = jnp.bfloat16
D = 16
H = 16
L = 128


def plane(index):
    if isinstance(index, int):
        return pl.ds(index * H, H)
    return pl.ds(pl.multiple_of(index * H, H), H)


def each(count, step, carry, width):
    if width == count:
        for k in range(count):
            carry = step(k, carry)
        return carry

    def group(g, carry):
        for k in range(width):
            carry = step(g * width + k, carry)
        return carry

    return lax.fori_loop(0, count // width, group, carry)


def mod(a, b):
    return a % b if isinstance(a, int) else lax.rem(a, b)


def clamp(value):
    if isinstance(value, int):
        return min(max(value, 0), D - 1)
    return jnp.clip(value, 0, D - 1)


def tri(value):
    value = jnp.maximum(value, 0)
    return value * (value + 1) // 2


def norm_of(radius, position, length):
    whole = (radius + 1) * (radius + 1)
    return whole - tri(radius - position) - tri(radius - (length - 1 - position))


def make_kernel(sizes):
    nz, ny, nx = sizes["gz"], sizes["gy"], sizes["gx"]
    total = {"gz": nz * D, "gy": ny * H, "gx": nx * L}
    scale = 4.0 / (total["gz"] * total["gy"] * total["gx"])

    def kernel(fwd_h, adj_h, den_h, lab_h, prt_h, zt_h, rz_h, ry_h, rx_h,
               adj_o, grad_o, imp_o,
               zt, rz, ry, rx, f, a0, den, lab, prt, a1, a2, t,
               nu, kap, wzm, wzp, wym, wyp, wxm, wxp, al, be, hx, kk, qq, s,
               zs0, ys0, xs0, zr0, yr0, xr0,
               zsf, ysf, xsf, zrf, yrf, xrf,
               zs1, ys1, xs1, zr1, yr1, xr1,
               zs2, ys2, xs2, zr2, yr2, xr2,
               ky, kz, bx, ysF, yrF, zsF, zrF, ysG, yrG, zsG, zrG, oyF, ozF, oyG, ozG,
               stA, srA, stB, srB, vbA, vbB, xin,
               sum_core, sum_x, sum_y, sum_z, in_sem, out_sem, grad, ss, rs,
               ss_core, rs_core, ss_x, rs_x, ss_y, rs_y, ss_z, rs_z):
        sums = {"core": sum_core, "gx": sum_x, "gy": sum_y, "gz": sum_z}
        sum_ss = {"core": ss_core, "gx": ss_x, "gy": ss_y, "gz": ss_z}
        sum_rs = {"core": rs_core, "gx": rs_x, "gy": rs_y, "gz": rs_z}
        gz, gy, gx = (lax.axis_index(a) for a in AXES)
        pos = {"gz": gz, "gy": gy, "gx": gx}
        core = lax.rem(gz, CORES)

        def inside(axis, d):
            size = {"gz": nz, "gy": ny, "gx": nx}[axis]
            return pos[axis] < size - 1 if d > 0 else pos[axis] > 0

        stages = {
            "core": (CORES, lambda d: {"gz": gz - core + lax.rem(core + d, CORES)}, core),
            "gx": (nx, lambda d: {"gx": lax.rem(gx + d, nx)}, gx),
            "gy": (ny, lambda d: {"gy": lax.rem(gy + d, ny)}, gy),
            "gz": (nz // CORES, lambda d: {"gz": lax.rem(gz + CORES * d, nz)}, gz // CORES),
        }
        barrier = pltpu.get_barrier_semaphore()
        others = []
        for axis, dx in (("gz", 1), ("gy", -1)):
            for d in (-1, 1):
                others.append(({axis: pos[axis] + d, "gx": gx + dx},
                               jnp.logical_and(inside(axis, d), inside("gx", dx)),
                               jnp.logical_and(inside(axis, -d), inside("gx", -dx))))
        for d in (-1, 1):
            near = jnp.logical_and(inside("gz", d), (core == 0) if d < 0 else (core == CORES - 1))
            others.append(({"gz": gz + d}, near, near))
        expected = 0
        for members, peer, _ in stages.values():
            for d in range(1, members):
                pl.semaphore_signal(barrier, inc=1, device_id=peer(d), device_id_type=MESH)
                expected += 1
        for where, comes, goes in others:
            @pl.when(comes)
            def _():
                pl.semaphore_signal(barrier, inc=1, device_id=where, device_id_type=MESH)
            expected = expected + goes.astype(jnp.int32)

        loads = [
            pltpu.make_async_copy(src, dst, in_sem.at[k])
            for k, (src, dst) in enumerate((
                (den_h, den), (lab_h, lab), (adj_h, a0), (fwd_h, f), (prt_h, prt),
                (rx_h, rx), (ry_h, ry), (rz_h, rz), (zt_h, zt)))
        ]
        for load in loads[5:] + loads[:5]:
            load.start()

        def remote(src, dst, slot, where):
            return pltpu.make_async_remote_copy(
                src_ref=src, dst_ref=dst, send_sem=ss.at[slot], recv_sem=rs.at[slot],
                device_id=where, device_id_type=MESH)

        sent = []

        def beside(axis, d, src, dst, slot):
            copy = remote(src, dst, slot, {axis: pos[axis] + d})
            pl.when(inside(axis, d))(copy.start)
            sent.append((inside(axis, d), copy))
            return (inside(axis, -d), copy)

        def arrive(copies):
            for cond, copy in copies:
                pl.when(cond)(copy.wait_recv)

        def exchange(base, zs, zr, ys, yr, xs, xr):
            copies = []
            for axis, src, dst, k in (("gy", ys, yr, 2), ("gx", xs, xr, 4), ("gz", zs, zr, 0)):
                for d in (-1, 1):
                    side = 0 if d < 0 else 1
                    piece = src if axis == "gx" else src.at[side]
                    copies.append(beside(axis, d, piece, dst.at[1 - side], base + k + side))
            return copies

        edges = {axis: (pos[axis] == 0, pos[axis] == {"gz": nz, "gy": ny, "gx": nx}[axis] - 1) for axis in AXES}
        for axis, bufs in (("gz", (zr0, zrf, zr1, zr2, zrF, zrG)), ("gy", (yr0, yrf, yr1, yr2, yrF, yrG)),
                           ("gx", (xr0, xrf, xr1, xr2))):
            for side in (0, 1):
                @pl.when(edges[axis][side])
                def _():
                    for buf in bufs:
                        buf[side] = jnp.zeros(buf.shape[1:], F32)
                    if axis == "gx":
                        column = lax.rem(lax.broadcasted_iota(jnp.int32, (H, L), 1), 8)
                        xr0[side, 1] = jnp.where(column // 2 == 2, 1.0, 0.0).astype(F32)
                    else:
                        buf = zr0 if axis == "gz" else yr0
                        buf[side, pl.ds(6 * H, H), :] = jnp.ones((H, L), F32)
        for strip, axis, side in ((srA, "gz", 1), (srB, "gy", 0)):
            for cond, slots in ((edges["gx"][side], (0, 1, 2)), (edges[axis][0], (1,)), (edges[axis][1], (2,))):
                @pl.when(cond)
                def _():
                    for slot in slots:
                        strip[slot] = jnp.zeros(strip.shape[1:], F32)

        lane = lax.broadcasted_iota(jnp.int32, (H, L), 1)
        row = lax.broadcasted_iota(jnp.int32, (H, L), 0)

        loads[0].wait()
        loads[1].wait()

        def reluctivity(z, _):
            density = den[plane(z), :]
            design = jnp.where(lab[plane(z), :] == 2, 1.0, 0.0).astype(F32)
            cube = density * density * density
            nu_design = 1.0 / (1.0 + MU_GAIN * cube)
            nu[plane(z), :] = 1.0 - design + design * nu_design
            kap[plane(z), :] = design * KAPPA_GAIN * cube
            return 0

        each(D, reluctivity, 0, WIDTH['reluctivity'])

        def pack(z, tiles, values):
            out = list(tiles)
            for c, v in enumerate(values):
                moved = pltpu.roll(v, (z * 8 + 2 * (c % 4) + 1) % L, 1)
                out[c // 4] = jnp.where(lane // 2 == z * 4 + c % 4, moved, out[c // 4])
            return tuple(out)

        def pair(xr, n):
            below = pltpu.roll(xr[0, n], 1, 1)
            above = pltpu.roll(xr[1, n], L - 1, 1)
            return jnp.where(lax.rem(lane, 2) == 0, above, below)

        def unpack(tile, z, count, first=0):
            return [pltpu.roll(tile, (-z * 8 - 2 * c - 1) % L, 1) for c in range(first, first + count)]

        zero = jnp.zeros((H, L), F32)

        def cell_rows(ref, count, first):
            return ref[pl.ds(first, count * D, stride=H), :]

        loads[2].wait()
        for side, z in ((0, 0), (1, D - 1)):
            for c in range(6):
                zs0[side, pl.ds(c * H, H), :] = a0[pl.ds((c * D + z) * H, H), :]
            zs0[side, pl.ds(6 * H, H), :] = nu[pl.ds(z * H, H), :]
            ys0[side, pl.ds(0, 6 * D), :] = cell_rows(a0, 6, side * (H - 1))
            ys0[side, pl.ds(6 * D, D), :] = cell_rows(nu, 1, side * (H - 1))

        def pack0(z, tiles):
            return pack(z, tiles, [a0[plane(c * D + z), :] for c in range(6)] + [nu[plane(z), :]])

        tiles = each(D, pack0, (zero, zero), WIDTH['pack0'])
        xs0[0] = tiles[0]
        xs0[1] = tiles[1]

        pl.semaphore_wait(barrier, expected)
        got0 = exchange(0, zs0, zr0, ys0, yr0, xs0, xr0)

        def sum_copy(stage, d, arriving):
            members, peer, slot = stages[stage]
            at = lax.rem(slot + d, members) if arriving else slot
            ref = sums[stage].at[at]
            return pltpu.make_async_remote_copy(
                src_ref=ref, dst_ref=ref, send_sem=sum_ss[stage].at[d], recv_sem=sum_rs[stage].at[at],
                device_id=peer(d), device_id_type=MESH)

        def sum_start(stage, value):
            members, _, slot = stages[stage]
            sums[stage][slot] = value
            for d in range(1, members):
                sum_copy(stage, d, False).start()

        def sum_finish(stage):
            members = stages[stage][0]
            for d in range(1, members):
                sum_copy(stage, d, True).wait_recv()
            value = sums[stage][0]
            for q in range(1, members):
                value = value + sums[stage][q]
            return value

        loads[3].wait()
        loads[4].wait()
        for side, z in ((0, 0), (1, D - 1)):
            for c in range(6):
                zsf[side, pl.ds(c * H, H), :] = f[pl.ds((c * D + z) * H, H), :]
            ysf[side] = cell_rows(f, 6, side * (H - 1))

        def packf(z, carry):
            tiles, re, im = carry
            values = [f[plane(c * D + z), :] for c in range(6)]
            mask = prt[plane(z), :].astype(F32)
            return (pack(z, tiles, values), re + mask * values[2], im + mask * values[5])

        tiles, port_re, port_im = each(D, packf, ((zero, zero), zero, zero), WIDTH['packf'])
        xsf[0] = tiles[0]
        xsf[1] = tiles[1]
        port_sum = jnp.concatenate(
            [jnp.sum(port_re, axis=0, keepdims=True), jnp.sum(port_im, axis=0, keepdims=True)], axis=0)

        sum_start("core", port_sum)

        def faces(z, _):
            v = nu[plane(z), :]
            below = nu[plane(clamp(z - 1)), :]
            above = nu[plane(clamp(z + 1)), :]
            wzm[plane(z), :] = jnp.where(z > 0, 0.5 * (v + below), 0.0)
            wzp[plane(z), :] = jnp.where(z < D - 1, 0.5 * (v + above), 0.0)
            wym[plane(z), :] = jnp.where(row > 0, 0.5 * (v + pltpu.roll(v, 1, 0)), 0.0)
            wyp[plane(z), :] = jnp.where(row < H - 1, 0.5 * (v + pltpu.roll(v, H - 1, 0)), 0.0)
            wxm[plane(z), :] = jnp.where(lane > 0, 0.5 * (v + pltpu.roll(v, 1, 1)), 0.0)
            wxp[plane(z), :] = jnp.where(lane < L - 1, 0.5 * (v + pltpu.roll(v, L - 1, 1)), 0.0)
            return 0

        each(D, faces, 0, WIDTH['faces'])

        def inner(a, count, z, begin):
            zm = clamp(z - 1)
            zp = clamp(z + 1)
            w = [ref[plane(z), :] for ref in (wzm, wzp, wym, wyp, wxm, wxp)]
            for c in range(count):
                v = a[plane(c * D + z), :]
                total_ = w[0] * a[plane(c * D + zm), :] + w[1] * a[plane(c * D + zp), :]
                total_ += w[2] * pltpu.roll(v, 1, 0) + w[3] * pltpu.roll(v, H - 1, 0)
                total_ += w[4] * pltpu.roll(v, 1, 1) + w[5] * pltpu.roll(v, L - 1, 1)
                first = begin(c)
                t[plane(c * D + z), :] = total_ if first is None else total_ + first

        def inner1(z, _):
            kappa = kap[plane(z), :]
            inner(a0, 6, z, lambda c: kappa * f[plane(c * D + z), :])
            return 0

        each(D, inner1, 0, WIDTH['inner1'])
        sum_start("gx", sum_finish("core"))
        gotf = exchange(6, zsf, zrf, ysf, yrf, xsf, xrf)

        arrive(got0)
        x0 = [pair(xr0, 0), pair(xr0, 1)]
        outer_x = jnp.logical_or(lane == 0, lane == L - 1)

        hz = []
        hy = []
        for side, z in ((0, 0), (1, D - 1)):
            hz.append(0.5 * (nu[pl.ds(z * H, H), :] + zr0[side, pl.ds(6 * H, H), :]))
            hy.append(0.5 * (cell_rows(nu, 1, side * (H - 1)) + yr0[side, pl.ds(6 * D, D), :]))

        def add_outer(zr, yr, count):
            for side, z in ((0, 0), (1, D - 1)):
                for c in range(count):
                    t[pl.ds((c * D + z) * H, H), :] += hz[side] * zr[side, pl.ds(c * H, H), :]
                for c in range(count):
                    at = pl.ds(c * D * H + side * (H - 1), D, stride=H)
                    t[at, :] = t[at, :] + hy[side] * yr[side, pl.ds(c * D, D), :]

        add_outer(zr0, yr0, 6)
        def diagonal(z, _):
            total_ = wzm[plane(z), :] + wzp[plane(z), :] + wym[plane(z), :] + wyp[plane(z), :]
            v = nu[plane(z), :]
            outside = unpack(x0[1], z, 1, 2)[0]
            face = jnp.where(outer_x, 0.5 * (v + outside), 0.0)
            hx[plane(z), :] = face
            al[plane(z), :] = total_ + wxm[plane(z), :] + wxp[plane(z), :] + face
            return 0

        each(D, diagonal, 0, WIDTH['diagonal'])
        for side, z in ((0, 0), (1, D - 1)):
            al[pl.ds(z * H, H), :] += hz[side]
            at = pl.ds(side * (H - 1), D, stride=H)
            al[at, :] = al[at, :] + hy[side]

        def finish(z, a, tiles_in, count):
            alpha = al[plane(z), :]
            beta = be[plane(z), :]
            face = hx[plane(z), :]
            outside = unpack(tiles_in[0], z, 4) + unpack(tiles_in[1], z, count - 4)
            tt = [t[plane(c * D + z), :] + face * outside[c] for c in range(count)]
            out = [None] * count
            pairs = [(0, 3), (1, 4), (2, 5)] + ([(6, 7)] if count == 8 else [])
            for re, im in pairs:
                out[re] = (1.0 - RELAX) * a[plane(re * D + z), :] + (tt[re] * alpha + tt[im] * beta)
                out[im] = (1.0 - RELAX) * a[plane(im * D + z), :] + (tt[im] * alpha - tt[re] * beta)
            return out

        def sweep1(z, tiles):
            d = al[plane(z), :]
            kappa = kap[plane(z), :]
            weight = RELAX / (d * d + kappa * kappa)
            al[plane(z), :] = d * weight
            be[plane(z), :] = kappa * weight
            out = finish(z, a0, x0, 6)
            mask = prt[plane(z), :].astype(F32)
            out.append(mask * (d * weight))
            out.append(-mask * (kappa * weight))
            for c in range(8):
                a1[plane(c * D + z), :] = out[c]
            return pack(z, tiles, out)

        tiles = each(D, sweep1, (zero, zero), WIDTH['sweep1'])
        xs1[0] = tiles[0]
        xs1[1] = tiles[1]
        for side, z in ((0, 0), (1, D - 1)):
            for c in range(8):
                zs1[side, pl.ds(c * H, H), :] = a1[pl.ds((c * D + z) * H, H), :]
            ys1[side] = cell_rows(a1, 8, side * (H - 1))
        got1 = exchange(12, zs1, zr1, ys1, yr1, xs1, xr1)

        sum_start("gy", sum_finish("gx"))

        def inner2(z, _):
            kappa = kap[plane(z), :]

            def begin(c):
                if c < 6:
                    return kappa * f[plane(c * D + z), :]
                return prt[plane(z), :].astype(F32) if c == 6 else None

            inner(a1, 8, z, begin)
            return 0

        each(D, inner2, 0, WIDTH['inner2'])
        for load in loads[5:]:
            load.wait()
        ry_l = jnp.zeros((H, L), jnp.int32)
        rz_l = jnp.zeros((H, L), jnp.int32)
        ry_r = jnp.zeros((H, L), jnp.int32)
        for b in range(H):
            ry_b = ry[gy * H + b]
            rz_b = rz[gz * D + b]
            ry_l = jnp.where(lax.rem(lane, H) == b, ry_b, ry_l)
            rz_l = jnp.where(lane // 8 == b, rz_b, rz_l)
            ry_r = jnp.where(row == b, ry_b, ry_r)

        def build(k, _):
            n = k // 8
            q = mod(k, 8)
            band_y = jnp.maximum(ry_l + 1 - jnp.abs(lax.rem(lane, H) - (row + (n - 1) * H)), 0)
            ky[plane(k), :] = jnp.where(lane // H == q, band_y, 0).astype(F32).astype(BF16)
            band_z = jnp.maximum(rz_l + 1 - jnp.abs(lane // 8 - (2 * q + row // 8 + (n - 1) * D)), 0)
            kz[plane(k), :] = jnp.where(lax.rem(lane, 8) == lax.rem(row, 8), band_z, 0).astype(F32).astype(BF16)
            return 0

        each(24, build, 0, WIDTH['build'])
        rx_own = jnp.broadcast_to(rx[pl.ds(gx, 1), :], (H, L))
        rx_low = jnp.broadcast_to(rx[pl.ds(jnp.maximum(gx - 1, 0), 1), :], (H, L))
        rx_high = jnp.broadcast_to(rx[pl.ds(jnp.minimum(gx + 1, nx - 1), 1), :], (H, L))

        def build_x(k, _):
            target = row + k * H
            own = jnp.maximum(rx_own + 1 - jnp.abs(lane - target), 0)
            low = jnp.maximum(rx_low + 1 - jnp.abs(lane - L - target), 0)
            high = jnp.maximum(rx_high + 1 - jnp.abs(lane + L - target), 0)
            bx[plane(k), pl.ds(0, L)] = own.astype(F32).astype(BF16)
            bx[plane(k), pl.ds(L, L)] = jnp.where(lane < L // 2, high, low).astype(F32).astype(BF16)
            return 0

        each(L // H, build_x, 0, WIDTH['build_x'])
        norm_yx = (norm_of(ry_r, gy * H + row, total["gy"]) * norm_of(rx_own, gx * L + lane, total["gx"])).astype(F32)

        def material(z, _):
            density = den[plane(z), :]
            design = jnp.where(lab[plane(z), :] == 2, 1.0, 0.0).astype(F32)
            square = density * density
            cube = square * density
            nu_design = 1.0 / (1.0 + MU_GAIN * cube)
            gz_i = gz * D + z
            norm_z = norm_of(rz[gz_i], gz_i, total["gz"]).astype(F32)
            inverse = SENS_GAIN / (norm_yx * norm_z)
            nu_slope = -3.0 * MU_GAIN * design * square * nu_design * nu_design
            kk[plane(z), :] = -0.5 * nu_slope * inverse
            qq[plane(z), :] = 3.0 * KAPPA_GAIN * design * square * inverse
            return 0

        each(D, material, 0, WIDTH['material'])

        sum_start("gz", sum_finish("gy"))
        arrive(gotf)
        xf = [pair(xrf, 0), pair(xrf, 1)]
        arrive(got1)
        add_outer(zr1, yr1, 8)
        x1 = [pair(xr1, 0), pair(xr1, 1)]

        def shares(answers, near):
            main = None
            for c in range(6):
                term = answers[c] * near[c]
                main = term if c == 0 else main + term if c < 3 else main - term
            return [main, answers[6] * near[2] - answers[7] * near[5], -(answers[7] * near[2]) - answers[6] * near[5]]

        def sweep2(z, tile):
            out = finish(z, a1, x1, 8)
            for c in range(8):
                a2[plane(c * D + z), :] = out[c]
            outside = unpack(xf[0], z, 4) + unpack(xf[1], z, 2)
            near = [f[plane(c * D + z), :] - outside[c] for c in range(6)]
            share = [jnp.where(outer_x, v, 0.0) for v in shares(out, near)]
            for k in range(3):
                t[plane(k * D + z), :] = share[k]
            return pack(z, (tile,), share)[0]

        xs2[0] = each(D, sweep2, zero, WIDTH['sweep2'])
        hz2 = []
        hy2 = []
        for side, z in ((0, 0), (1, D - 1)):
            at = [pl.ds((c * D + z) * H, H) for c in range(8)]
            near = [f[at[c], :] - zrf[side, pl.ds(c * H, H), :] for c in range(6)]
            share = shares([a2[where, :] for where in at], near)
            for k in range(3):
                zs2[side, pl.ds(k * H, H), :] = share[k]
            hz2.append(share)
            at = [pl.ds(c * D * H + side * (H - 1), D, stride=H) for c in range(8)]
            near = [f[at[c], :] - yrf[side, pl.ds(c * D, D), :] for c in range(6)]
            share = shares([a2[where, :] for where in at], near)
            for k in range(3):
                ys2[side, pl.ds(k * D, D), :] = share[k]
            hy2.append(share)
        got2 = exchange(18, zs2, zr2, ys2, yr2, xs2, xr2)

        def sens(z, last):
            zp = clamp(z + 1)
            av = [a2[plane(c * D + z), :] for c in range(8)]
            fv = [f[plane(c * D + z), :] for c in range(6)]
            above = [a2[plane(c * D + zp), :] for c in range(8)], [f[plane(c * D + zp), :] for c in range(6)]
            ez = shares([v - w for v, w in zip(av, above[0])], [v - w for v, w in zip(fv, above[1])])
            ey = shares([v - pltpu.roll(v, H - 1, 0) for v in av], [v - pltpu.roll(v, H - 1, 0) for v in fv])
            ex = shares([v - pltpu.roll(v, L - 1, 1) for v in av], [v - pltpu.roll(v, L - 1, 1) for v in fv])
            more = [zero, av[6] * fv[5] + av[7] * fv[2], av[6] * fv[2] - av[7] * fv[5]]
            for c in range(6):
                more[0] = more[0] + fv[c] * (fv[c] + av[(c + 3) % 6])
            for k in range(3):
                along_y = jnp.where(row < H - 1, ey[k], 0.0)
                along_x = jnp.where(lane < L - 1, ex[k], 0.0)
                energy = ez[k] + last[k] + along_y + pltpu.roll(along_y, 1, 0)
                energy = energy + along_x + pltpu.roll(along_x, 1, 1) + t[plane(k * D + z), :]
                s[plane(k * D + z), :] = kk[plane(z), :] * energy + qq[plane(z), :] * more[k]
            return ez

        each(D, sens, [zero] * 3, WIDTH['sens'])
        total_ports = sum_finish("gz")
        link_re = scale * jnp.sum(total_ports[0:1])
        link_im = scale * jnp.sum(total_ports[1:2])
        imp_o[0] = link_re
        imp_o[1] = link_im
        coef_re = 2.0 * (link_re - zt[0])
        coef_im = -2.0 * (link_im - zt[1])

        def joined(parts):
            return parts[0] + (coef_re * parts[1] + coef_im * parts[2])

        def join(z, _):
            s[plane(z), :] = joined([s[plane(k * D + z), :] for k in range(3)])
            return 0

        each(D, join, 0, WIDTH['join'])
        for side, z in ((0, 0), (1, D - 1)):
            at = pl.ds(z * H, H)
            s[at, :] += kk[at, :] * joined(hz2[side])
            at = pl.ds(side * (H - 1), D, stride=H)
            s[at, :] = s[at, :] + kk[at, :] * joined(hy2[side])
        arrive(got2)
        for side, z in ((0, 0), (1, D - 1)):
            at = pl.ds(z * H, H)
            s[at, :] += kk[at, :] * joined([zr2[side, pl.ds(k * H, H), :] for k in range(3)])
            at = pl.ds(side * (H - 1), D, stride=H)
            s[at, :] = s[at, :] + kk[at, :] * joined([yr2[side, pl.ds(k * D, D), :] for k in range(3)])
        tile2 = pair(xr2, 0)
        tile2 = joined([tile2, pltpu.roll(tile2, L - 2, 1), pltpu.roll(tile2, L - 4, 1)])

        def add_x(z, _):
            outside = unpack(tile2, z, 1)[0]
            s[plane(z), :] += kk[plane(z), :] * jnp.where(outer_x, outside, 0.0)
            return 0

        each(D, add_x, 0, WIDTH['add_x'])

        lane8 = lax.broadcasted_iota(jnp.int32, (8, L), 1)
        left = lane < L // 2
        left8 = lane8 < L // 2

        def turn(v):
            return pltpu.roll(v, L // 2, 1)

        def split(v):
            high = v.astype(BF16)
            return high, (v - high.astype(F32)).astype(BF16)

        def keep(ref, k, v):
            high, low = split(v)
            ref[pl.ds(k * H, H), pl.ds(0, L)] = high
            ref[pl.ds(k * H, H), pl.ds(L, L)] = low

        def stack(a, b):
            return jnp.concatenate([a, b], axis=0)

        def band(matrix, value, dst_low, dst_own, dst_high):
            for n, dst in ((0, dst_low), (2, dst_high), (1, dst_own)):
                both = jnp.dot(matrix[pl.ds(n * L, L), :], value[...], preferred_element_type=F32)
                dst[...] = both[:, :L] + both[:, L:]

        def both_ways(axis, src, dst, slot):
            return [beside(axis, d, src.at[side], dst.at[1 - side], slot + side) for side, d in ((0, -1), (1, 1))]

        for p in range(8):
            keep(vbA, p, jnp.where(left, s[plane(p), :], turn(s[plane(p + 8), :])))
        band(ky, vbA, ysF.at[0], oyF, ysF.at[1])
        gotY = both_ways("gy", ysF, yrF, 24)
        for k in range(8):
            tiles = []
            for z in (2 * k, 2 * k + 1):
                v = s[plane(z), :]
                tiles.append(jnp.where(left8, turn(v[:8]), v[8:]))
            keep(vbB, k, stack(*tiles))
        band(kz, vbB, zsF.at[0], ozF, zsF.at[1])
        gotZ = both_ways("gz", zsF, zrF, 26)

        def answer(z, _):
            re, im = a2[plane(6 * D + z), :], a2[plane(7 * D + z), :]
            added = {2: coef_re * re - coef_im * im, 5: coef_re * im + coef_im * re}
            for c in added:
                a2[plane(c * D + z), :] += added[c]
            return 0

        each(D, answer, 0, WIDTH['answer'])
        adj_copy = pltpu.make_async_copy(a2.at[pl.ds(0, 6 * D * H), :], adj_o, out_sem.at[0])
        adj_copy.start()

        def eight(ref, k):
            return ref[pl.ds(8 * k, 8), :]

        arrive(gotZ)
        vz = [eight(ozF, z) + eight(zrF.at[0], z) + eight(zrF.at[1], z) for z in range(D)]
        for p in range(8):
            low, high = vz[p], vz[p + 8]
            keep(vbB, p, stack(jnp.where(left8, low, turn(high)), jnp.where(left8, turn(low), high)))
        band(ky, vbB, ysG.at[0], oyG, ysG.at[1])
        gotY2 = both_ways("gy", ysG, yrG, 30)
        arrive(gotY)
        vy = [oyF[plane(p), :] + yrF[0, plane(p), :] + yrF[1, plane(p), :] for p in range(8)]
        for k in range(4):
            near, far = [], []
            for p in (2 * k, 2 * k + 1):
                top, bottom = vy[p][:8], vy[p][8:]
                near.append(jnp.where(left8, top, turn(bottom)))
                far.append(jnp.where(left8, turn(top), bottom))
            keep(vbA, k, stack(*near))
            keep(vbA, k + 4, stack(*far))
        band(kz, vbA, zsG.at[0], ozG, zsG.at[1])
        gotZ2 = both_ways("gz", zsG, zrG, 28)

        def columns(dst, src, count, rows_, offset, lanes):
            for g in range(count // 4):
                tile = None
                for q in range(4):
                    moved = pltpu.roll(src[pl.ds((4 * g + q) * rows_, rows_), :], (16 * q - offset) % L, 1)
                    tile = moved if q == 0 else jnp.where(lax.rem(lanes // REACH, 4) == q, moved, tile)
                dst[pl.ds(g * rows_, rows_), :] = tile

        gotX = []
        for axis, dx, st, sr, src, slot in (("gy", 1, stB, srB, (oyG, ysG.at[0], ysG.at[1]), 35),
                                            ("gz", -1, stA, srA, (ozG, zsG.at[0], zsG.at[1]), 32)):
            for n, d in ((0, 0), (1, -1), (2, 1)):
                if axis == "gz":
                    columns(st.at[n], src[n], D, 8, 0, lane8)
                else:
                    columns(st.at[n], src[n], 8, H, 48, lane)
                if d == 0:
                    gotX.append(beside("gx", dx, st.at[0], sr.at[0], slot))
                    continue
                go = jnp.logical_and(inside("gx", dx), inside(axis, d))
                come = jnp.logical_and(inside("gx", -dx), inside(axis, -d))
                copy = remote(st.at[n], sr.at[3 - n], slot + n, {axis: pos[axis] + d, "gx": gx + dx})
                pl.when(go)(copy.start)
                sent.append((go, copy))
                gotX.append((come, copy))
        arrive(gotY2)
        arrive(gotZ2)
        arrive(gotX)
        ga = [sum(srA[n, pl.ds(8 * g, 8), :] for n in range(3)) for g in range(4)]
        gb = [sum(srB[n, plane(g), :] for n in range(3)) for g in range(2)]
        vy = [oyG[plane(p), :] + yrG[0, plane(p), :] + yrG[1, plane(p), :] for p in range(8)]
        for z in range(D):
            v = eight(ozG, z) + eight(zrG.at[0], z) + eight(zrG.at[1], z)
            own = jnp.where(left, stack(v, turn(v)), turn(vy[z]) if z < 8 else vy[z - 8])
            group = ga[z // 4]
            above = stack(*(pltpu.roll(group, (-16 * (z % 4) - 64 * h) % L, 1) for h in range(2)))
            below = pltpu.roll(gb[z % 8 // 4], (112 - 64 * (z // 8) - 16 * (z % 4)) % L, 1)
            for k, part in enumerate((own, jnp.where(left, above, below))):
                big, small = split(part)
                xin[plane(z), pl.ds(k * L, L)] = big
                xin[plane(z + D), pl.ds(k * L, L)] = small
        both = lax.dot_general(xin[...], bx[...], (((1,), (1,)), ((), ())), preferred_element_type=F32)
        grad[...] = both[:D * H] + both[D * H:]
        grad_copy = pltpu.make_async_copy(grad, grad_o, out_sem.at[1])
        grad_copy.start()

        for cond, copy in sent:
            pl.when(cond)(copy.wait_send)
        for stage in stages:
            for d in range(1, stages[stage][0]):
                sum_copy(stage, d, False).wait_send()
        adj_copy.wait()
        grad_copy.wait()

    return kernel


def solution(mesh):
    sizes = dict(mesh.shape)
    nz, ny, nx = (sizes[a] for a in AXES)
    rows = D * H
    vm = lambda *shape: pltpu.VMEM(shape, F32)
    field = vm(rows, L)

    def halo(planes, tiles):
        y = vm(2, planes * D, L)
        z = vm(2, planes * H, L)
        return [z, y, vm(tiles, H, L), z, y, vm(2, tiles, H, L)]

    scratch = [
        pltpu.SMEM((2,), F32), pltpu.SMEM((nz * D,), jnp.int32), pltpu.SMEM((ny * H,), jnp.int32),
        pltpu.VMEM((nx, L), jnp.int32),
        vm(6 * rows, L), vm(6 * rows, L), field, pltpu.VMEM((rows, L), jnp.int32), pltpu.VMEM((rows, L), jnp.int32),
        vm(8 * rows, L), vm(8 * rows, L), vm(8 * rows, L),
    ] + [field] * 13 + [vm(3 * rows, L)] + halo(7, 2) + halo(6, 2) + halo(8, 2) + [
        vm(2, 3 * H, L), vm(2, 3 * D, L), vm(1, H, L), vm(2, 3 * H, L), vm(2, 3 * D, L), vm(2, 1, H, L),
        pltpu.VMEM((3 * L, L), BF16), pltpu.VMEM((3 * L, L), BF16), pltpu.VMEM((L, 2 * L), BF16),
    ] + [vm(2, L, L)] * 8 + [vm(L, L)] * 4 + [vm(3, 32, L)] * 4 + [
        pltpu.VMEM((L, 2 * L), BF16), pltpu.VMEM((L, 2 * L), BF16), pltpu.VMEM((2 * rows, 2 * L), BF16),
    ] + [vm(n, 2, L) for n in (CORES, nx, ny, nz // CORES)] + [
        pltpu.SemaphoreType.DMA((9,)), pltpu.SemaphoreType.DMA((2,)), field,
        pltpu.SemaphoreType.DMA((38,)), pltpu.SemaphoreType.DMA((38,)),
    ] + [pltpu.SemaphoreType.DMA((n,)) for n in (CORES, nx, ny, nz // CORES) for _ in range(2)]
    hbm = pl.BlockSpec(memory_space=pl.ANY)
    smem = pl.BlockSpec(memory_space=pltpu.SMEM)
    call = pl.pallas_call(
        make_kernel(sizes),
        out_shape=(
            jax.ShapeDtypeStruct((6 * rows, L), F32),
            jax.ShapeDtypeStruct((rows, L), F32),
            jax.ShapeDtypeStruct((2,), F32),
        ),
        in_specs=[hbm] * 9,
        out_specs=(hbm, hbm, smem),
        scratch_shapes=scratch,
        compiler_params=pltpu.CompilerParams(
            collective_id=0, has_side_effects=True, vmem_limit_bytes=60 * 2**20),
    )

    parts = 4

    def hand_over(adj_i, grad_i, imp_i, adj_o, grad_o, imp_o, adj, grad, imp, sem_in, sem_out):
        size = 6 * rows // parts
        pieces = [tuple(ref.at[pl.ds(k * size, size), :] for ref in (adj_i, adj, adj_o)) for k in range(parts)]
        pieces += [(grad_i, grad, grad_o), (imp_i, imp, imp_o)]
        loads = [pltpu.make_async_copy(src, mid, sem_in.at[k]) for k, (src, mid, _) in enumerate(pieces)]
        stores = [pltpu.make_async_copy(mid, dst, sem_out.at[k]) for k, (_, mid, dst) in enumerate(pieces)]
        for load in loads:
            load.start()
        for load, store in zip(loads, stores):
            load.wait()
            store.start()
        for store in stores:
            store.wait()

    results = pl.pallas_call(
        hand_over,
        out_shape=(
            jax.ShapeDtypeStruct((6 * rows, L), F32),
            jax.ShapeDtypeStruct((rows, L), F32),
            jax.ShapeDtypeStruct((2,), F32),
        ),
        in_specs=[hbm] * 3,
        out_specs=(hbm,) * 3,
        scratch_shapes=[
            vm(6 * rows, L), vm(rows, L), pltpu.SMEM((2,), F32),
            pltpu.SemaphoreType.DMA((parts + 2,)), pltpu.SemaphoreType.DMA((parts + 2,))],
        compiler_params=pltpu.CompilerParams(vmem_limit_bytes=60 * 2**20))

    def body(forward, adjoint_prev, density, labels, ports, z_target, radius_z, radius_y, radius_x):
        adjoint, gradient, impedance = results(*call(
            forward.reshape(6 * rows, L), adjoint_prev.reshape(6 * rows, L), density.reshape(rows, L),
            labels.reshape(rows, L), ports.reshape(rows, L), z_target, radius_z, radius_y,
            radius_x.reshape(nx, L)))
        return adjoint.reshape(6, D, H, L), gradient.reshape(D, H, L), impedance

    in_specs = (P(None, *AXES),) * 2 + (P(*AXES),) * 3 + (P(),) * 4
    out_specs = (P(None, *AXES), P(*AXES), P())
    return jax.shard_map(body, mesh=mesh, in_specs=in_specs, out_specs=out_specs, check_vma=False)
```

```python
import jax
import jax.numpy as jnp
from jax import lax
from jax.experimental import pallas as pl
from jax.experimental.pallas import tpu as pltpu
from jax.sharding import PartitionSpec as P

MU_GAIN = 19.0
KAPPA_GAIN = 2.0
RELAX = 0.8
SENS_GAIN = 0.1
REACH = 16
CORES = 2
WIDTH = dict(add_x=16, add_y=16, add_z=8, build=4, build_x=4, faces=16, inner1=16, inner2=16, material=16, pack0=16, packf=16, sens=16, step=8, sweep1=16, sweep2=16, reluctivity=16, join=16, answer=16)
MESH = pl.DeviceIdType.MESH
AXES = ("gz", "gy", "gx")
F32 = jnp.float32
BF16 = jnp.bfloat16
D = 16
H = 16
L = 128


def plane(index):
    if isinstance(index, int):
        return pl.ds(index * H, H)
    return pl.ds(pl.multiple_of(index * H, H), H)


def each(count, step, carry, width):
    if width == count:
        for k in range(count):
            carry = step(k, carry)
        return carry

    def group(g, carry):
        for k in range(width):
            carry = step(g * width + k, carry)
        return carry

    return lax.fori_loop(0, count // width, group, carry)


def mod(a, b):
    return a % b if isinstance(a, int) else lax.rem(a, b)


def clamp(value):
    if isinstance(value, int):
        return min(max(value, 0), D - 1)
    return jnp.clip(value, 0, D - 1)


def tri(value):
    value = jnp.maximum(value, 0)
    return value * (value + 1) // 2


def norm_of(radius, position, length):
    whole = (radius + 1) * (radius + 1)
    return whole - tri(radius - position) - tri(radius - (length - 1 - position))


def make_kernel(sizes):
    nz, ny, nx = sizes["gz"], sizes["gy"], sizes["gx"]
    total = {"gz": nz * D, "gy": ny * H, "gx": nx * L}
    scale = 4.0 / (total["gz"] * total["gy"] * total["gx"])

    def kernel(fwd_h, adj_h, den_h, lab_h, prt_h, zt_h, rz_h, ry_h, rx_h,
               adj_o, grad_o, imp_o,
               zt, rz, ry, rx, f, a0, den, lab, prt, a1, a2, t,
               nu, kap, wzm, wzp, wym, wyp, wxm, wxp, al, be, hx, kk, qq, s,
               zs0, ys0, xs0, zr0, yr0, xr0,
               zsf, ysf, xsf, zrf, yrf, xrf,
               zs1, ys1, xs1, zr1, yr1, xr1,
               zs2, ys2, xs2, zr2, yr2, xr2,
               ky, kz, bx, ysF, yrF, zsF, zrF, ysG, yrG, zsG, zrG, oyF, ozF, oyG, ozG,
               stA, srA, stB, srB, vbA, vbB, xin,
               sum_core, sum_x, sum_y, sum_z, in_sem, out_sem, ss, rs,
               ss_core, rs_core, ss_x, rs_x, ss_y, rs_y, ss_z, rs_z):
        sums = {"core": sum_core, "gx": sum_x, "gy": sum_y, "gz": sum_z}
        sum_ss = {"core": ss_core, "gx": ss_x, "gy": ss_y, "gz": ss_z}
        sum_rs = {"core": rs_core, "gx": rs_x, "gy": rs_y, "gz": rs_z}
        gz, gy, gx = (lax.axis_index(a) for a in AXES)
        pos = {"gz": gz, "gy": gy, "gx": gx}
        core = lax.rem(gz, CORES)

        def inside(axis, d):
            size = {"gz": nz, "gy": ny, "gx": nx}[axis]
            return pos[axis] < size - 1 if d > 0 else pos[axis] > 0

        stages = {
            "core": (CORES, lambda d: {"gz": gz - core + lax.rem(core + d, CORES)}, core),
            "gx": (nx, lambda d: {"gx": lax.rem(gx + d, nx)}, gx),
            "gy": (ny, lambda d: {"gy": lax.rem(gy + d, ny)}, gy),
            "gz": (nz // CORES, lambda d: {"gz": lax.rem(gz + CORES * d, nz)}, gz // CORES),
        }
        barrier = pltpu.get_barrier_semaphore()
        others = []
        for axis, dx in (("gz", 1), ("gy", -1)):
            for d in (-1, 1):
                others.append(({axis: pos[axis] + d, "gx": gx + dx},
                               jnp.logical_and(inside(axis, d), inside("gx", dx)),
                               jnp.logical_and(inside(axis, -d), inside("gx", -dx))))
        for d in (-1, 1):
            near = jnp.logical_and(inside("gz", d), (core == 0) if d < 0 else (core == CORES - 1))
            others.append(({"gz": gz + d}, near, near))
        expected = 0
        for members, peer, _ in stages.values():
            for d in range(1, members):
                pl.semaphore_signal(barrier, inc=1, device_id=peer(d), device_id_type=MESH)
                expected += 1
        for where, comes, goes in others:
            @pl.when(comes)
            def _():
                pl.semaphore_signal(barrier, inc=1, device_id=where, device_id_type=MESH)
            expected = expected + goes.astype(jnp.int32)

        loads = [
            pltpu.make_async_copy(src, dst, in_sem.at[k])
            for k, (src, dst) in enumerate((
                (den_h, den), (lab_h, lab), (adj_h, a0), (fwd_h, f), (prt_h, prt),
                (rx_h, rx), (ry_h, ry), (rz_h, rz), (zt_h, zt)))
        ]
        for load in loads[5:] + loads[:5]:
            load.start()

        def remote(src, dst, slot, where):
            return pltpu.make_async_remote_copy(
                src_ref=src, dst_ref=dst, send_sem=ss.at[slot], recv_sem=rs.at[slot],
                device_id=where, device_id_type=MESH)

        sent = []

        def beside(axis, d, src, dst, slot):
            copy = remote(src, dst, slot, {axis: pos[axis] + d})
            pl.when(inside(axis, d))(copy.start)
            sent.append((inside(axis, d), copy))
            return (inside(axis, -d), copy)

        def arrive(copies):
            for cond, copy in copies:
                pl.when(cond)(copy.wait_recv)

        def exchange(base, zs, zr, ys, yr, xs, xr):
            copies = []
            for axis, src, dst, k in (("gy", ys, yr, 2), ("gz", zs, zr, 0), ("gx", xs, xr, 4)):
                for d in (-1, 1):
                    side = 0 if d < 0 else 1
                    piece = src if axis == "gx" else src.at[side]
                    copies.append(beside(axis, d, piece, dst.at[1 - side], base + k + side))
            return copies

        edges = {axis: (pos[axis] == 0, pos[axis] == {"gz": nz, "gy": ny, "gx": nx}[axis] - 1) for axis in AXES}
        for axis, bufs in (("gz", (zr0, zrf, zr1, zr2, zrF, zrG)), ("gy", (yr0, yrf, yr1, yr2, yrF, yrG)),
                           ("gx", (xr0, xrf, xr1, xr2))):
            for side in (0, 1):
                @pl.when(edges[axis][side])
                def _():
                    for buf in bufs:
                        buf[side] = jnp.zeros(buf.shape[1:], F32)
                    if axis == "gx":
                        column = lax.rem(lax.broadcasted_iota(jnp.int32, (H, L), 1), 8)
                        xr0[side, 1] = jnp.where(column // 2 == 2, 1.0, 0.0).astype(F32)
                    else:
                        buf = zr0 if axis == "gz" else yr0
                        buf[side, pl.ds(6 * H, H), :] = jnp.ones((H, L), F32)
        for strip, axis, side in ((srA, "gz", 1), (srB, "gy", 0)):
            for cond, slots in ((edges["gx"][side], (0, 1, 2)), (edges[axis][0], (1,)), (edges[axis][1], (2,))):
                @pl.when(cond)
                def _():
                    for slot in slots:
                        strip[slot] = jnp.zeros(strip.shape[1:], F32)

        lane = lax.broadcasted_iota(jnp.int32, (H, L), 1)
        row = lax.broadcasted_iota(jnp.int32, (H, L), 0)

        loads[0].wait()
        loads[1].wait()

        def reluctivity(z, _):
            density = den[plane(z), :]
            design = jnp.where(lab[plane(z), :] == 2, 1.0, 0.0).astype(F32)
            cube = density * density * density
            nu_design = 1.0 / (1.0 + MU_GAIN * cube)
            nu[plane(z), :] = 1.0 - design + design * nu_design
            kap[plane(z), :] = design * KAPPA_GAIN * cube
            return 0

        each(D, reluctivity, 0, WIDTH['reluctivity'])

        def pack(z, tiles, values):
            out = list(tiles)
            for c, v in enumerate(values):
                moved = pltpu.roll(v, (z * 8 + 2 * (c % 4) + 1) % L, 1)
                out[c // 4] = jnp.where(lane // 2 == z * 4 + c % 4, moved, out[c // 4])
            return tuple(out)

        def pair(xr, n):
            below = pltpu.roll(xr[0, n], 1, 1)
            above = pltpu.roll(xr[1, n], L - 1, 1)
            return jnp.where(lax.rem(lane, 2) == 0, above, below)

        def unpack(tile, z, count, first=0):
            return [pltpu.roll(tile, (-z * 8 - 2 * c - 1) % L, 1) for c in range(first, first + count)]

        zero = jnp.zeros((H, L), F32)

        def cell_rows(ref, count, first):
            return ref[pl.ds(first, count * D, stride=H), :]

        loads[2].wait()
        for side, z in ((0, 0), (1, D - 1)):
            for c in range(6):
                zs0[side, pl.ds(c * H, H), :] = a0[pl.ds((c * D + z) * H, H), :]
            zs0[side, pl.ds(6 * H, H), :] = nu[pl.ds(z * H, H), :]
            ys0[side, pl.ds(0, 6 * D), :] = cell_rows(a0, 6, side * (H - 1))
            ys0[side, pl.ds(6 * D, D), :] = cell_rows(nu, 1, side * (H - 1))

        def pack0(z, tiles):
            return pack(z, tiles, [a0[plane(c * D + z), :] for c in range(6)] + [nu[plane(z), :]])

        tiles = each(D, pack0, (zero, zero), WIDTH['pack0'])
        xs0[0] = tiles[0]
        xs0[1] = tiles[1]

        pl.semaphore_wait(barrier, expected)
        got0 = exchange(0, zs0, zr0, ys0, yr0, xs0, xr0)

        def sum_copy(stage, d, arriving):
            members, peer, slot = stages[stage]
            at = lax.rem(slot + d, members) if arriving else slot
            ref = sums[stage].at[at]
            return pltpu.make_async_remote_copy(
                src_ref=ref, dst_ref=ref, send_sem=sum_ss[stage].at[d], recv_sem=sum_rs[stage].at[at],
                device_id=peer(d), device_id_type=MESH)

        def sum_start(stage, value):
            members, _, slot = stages[stage]
            sums[stage][slot] = value
            for d in range(1, members):
                sum_copy(stage, d, False).start()

        def sum_finish(stage):
            members = stages[stage][0]
            for d in range(1, members):
                sum_copy(stage, d, True).wait_recv()
            value = sums[stage][0]
            for q in range(1, members):
                value = value + sums[stage][q]
            return value

        loads[3].wait()
        loads[4].wait()
        for side, z in ((0, 0), (1, D - 1)):
            for c in range(6):
                zsf[side, pl.ds(c * H, H), :] = f[pl.ds((c * D + z) * H, H), :]
            ysf[side] = cell_rows(f, 6, side * (H - 1))

        def packf(z, carry):
            tiles, re, im = carry
            values = [f[plane(c * D + z), :] for c in range(6)]
            mask = prt[plane(z), :].astype(F32)
            return (pack(z, tiles, values), re + mask * values[2], im + mask * values[5])

        tiles, port_re, port_im = each(D, packf, ((zero, zero), zero, zero), WIDTH['packf'])
        xsf[0] = tiles[0]
        xsf[1] = tiles[1]
        port_sum = jnp.concatenate(
            [jnp.sum(port_re, axis=0, keepdims=True), jnp.sum(port_im, axis=0, keepdims=True)], axis=0)

        sum_start("core", port_sum)

        def faces(z, _):
            v = nu[plane(z), :]
            below = nu[plane(clamp(z - 1)), :]
            above = nu[plane(clamp(z + 1)), :]
            wzm[plane(z), :] = jnp.where(z > 0, 0.5 * (v + below), 0.0)
            wzp[plane(z), :] = jnp.where(z < D - 1, 0.5 * (v + above), 0.0)
            wym[plane(z), :] = jnp.where(row > 0, 0.5 * (v + pltpu.roll(v, 1, 0)), 0.0)
            wyp[plane(z), :] = jnp.where(row < H - 1, 0.5 * (v + pltpu.roll(v, H - 1, 0)), 0.0)
            wxm[plane(z), :] = jnp.where(lane > 0, 0.5 * (v + pltpu.roll(v, 1, 1)), 0.0)
            wxp[plane(z), :] = jnp.where(lane < L - 1, 0.5 * (v + pltpu.roll(v, L - 1, 1)), 0.0)
            inner_sum = wzm[plane(z), :] + wzp[plane(z), :] + wym[plane(z), :] + wyp[plane(z), :]
            al[plane(z), :] = inner_sum + wxm[plane(z), :] + wxp[plane(z), :]
            return 0

        each(D, faces, 0, WIDTH['faces'])

        def inner(a, count, z, begin):
            zm = clamp(z - 1)
            zp = clamp(z + 1)
            w = [ref[plane(z), :] for ref in (wzm, wzp, wym, wyp, wxm, wxp)]
            for c in range(count):
                v = a[plane(c * D + z), :]
                total_ = w[0] * a[plane(c * D + zm), :] + w[1] * a[plane(c * D + zp), :]
                total_ += w[2] * pltpu.roll(v, 1, 0) + w[3] * pltpu.roll(v, H - 1, 0)
                total_ += w[4] * pltpu.roll(v, 1, 1) + w[5] * pltpu.roll(v, L - 1, 1)
                first = begin(c)
                t[plane(c * D + z), :] = total_ if first is None else total_ + first

        def inner1(z, _):
            kappa = kap[plane(z), :]
            inner(a0, 6, z, lambda c: kappa * f[plane(c * D + z), :])
            return 0

        each(D, inner1, 0, WIDTH['inner1'])
        sum_start("gx", sum_finish("core"))
        gotf = exchange(6, zsf, zrf, ysf, yrf, xsf, xrf)

        arrive(got0)
        x0 = [pair(xr0, 0), pair(xr0, 1)]
        outer_x = jnp.logical_or(lane == 0, lane == L - 1)

        hz = []
        hy = []
        for side, z in ((0, 0), (1, D - 1)):
            hz.append(0.5 * (nu[pl.ds(z * H, H), :] + zr0[side, pl.ds(6 * H, H), :]))
            hy.append(0.5 * (cell_rows(nu, 1, side * (H - 1)) + yr0[side, pl.ds(6 * D, D), :]))

        def add_outer(zr, yr, count):
            for side, z in ((0, 0), (1, D - 1)):
                for c in range(count):
                    t[pl.ds((c * D + z) * H, H), :] += hz[side] * zr[side, pl.ds(c * H, H), :]
                for c in range(count):
                    at = pl.ds(c * D * H + side * (H - 1), D, stride=H)
                    t[at, :] = t[at, :] + hy[side] * yr[side, pl.ds(c * D, D), :]

        add_outer(zr0, yr0, 6)
        for side, z in ((0, 0), (1, D - 1)):
            al[pl.ds(z * H, H), :] += hz[side]
            at = pl.ds(side * (H - 1), D, stride=H)
            al[at, :] = al[at, :] + hy[side]

        def finish(z, a, tiles_in, count):
            alpha = al[plane(z), :]
            beta = be[plane(z), :]
            face = hx[plane(z), :]
            outside = unpack(tiles_in[0], z, 4) + unpack(tiles_in[1], z, count - 4)
            tt = [t[plane(c * D + z), :] + face * outside[c] for c in range(count)]
            out = [None] * count
            pairs = [(0, 3), (1, 4), (2, 5)] + ([(6, 7)] if count == 8 else [])
            for re, im in pairs:
                out[re] = (1.0 - RELAX) * a[plane(re * D + z), :] + (tt[re] * alpha + tt[im] * beta)
                out[im] = (1.0 - RELAX) * a[plane(im * D + z), :] + (tt[im] * alpha - tt[re] * beta)
            return out

        def sweep1(z, tiles):
            face = jnp.where(outer_x, 0.5 * (nu[plane(z), :] + unpack(x0[1], z, 1, 2)[0]), 0.0)
            hx[plane(z), :] = face
            d = al[plane(z), :] + face
            kappa = kap[plane(z), :]
            weight = RELAX / (d * d + kappa * kappa)
            al[plane(z), :] = d * weight
            be[plane(z), :] = kappa * weight
            out = finish(z, a0, x0, 6)
            mask = prt[plane(z), :].astype(F32)
            out.append(mask * (d * weight))
            out.append(-mask * (kappa * weight))
            for c in range(8):
                a1[plane(c * D + z), :] = out[c]
            return pack(z, tiles, out)

        tiles = each(D, sweep1, (zero, zero), WIDTH['sweep1'])
        xs1[0] = tiles[0]
        xs1[1] = tiles[1]
        for side, z in ((0, 0), (1, D - 1)):
            for c in range(8):
                zs1[side, pl.ds(c * H, H), :] = a1[pl.ds((c * D + z) * H, H), :]
            ys1[side] = cell_rows(a1, 8, side * (H - 1))
        got1 = exchange(12, zs1, zr1, ys1, yr1, xs1, xr1)

        sum_start("gy", sum_finish("gx"))

        def inner2(z, _):
            kappa = kap[plane(z), :]

            def begin(c):
                if c < 6:
                    return kappa * f[plane(c * D + z), :]
                return prt[plane(z), :].astype(F32) if c == 6 else None

            inner(a1, 8, z, begin)
            return 0

        each(D, inner2, 0, WIDTH['inner2'])
        for load in loads[5:]:
            load.wait()
        ry_l = jnp.zeros((H, L), jnp.int32)
        rz_l = jnp.zeros((H, L), jnp.int32)
        ry_r = jnp.zeros((H, L), jnp.int32)
        for b in range(H):
            ry_b = ry[gy * H + b]
            rz_b = rz[gz * D + b]
            ry_l = jnp.where(lax.rem(lane, H) == b, ry_b, ry_l)
            rz_l = jnp.where(lane // 8 == b, rz_b, rz_l)
            ry_r = jnp.where(row == b, ry_b, ry_r)

        def build(k, _):
            n = k // 8
            q = mod(k, 8)
            band_y = jnp.maximum(ry_l + 1 - jnp.abs(lax.rem(lane, H) - (row + (n - 1) * H)), 0)
            ky[plane(k), :] = jnp.where(lane // H == q, band_y, 0).astype(F32).astype(BF16)
            band_z = jnp.maximum(rz_l + 1 - jnp.abs(lane // 8 - (2 * q + row // 8 + (n - 1) * D)), 0)
            kz[plane(k), :] = jnp.where(lax.rem(lane, 8) == lax.rem(row, 8), band_z, 0).astype(F32).astype(BF16)
            return 0

        each(24, build, 0, WIDTH['build'])
        rx_own = jnp.broadcast_to(rx[pl.ds(gx, 1), :], (H, L))
        rx_low = jnp.broadcast_to(rx[pl.ds(jnp.maximum(gx - 1, 0), 1), :], (H, L))
        rx_high = jnp.broadcast_to(rx[pl.ds(jnp.minimum(gx + 1, nx - 1), 1), :], (H, L))

        def build_x(k, _):
            target = row + k * H
            own = jnp.maximum(rx_own + 1 - jnp.abs(lane - target), 0)
            low = jnp.maximum(rx_low + 1 - jnp.abs(lane - L - target), 0)
            high = jnp.maximum(rx_high + 1 - jnp.abs(lane + L - target), 0)
            bx[plane(k), pl.ds(0, L)] = own.astype(F32).astype(BF16)
            bx[plane(k), pl.ds(L, L)] = jnp.where(lane < L // 2, high, low).astype(F32).astype(BF16)
            return 0

        each(L // H, build_x, 0, WIDTH['build_x'])
        norm_yx = (norm_of(ry_r, gy * H + row, total["gy"]) * norm_of(rx_own, gx * L + lane, total["gx"])).astype(F32)

        def material(z, _):
            density = den[plane(z), :]
            design = jnp.where(lab[plane(z), :] == 2, 1.0, 0.0).astype(F32)
            square = density * density
            cube = square * density
            nu_design = 1.0 / (1.0 + MU_GAIN * cube)
            gz_i = gz * D + z
            norm_z = norm_of(rz[gz_i], gz_i, total["gz"]).astype(F32)
            inverse = SENS_GAIN / (norm_yx * norm_z)
            nu_slope = -3.0 * MU_GAIN * design * square * nu_design * nu_design
            kk[plane(z), :] = -0.5 * nu_slope * inverse
            qq[plane(z), :] = 3.0 * KAPPA_GAIN * design * square * inverse
            return 0

        each(D, material, 0, WIDTH['material'])

        sum_start("gz", sum_finish("gy"))
        arrive(gotf)
        xf = [pair(xrf, 0), pair(xrf, 1)]
        arrive(got1)
        add_outer(zr1, yr1, 8)
        x1 = [pair(xr1, 0), pair(xr1, 1)]

        def shares(answers, near):
            main = None
            for c in range(6):
                term = answers[c] * near[c]
                main = term if c == 0 else main + term if c < 3 else main - term
            return [main, answers[6] * near[2] - answers[7] * near[5], -(answers[7] * near[2]) - answers[6] * near[5]]

        def sweep2(z, tile):
            out = finish(z, a1, x1, 8)
            for c in range(8):
                a2[plane(c * D + z), :] = out[c]
            outside = unpack(xf[0], z, 4) + unpack(xf[1], z, 2)
            near = [f[plane(c * D + z), :] - outside[c] for c in range(6)]
            share = [jnp.where(outer_x, v, 0.0) for v in shares(out, near)]
            for k in range(3):
                t[plane(k * D + z), :] = share[k]
            return pack(z, (tile,), share)[0]

        xs2[0] = each(D, sweep2, zero, WIDTH['sweep2'])
        hz2 = []
        hy2 = []
        for side, z in ((0, 0), (1, D - 1)):
            at = [pl.ds((c * D + z) * H, H) for c in range(8)]
            near = [f[at[c], :] - zrf[side, pl.ds(c * H, H), :] for c in range(6)]
            share = shares([a2[where, :] for where in at], near)
            for k in range(3):
                zs2[side, pl.ds(k * H, H), :] = share[k]
            hz2.append(share)
            at = [pl.ds(c * D * H + side * (H - 1), D, stride=H) for c in range(8)]
            near = [f[at[c], :] - yrf[side, pl.ds(c * D, D), :] for c in range(6)]
            share = shares([a2[where, :] for where in at], near)
            for k in range(3):
                ys2[side, pl.ds(k * D, D), :] = share[k]
            hy2.append(share)
        got2 = exchange(18, zs2, zr2, ys2, yr2, xs2, xr2)

        def sens(z, last):
            zp = clamp(z + 1)
            av = [a2[plane(c * D + z), :] for c in range(8)]
            fv = [f[plane(c * D + z), :] for c in range(6)]
            above = [a2[plane(c * D + zp), :] for c in range(8)], [f[plane(c * D + zp), :] for c in range(6)]
            ez = shares([v - w for v, w in zip(av, above[0])], [v - w for v, w in zip(fv, above[1])])
            ey = shares([v - pltpu.roll(v, H - 1, 0) for v in av], [v - pltpu.roll(v, H - 1, 0) for v in fv])
            ex = shares([v - pltpu.roll(v, L - 1, 1) for v in av], [v - pltpu.roll(v, L - 1, 1) for v in fv])
            more = [zero, av[6] * fv[5] + av[7] * fv[2], av[6] * fv[2] - av[7] * fv[5]]
            for c in range(6):
                more[0] = more[0] + fv[c] * (fv[c] + av[(c + 3) % 6])
            for k in range(3):
                along_y = jnp.where(row < H - 1, ey[k], 0.0)
                along_x = jnp.where(lane < L - 1, ex[k], 0.0)
                energy = ez[k] + last[k] + along_y + pltpu.roll(along_y, 1, 0)
                energy = energy + along_x + pltpu.roll(along_x, 1, 1) + t[plane(k * D + z), :]
                s[plane(k * D + z), :] = kk[plane(z), :] * energy + qq[plane(z), :] * more[k]
            return ez

        each(D, sens, [zero] * 3, WIDTH['sens'])
        total_ports = sum_finish("gz")
        link_re = scale * jnp.sum(total_ports[0:1])
        link_im = scale * jnp.sum(total_ports[1:2])
        imp_o[0] = link_re
        imp_o[1] = link_im
        coef_re = 2.0 * (link_re - zt[0])
        coef_im = -2.0 * (link_im - zt[1])

        def joined(parts):
            return parts[0] + (coef_re * parts[1] + coef_im * parts[2])

        def join(z, _):
            s[plane(z), :] = joined([s[plane(k * D + z), :] for k in range(3)])
            return 0

        each(D, join, 0, WIDTH['join'])
        for side, z in ((0, 0), (1, D - 1)):
            at = pl.ds(z * H, H)
            s[at, :] += kk[at, :] * joined(hz2[side])
            at = pl.ds(side * (H - 1), D, stride=H)
            s[at, :] = s[at, :] + kk[at, :] * joined(hy2[side])
        arrive(got2)
        for side, z in ((0, 0), (1, D - 1)):
            at = pl.ds(z * H, H)
            s[at, :] += kk[at, :] * joined([zr2[side, pl.ds(k * H, H), :] for k in range(3)])
            at = pl.ds(side * (H - 1), D, stride=H)
            s[at, :] = s[at, :] + kk[at, :] * joined([yr2[side, pl.ds(k * D, D), :] for k in range(3)])
        tile2 = pair(xr2, 0)
        tile2 = joined([tile2, pltpu.roll(tile2, L - 2, 1), pltpu.roll(tile2, L - 4, 1)])

        def add_x(z, _):
            outside = unpack(tile2, z, 1)[0]
            s[plane(z), :] += kk[plane(z), :] * jnp.where(outer_x, outside, 0.0)
            return 0

        each(D, add_x, 0, WIDTH['add_x'])

        lane8 = lax.broadcasted_iota(jnp.int32, (8, L), 1)
        left = lane < L // 2
        left8 = lane8 < L // 2

        def turn(v):
            return pltpu.roll(v, L // 2, 1)

        def split(v):
            high = v.astype(BF16)
            return high, (v - high.astype(F32)).astype(BF16)

        def keep(ref, k, v):
            high, low = split(v)
            ref[pl.ds(k * H, H), pl.ds(0, L)] = high
            ref[pl.ds(k * H, H), pl.ds(L, L)] = low

        def stack(a, b):
            return jnp.concatenate([a, b], axis=0)

        def band(matrix, value, dst_low, dst_own, dst_high):
            for n, dst in ((0, dst_low), (2, dst_high), (1, dst_own)):
                both = jnp.dot(matrix[pl.ds(n * L, L), :], value[...], preferred_element_type=F32)
                dst[...] = both[:, :L] + both[:, L:]

        def both_ways(axis, src, dst, slot):
            return [beside(axis, d, src.at[side], dst.at[1 - side], slot + side) for side, d in ((0, -1), (1, 1))]

        for p in range(8):
            keep(vbA, p, jnp.where(left, s[plane(p), :], turn(s[plane(p + 8), :])))
        band(ky, vbA, ysF.at[0], oyF, ysF.at[1])
        gotY = both_ways("gy", ysF, yrF, 24)
        for k in range(8):
            tiles = []
            for z in (2 * k, 2 * k + 1):
                v = s[plane(z), :]
                tiles.append(jnp.where(left8, turn(v[:8]), v[8:]))
            keep(vbB, k, stack(*tiles))
        band(kz, vbB, zsF.at[0], ozF, zsF.at[1])
        gotZ = both_ways("gz", zsF, zrF, 26)

        def answer(z, _):
            re, im = a2[plane(6 * D + z), :], a2[plane(7 * D + z), :]
            added = {2: coef_re * re - coef_im * im, 5: coef_re * im + coef_im * re}
            for c in added:
                a2[plane(c * D + z), :] += added[c]
            return 0

        each(D, answer, 0, WIDTH['answer'])
        adj_copy = pltpu.make_async_copy(a2.at[pl.ds(0, 6 * D * H), :], adj_o, out_sem)
        adj_copy.start()

        def eight(ref, k):
            return ref[pl.ds(8 * k, 8), :]

        arrive(gotZ)
        vz = [eight(ozF, z) + eight(zrF.at[0], z) + eight(zrF.at[1], z) for z in range(D)]
        for p in range(8):
            low, high = vz[p], vz[p + 8]
            keep(vbB, p, stack(jnp.where(left8, low, turn(high)), jnp.where(left8, turn(low), high)))
        band(ky, vbB, ysG.at[0], oyG, ysG.at[1])
        gotY2 = both_ways("gy", ysG, yrG, 30)
        def columns(dst, src, count, rows_, offset, lanes):
            for g in range(count // 4):
                tile = None
                for q in range(4):
                    moved = pltpu.roll(src[pl.ds((4 * g + q) * rows_, rows_), :], (16 * q - offset) % L, 1)
                    tile = moved if q == 0 else jnp.where(lax.rem(lanes // REACH, 4) == q, moved, tile)
                dst[pl.ds(g * rows_, rows_), :] = tile

        def send_columns(axis, dx, st, sr, src, slot):
            got = []
            for n, d in ((0, 0), (1, -1), (2, 1)):
                if axis == "gz":
                    columns(st.at[n], src[n], D, 8, 0, lane8)
                else:
                    columns(st.at[n], src[n], 8, H, 48, lane)
                if d == 0:
                    got.append(beside("gx", dx, st.at[0], sr.at[0], slot))
                    continue
                go = jnp.logical_and(inside("gx", dx), inside(axis, d))
                come = jnp.logical_and(inside("gx", -dx), inside(axis, -d))
                copy = remote(st.at[n], sr.at[3 - n], slot + n, {axis: pos[axis] + d, "gx": gx + dx})
                pl.when(go)(copy.start)
                sent.append((go, copy))
                got.append((come, copy))
            return got

        gotX = send_columns("gy", 1, stB, srB, (oyG, ysG.at[0], ysG.at[1]), 35)
        arrive(gotY)
        vy = [oyF[plane(p), :] + yrF[0, plane(p), :] + yrF[1, plane(p), :] for p in range(8)]
        for k in range(4):
            near, far = [], []
            for p in (2 * k, 2 * k + 1):
                top, bottom = vy[p][:8], vy[p][8:]
                near.append(jnp.where(left8, top, turn(bottom)))
                far.append(jnp.where(left8, turn(top), bottom))
            keep(vbA, k, stack(*near))
            keep(vbA, k + 4, stack(*far))
        band(kz, vbA, zsG.at[0], ozG, zsG.at[1])
        gotZ2 = both_ways("gz", zsG, zrG, 28)

        gotX += send_columns("gz", -1, stA, srA, (ozG, zsG.at[0], zsG.at[1]), 32)
        arrive(gotY2)
        arrive(gotZ2)
        arrive(gotX)
        ga = [sum(srA[n, pl.ds(8 * g, 8), :] for n in range(3)) for g in range(4)]
        gb = [sum(srB[n, plane(g), :] for n in range(3)) for g in range(2)]
        vy = [oyG[plane(p), :] + yrG[0, plane(p), :] + yrG[1, plane(p), :] for p in range(8)]
        for z in range(D):
            v = eight(ozG, z) + eight(zrG.at[0], z) + eight(zrG.at[1], z)
            own = jnp.where(left, stack(v, turn(v)), turn(vy[z]) if z < 8 else vy[z - 8])
            group = ga[z // 4]
            above = stack(*(pltpu.roll(group, (-16 * (z % 4) - 64 * h) % L, 1) for h in range(2)))
            below = pltpu.roll(gb[z % 8 // 4], (112 - 64 * (z // 8) - 16 * (z % 4)) % L, 1)
            for k, part in enumerate((own, jnp.where(left, above, below))):
                big, small = split(part)
                xin[plane(z), pl.ds(k * L, L)] = big
                xin[plane(z + D), pl.ds(k * L, L)] = small
        both = lax.dot_general(xin[...], bx[...], (((1,), (1,)), ((), ())), preferred_element_type=F32)
        grad_o[...] = both[:D * H] + both[D * H:]

        for cond, copy in sent:
            pl.when(cond)(copy.wait_send)
        for stage in stages:
            for d in range(1, stages[stage][0]):
                sum_copy(stage, d, False).wait_send()
        adj_copy.wait()

    return kernel


def solution(mesh):
    sizes = dict(mesh.shape)
    nz, ny, nx = (sizes[a] for a in AXES)
    rows = D * H
    vm = lambda *shape: pltpu.VMEM(shape, F32)
    field = vm(rows, L)

    def halo(planes, tiles):
        y = vm(2, planes * D, L)
        z = vm(2, planes * H, L)
        return [z, y, vm(tiles, H, L), z, y, vm(2, tiles, H, L)]

    scratch = [
        pltpu.SMEM((2,), F32), pltpu.SMEM((nz * D,), jnp.int32), pltpu.SMEM((ny * H,), jnp.int32),
        pltpu.VMEM((nx, L), jnp.int32),
        vm(6 * rows, L), vm(6 * rows, L), field, pltpu.VMEM((rows, L), jnp.int32), pltpu.VMEM((rows, L), jnp.int32),
        vm(8 * rows, L), vm(8 * rows, L), vm(8 * rows, L),
    ] + [field] * 13 + [vm(3 * rows, L)] + halo(7, 2) + halo(6, 2) + halo(8, 2) + [
        vm(2, 3 * H, L), vm(2, 3 * D, L), vm(1, H, L), vm(2, 3 * H, L), vm(2, 3 * D, L), vm(2, 1, H, L),
        pltpu.VMEM((3 * L, L), BF16), pltpu.VMEM((3 * L, L), BF16), pltpu.VMEM((L, 2 * L), BF16),
    ] + [vm(2, L, L)] * 8 + [vm(L, L)] * 4 + [vm(3, 32, L)] * 4 + [
        pltpu.VMEM((L, 2 * L), BF16), pltpu.VMEM((L, 2 * L), BF16), pltpu.VMEM((2 * rows, 2 * L), BF16),
    ] + [vm(n, 2, L) for n in (CORES, nx, ny, nz // CORES)] + [
        pltpu.SemaphoreType.DMA((9,)), pltpu.SemaphoreType.DMA,
        pltpu.SemaphoreType.DMA((38,)), pltpu.SemaphoreType.DMA((38,)),
    ] + [pltpu.SemaphoreType.DMA((n,)) for n in (CORES, nx, ny, nz // CORES) for _ in range(2)]
    hbm = pl.BlockSpec(memory_space=pl.ANY)
    smem = pl.BlockSpec(memory_space=pltpu.SMEM)
    vmem = pl.BlockSpec(memory_space=pltpu.VMEM)
    call = pl.pallas_call(
        make_kernel(sizes),
        out_shape=(
            pltpu.VMEM((6 * rows, L), F32),
            pltpu.VMEM((rows, L), F32),
            jax.ShapeDtypeStruct((2,), F32),
        ),
        in_specs=[hbm] * 9,
        out_specs=(hbm, vmem, smem),
        scratch_shapes=scratch,
        compiler_params=pltpu.CompilerParams(
            collective_id=0, has_side_effects=True, vmem_limit_bytes=32 * 2**20),
    )

    def hand_over(adj_i, grad_i, imp_i, adj_o, grad_o, imp_o, imp, sem, imp_sem):
        first = pltpu.make_async_copy(imp_i, imp, imp_sem)
        copies = [
            pltpu.make_async_copy(src, dst, sem.at[k])
            for k, (src, dst) in enumerate(((adj_i, adj_o), (grad_i, grad_o), (imp, imp_o)))
        ]
        first.start()
        copies[0].start()
        copies[1].start()
        first.wait()
        copies[2].start()
        for copy in copies:
            copy.wait()

    results = pl.pallas_call(
        hand_over,
        out_shape=(
            jax.ShapeDtypeStruct((6 * rows, L), F32),
            jax.ShapeDtypeStruct((rows, L), F32),
            jax.ShapeDtypeStruct((2,), F32),
        ),
        in_specs=[hbm] * 3,
        out_specs=(hbm,) * 3,
        scratch_shapes=[pltpu.SMEM((2,), F32), pltpu.SemaphoreType.DMA((3,)), pltpu.SemaphoreType.DMA],
        compiler_params=pltpu.CompilerParams(vmem_limit_bytes=16 * 2**20))

    def body(forward, adjoint_prev, density, labels, ports, z_target, radius_z, radius_y, radius_x):
        arrays = (
            forward.reshape(6 * rows, L), adjoint_prev.reshape(6 * rows, L), density.reshape(rows, L),
            labels.reshape(rows, L), ports.reshape(rows, L), z_target, radius_z, radius_y,
            radius_x.reshape(nx, L))
        place = pltpu.with_memory_space_constraint
        made = call(*(place(v, pltpu.HBM) for v in arrays))
        adjoint, gradient, impedance = results(place(made[0], pltpu.VMEM), place(made[1], pltpu.VMEM), made[2])
        return adjoint.reshape(6, D, H, L), gradient.reshape(D, H, L), impedance

    in_specs = (P(None, *AXES),) * 2 + (P(*AXES),) * 3 + (P(),) * 4
    out_specs = (P(None, *AXES), P(*AXES), P())
    return jax.shard_map(body, mesh=mesh, in_specs=in_specs, out_specs=out_specs, check_vma=False)
```

```python
import jax
import jax.numpy as jnp
from jax import lax
from jax.experimental import pallas as pl
from jax.experimental.pallas import tpu as pltpu
from jax.sharding import PartitionSpec as P

MU_GAIN = 19.0
KAPPA_GAIN = 2.0
RELAX = 0.8
SENS_GAIN = 0.1
REACH = 16
CORES = 2
WIDTH = dict(add_x=16, add_y=16, add_z=8, build=4, build_x=4, faces=16, inner1=16, inner2=16, material=16, pack0=16, packf=16, sens=16, step=8, sweep1=16, sweep2=16, across_x=16, reluctivity=16, join=16, answer=16)
MESH = pl.DeviceIdType.MESH
AXES = ("gz", "gy", "gx")
F32 = jnp.float32
BF16 = jnp.bfloat16
D = 16
H = 16
L = 128


def plane(index):
    if isinstance(index, int):
        return pl.ds(index * H, H)
    return pl.ds(pl.multiple_of(index * H, H), H)


def each(count, step, carry, width):
    if width == count:
        for k in range(count):
            carry = step(k, carry)
        return carry

    def group(g, carry):
        for k in range(width):
            carry = step(g * width + k, carry)
        return carry

    return lax.fori_loop(0, count // width, group, carry)


def mod(a, b):
    return a % b if isinstance(a, int) else lax.rem(a, b)


def clamp(value):
    if isinstance(value, int):
        return min(max(value, 0), D - 1)
    return jnp.clip(value, 0, D - 1)


def tri(value):
    value = jnp.maximum(value, 0)
    return value * (value + 1) // 2


def norm_of(radius, position, length):
    whole = (radius + 1) * (radius + 1)
    return whole - tri(radius - position) - tri(radius - (length - 1 - position))


def make_kernel(sizes):
    nz, ny, nx = sizes["gz"], sizes["gy"], sizes["gx"]
    total = {"gz": nz * D, "gy": ny * H, "gx": nx * L}
    scale = 4.0 / (total["gz"] * total["gy"] * total["gx"])

    def kernel(fwd_h, adj_h, den_h, lab_h, prt_h, zt_h, rz_h, ry_h, rx_h,
               adj_o, grad_o, imp_o,
               near_x, zt, rz, ry, rx, f, a0, den, lab, prt, a1, a2, t,
               nu, kap, wzm, wzp, wym, wyp, wxm, wxp, al, be, hx, kk, qq, s,
               zs0, ys0, xs0, zr0, yr0, xr0,
               zsf, ysf, xsf, zrf, yrf, xrf,
               zs1, ys1, xs1, zr1, yr1, xr1,
               zs2, ys2, xs2, zr2, yr2, xr2,
               ky, kz, bx, ysF, yrF, zsF, zrF, ysG, yrG, zsG, zrG, oyF, ozF, oyG, ozG,
               stA, srA, stB, srB, vbA, vbB, xin,
               sum_core, sum_x, sum_y, sum_z, in_sem, out_sem, ss, rs,
               ss_core, rs_core, ss_x, rs_x, ss_y, rs_y, ss_z, rs_z):
        sums = {"core": sum_core, "gx": sum_x, "gy": sum_y, "gz": sum_z}
        sum_ss = {"core": ss_core, "gx": ss_x, "gy": ss_y, "gz": ss_z}
        sum_rs = {"core": rs_core, "gx": rs_x, "gy": rs_y, "gz": rs_z}
        gz, gy, gx = (lax.axis_index(a) for a in AXES)
        pos = {"gz": gz, "gy": gy, "gx": gx}
        core = lax.rem(gz, CORES)

        def inside(axis, d):
            size = {"gz": nz, "gy": ny, "gx": nx}[axis]
            return pos[axis] < size - 1 if d > 0 else pos[axis] > 0

        stages = {
            "core": (CORES, lambda d: {"gz": gz - core + lax.rem(core + d, CORES)}, core),
            "gx": (nx, lambda d: {"gx": lax.rem(gx + d, nx)}, gx),
            "gy": (ny, lambda d: {"gy": lax.rem(gy + d, ny)}, gy),
            "gz": (nz // CORES, lambda d: {"gz": lax.rem(gz + CORES * d, nz)}, gz // CORES),
        }
        barrier = pltpu.get_barrier_semaphore()
        others = []
        for axis, dx in (("gz", 1), ("gy", -1)):
            for d in (-1, 1):
                others.append(({axis: pos[axis] + d, "gx": gx + dx},
                               jnp.logical_and(inside(axis, d), inside("gx", dx)),
                               jnp.logical_and(inside(axis, -d), inside("gx", -dx))))
        for d in (-1, 1):
            near = jnp.logical_and(inside("gz", d), (core == 0) if d < 0 else (core == CORES - 1))
            others.append(({"gz": gz + d}, near, near))
        expected = 0
        for members, peer, _ in reversed(stages.values()):
            for d in sorted(range(1, members), key=lambda d: abs(d - members / 2)):
                pl.semaphore_signal(barrier, inc=1, device_id=peer(d), device_id_type=MESH)
                expected += 1
        for where, comes, goes in others:
            @pl.when(comes)
            def _():
                pl.semaphore_signal(barrier, inc=1, device_id=where, device_id_type=MESH)
            expected = expected + goes.astype(jnp.int32)

        loads = [
            pltpu.make_async_copy(src, dst, in_sem.at[k])
            for k, (src, dst) in enumerate((
                (den_h, den), (lab_h, lab), (adj_h, a0), (fwd_h, f), (prt_h, prt),
                (rx_h, rx), (ry_h, ry), (rz_h, rz), (zt_h, zt)))
        ]
        for load in loads[5:] + loads[:5]:
            load.start()

        def remote(src, dst, slot, where):
            return pltpu.make_async_remote_copy(
                src_ref=src, dst_ref=dst, send_sem=ss.at[slot], recv_sem=rs.at[slot],
                device_id=where, device_id_type=MESH)

        sent = []

        def beside(axis, d, src, dst, slot):
            copy = remote(src, dst, slot, {axis: pos[axis] + d})
            pl.when(inside(axis, d))(copy.start)
            sent.append((inside(axis, d), copy))
            return (inside(axis, -d), copy)

        def arrive(copies):
            for cond, copy in copies:
                pl.when(cond)(copy.wait_recv)

        def exchange(base, zs, zr, ys, yr, xs, xr):
            copies = []
            for axis, src, dst, k in (("gy", ys, yr, 2), ("gz", zs, zr, 0), ("gx", xs, xr, 4)):
                for d in (-1, 1):
                    side = 0 if d < 0 else 1
                    piece = src if axis == "gx" else src.at[side]
                    copies.append(beside(axis, d, piece, dst.at[1 - side], base + k + side))
            return copies

        edges = {axis: (pos[axis] == 0, pos[axis] == {"gz": nz, "gy": ny, "gx": nx}[axis] - 1) for axis in AXES}
        for axis, bufs in (("gz", (zr0, zrf, zr1, zr2, zrF, zrG)), ("gy", (yr0, yrf, yr1, yr2, yrF, yrG)),
                           ("gx", (xr0, xrf, xr1, xr2))):
            for side in (0, 1):
                @pl.when(edges[axis][side])
                def _():
                    for buf in bufs:
                        buf[side] = jnp.zeros(buf.shape[1:], F32)
                    if axis == "gx":
                        column = lax.rem(lax.broadcasted_iota(jnp.int32, (H, L), 1), 8)
                        xr0[side, 1] = jnp.where(column // 2 == 2, 1.0, 0.0).astype(F32)
                    else:
                        buf = zr0 if axis == "gz" else yr0
                        buf[side, pl.ds(6 * H, H), :] = jnp.ones((H, L), F32)
        for strip, axis, side in ((srA, "gz", 1), (srB, "gy", 0)):
            for cond, slots in ((edges["gx"][side], (0, 1, 2)), (edges[axis][0], (1,)), (edges[axis][1], (2,))):
                @pl.when(cond)
                def _():
                    for slot in slots:
                        strip[slot] = jnp.zeros(strip.shape[1:], F32)

        lane = lax.broadcasted_iota(jnp.int32, (H, L), 1)
        row = lax.broadcasted_iota(jnp.int32, (H, L), 0)

        loads[0].wait()
        loads[1].wait()

        def reluctivity(z, _):
            density = den[plane(z), :]
            design = jnp.where(lab[plane(z), :] == 2, 1.0, 0.0).astype(F32)
            cube = density * density * density
            nu_design = 1.0 / (1.0 + MU_GAIN * cube)
            nu[plane(z), :] = 1.0 - design + design * nu_design
            kap[plane(z), :] = design * KAPPA_GAIN * cube
            return 0

        each(D, reluctivity, 0, WIDTH['reluctivity'])

        def pack(z, tiles, values):
            out = list(tiles)
            for c, v in enumerate(values):
                moved = pltpu.roll(v, (z * 8 + 2 * (c % 4) + 1) % L, 1)
                out[c // 4] = jnp.where(lane // 2 == z * 4 + c % 4, moved, out[c // 4])
            return tuple(out)

        def pair(xr, n):
            below = pltpu.roll(xr[0, n], 1, 1)
            above = pltpu.roll(xr[1, n], L - 1, 1)
            return jnp.where(lax.rem(lane, 2) == 0, above, below)

        def unpack(tile, z, count, first=0):
            return [pltpu.roll(tile, (-z * 8 - 2 * c - 1) % L, 1) for c in range(first, first + count)]

        zero = jnp.zeros((H, L), F32)

        def cell_rows(ref, count, first):
            return ref[pl.ds(first, count * D, stride=H), :]

        loads[2].wait()
        for side, z in ((0, 0), (1, D - 1)):
            for c in range(6):
                zs0[side, pl.ds(c * H, H), :] = a0[pl.ds((c * D + z) * H, H), :]
            zs0[side, pl.ds(6 * H, H), :] = nu[pl.ds(z * H, H), :]
            ys0[side, pl.ds(0, 6 * D), :] = cell_rows(a0, 6, side * (H - 1))
            ys0[side, pl.ds(6 * D, D), :] = cell_rows(nu, 1, side * (H - 1))

        def pack0(z, tiles):
            return pack(z, tiles, [a0[plane(c * D + z), :] for c in range(6)] + [nu[plane(z), :]])

        tiles = each(D, pack0, (zero, zero), WIDTH['pack0'])
        xs0[0] = tiles[0]
        xs0[1] = tiles[1]

        pl.semaphore_wait(barrier, expected)
        got0 = exchange(0, zs0, zr0, ys0, yr0, xs0, xr0)

        def sum_copy(stage, d, arriving):
            members, peer, slot = stages[stage]
            at = lax.rem(slot + d, members) if arriving else slot
            ref = sums[stage].at[at]
            return pltpu.make_async_remote_copy(
                src_ref=ref, dst_ref=ref, send_sem=sum_ss[stage].at[d], recv_sem=sum_rs[stage].at[at],
                device_id=peer(d), device_id_type=MESH)

        def sum_start(stage, value):
            members, _, slot = stages[stage]
            sums[stage][slot] = value
            for d in range(1, members):
                sum_copy(stage, d, False).start()

        def sum_finish(stage):
            members = stages[stage][0]
            for d in range(1, members):
                sum_copy(stage, d, True).wait_recv()
            value = sums[stage][0]
            for q in range(1, members):
                value = value + sums[stage][q]
            return value

        loads[3].wait()
        loads[4].wait()
        for side, z in ((0, 0), (1, D - 1)):
            for c in range(6):
                zsf[side, pl.ds(c * H, H), :] = f[pl.ds((c * D + z) * H, H), :]
            ysf[side] = cell_rows(f, 6, side * (H - 1))

        def packf(z, carry):
            tiles, re, im = carry
            values = [f[plane(c * D + z), :] for c in range(6)]
            mask = prt[plane(z), :].astype(F32)
            return (pack(z, tiles, values), re + mask * values[2], im + mask * values[5])

        tiles, port_re, port_im = each(D, packf, ((zero, zero), zero, zero), WIDTH['packf'])
        xsf[0] = tiles[0]
        xsf[1] = tiles[1]
        port_sum = jnp.concatenate(
            [jnp.sum(port_re, axis=0, keepdims=True), jnp.sum(port_im, axis=0, keepdims=True)], axis=0)

        sum_start("core", port_sum)

        def faces(z, _):
            v = nu[plane(z), :]
            below = nu[plane(clamp(z - 1)), :]
            above = nu[plane(clamp(z + 1)), :]
            wzm[plane(z), :] = jnp.where(z > 0, 0.5 * (v + below), 0.0)
            wzp[plane(z), :] = jnp.where(z < D - 1, 0.5 * (v + above), 0.0)
            wym[plane(z), :] = jnp.where(row > 0, 0.5 * (v + pltpu.roll(v, 1, 0)), 0.0)
            wyp[plane(z), :] = jnp.where(row < H - 1, 0.5 * (v + pltpu.roll(v, H - 1, 0)), 0.0)
            wxm[plane(z), :] = jnp.where(lane > 0, 0.5 * (v + pltpu.roll(v, 1, 1)), 0.0)
            wxp[plane(z), :] = jnp.where(lane < L - 1, 0.5 * (v + pltpu.roll(v, L - 1, 1)), 0.0)
            inner_sum = wzm[plane(z), :] + wzp[plane(z), :] + wym[plane(z), :] + wyp[plane(z), :]
            al[plane(z), :] = inner_sum + wxm[plane(z), :] + wxp[plane(z), :]
            return 0

        each(D, faces, 0, WIDTH['faces'])

        def inner(a, count, z, begin):
            zm = clamp(z - 1)
            zp = clamp(z + 1)
            w = [ref[plane(z), :] for ref in (wzm, wzp, wym, wyp, wxm, wxp)]
            for c in range(count):
                v = a[plane(c * D + z), :]
                total_ = w[0] * a[plane(c * D + zm), :] + w[1] * a[plane(c * D + zp), :]
                total_ += w[2] * pltpu.roll(v, 1, 0) + w[3] * pltpu.roll(v, H - 1, 0)
                total_ += w[4] * pltpu.roll(v, 1, 1) + w[5] * pltpu.roll(v, L - 1, 1)
                first = begin(c)
                t[plane(c * D + z), :] = total_ if first is None else total_ + first

        def inner1(z, _):
            kappa = kap[plane(z), :]
            inner(a0, 6, z, lambda c: kappa * f[plane(c * D + z), :])
            return 0

        each(D, inner1, 0, WIDTH['inner1'])
        sum_start("gx", sum_finish("core"))
        gotf = exchange(6, zsf, zrf, ysf, yrf, xsf, xrf)

        arrive(got0)
        x0 = [pair(xr0, 0), pair(xr0, 1)]
        outer_x = jnp.logical_or(lane == 0, lane == L - 1)

        hz = []
        hy = []
        for side, z in ((0, 0), (1, D - 1)):
            hz.append(0.5 * (nu[pl.ds(z * H, H), :] + zr0[side, pl.ds(6 * H, H), :]))
            hy.append(0.5 * (cell_rows(nu, 1, side * (H - 1)) + yr0[side, pl.ds(6 * D, D), :]))

        def add_outer(zr, yr, count):
            for side, z in ((0, 0), (1, D - 1)):
                for c in range(count):
                    t[pl.ds((c * D + z) * H, H), :] += hz[side] * zr[side, pl.ds(c * H, H), :]
                for c in range(count):
                    at = pl.ds(c * D * H + side * (H - 1), D, stride=H)
                    t[at, :] = t[at, :] + hy[side] * yr[side, pl.ds(c * D, D), :]

        add_outer(zr0, yr0, 6)
        for side, z in ((0, 0), (1, D - 1)):
            al[pl.ds(z * H, H), :] += hz[side]
            at = pl.ds(side * (H - 1), D, stride=H)
            al[at, :] = al[at, :] + hy[side]

        def finish(z, a, tiles_in, count):
            alpha = al[plane(z), :]
            beta = be[plane(z), :]
            face = hx[plane(z), :]
            outside = unpack(tiles_in[0], z, 4) + unpack(tiles_in[1], z, count - 4)
            tt = [t[plane(c * D + z), :] + face * outside[c] for c in range(count)]
            out = [None] * count
            pairs = [(0, 3), (1, 4), (2, 5)] + ([(6, 7)] if count == 8 else [])
            for re, im in pairs:
                out[re] = (1.0 - RELAX) * a[plane(re * D + z), :] + (tt[re] * alpha + tt[im] * beta)
                out[im] = (1.0 - RELAX) * a[plane(im * D + z), :] + (tt[im] * alpha - tt[re] * beta)
            return out

        def sweep1(z, tiles):
            if z == 13:
                sum_start("gy", sum_finish("gx"))
            face = jnp.where(outer_x, 0.5 * (nu[plane(z), :] + unpack(x0[1], z, 1, 2)[0]), 0.0)
            hx[plane(z), :] = face
            d = al[plane(z), :] + face
            kappa = kap[plane(z), :]
            weight = RELAX / (d * d + kappa * kappa)
            al[plane(z), :] = d * weight
            be[plane(z), :] = kappa * weight
            out = finish(z, a0, x0, 6)
            mask = prt[plane(z), :].astype(F32)
            out.append(mask * (d * weight))
            out.append(-mask * (kappa * weight))
            for c in range(8):
                a1[plane(c * D + z), :] = out[c]
            return pack(z, tiles, out)

        tiles = each(D, sweep1, (zero, zero), WIDTH['sweep1'])
        xs1[0] = tiles[0]
        xs1[1] = tiles[1]
        for side, z in ((0, 0), (1, D - 1)):
            for c in range(8):
                zs1[side, pl.ds(c * H, H), :] = a1[pl.ds((c * D + z) * H, H), :]
            ys1[side] = cell_rows(a1, 8, side * (H - 1))
        got1 = exchange(12, zs1, zr1, ys1, yr1, xs1, xr1)

        def inner2(z, _):
            kappa = kap[plane(z), :]

            def begin(c):
                if c < 6:
                    return kappa * f[plane(c * D + z), :]
                return prt[plane(z), :].astype(F32) if c == 6 else None

            inner(a1, 8, z, begin)
            return 0

        each(D, inner2, 0, WIDTH['inner2'])
        for load in loads[5:]:
            load.wait()
        ry_l = jnp.zeros((H, L), jnp.int32)
        rz_l = jnp.zeros((H, L), jnp.int32)
        ry_r = jnp.zeros((H, L), jnp.int32)
        for b in range(H):
            ry_b = ry[gy * H + b]
            rz_b = rz[gz * D + b]
            ry_l = jnp.where(lax.rem(lane, H) == b, ry_b, ry_l)
            rz_l = jnp.where(lane // 8 == b, rz_b, rz_l)
            ry_r = jnp.where(row == b, ry_b, ry_r)

        def build(k, _):
            n = k // 8
            q = mod(k, 8)
            band_y = jnp.maximum(ry_l + 1 - jnp.abs(lax.rem(lane, H) - (row + (n - 1) * H)), 0)
            ky[plane(k), :] = jnp.where(lane // H == q, band_y, 0).astype(F32).astype(BF16)
            band_z = jnp.maximum(rz_l + 1 - jnp.abs(lane // 8 - (2 * q + row // 8 + (n - 1) * D)), 0)
            kz[plane(k), :] = jnp.where(lax.rem(lane, 8) == lax.rem(row, 8), band_z, 0).astype(F32).astype(BF16)
            return 0

        each(24, build, 0, WIDTH['build'])
        rx_own = jnp.broadcast_to(rx[pl.ds(gx, 1), :], (H, L))
        rx_low = jnp.broadcast_to(rx[pl.ds(jnp.maximum(gx - 1, 0), 1), :], (H, L))
        rx_high = jnp.broadcast_to(rx[pl.ds(jnp.minimum(gx + 1, nx - 1), 1), :], (H, L))

        def build_x(k, _):
            target = row + k * H
            own = jnp.maximum(rx_own + 1 - jnp.abs(lane - target), 0)
            low = jnp.maximum(rx_low + 1 - jnp.abs(lane - L - target), 0)
            high = jnp.maximum(rx_high + 1 - jnp.abs(lane + L - target), 0)
            bx[plane(k), pl.ds(0, L)] = own.astype(F32).astype(BF16)
            bx[plane(k), pl.ds(L, L)] = jnp.where(lane < L // 2, high, low).astype(F32).astype(BF16)
            return 0

        each(L // H, build_x, 0, WIDTH['build_x'])
        norm_yx = (norm_of(ry_r, gy * H + row, total["gy"]) * norm_of(rx_own, gx * L + lane, total["gx"])).astype(F32)

        def material(z, _):
            density = den[plane(z), :]
            design = jnp.where(lab[plane(z), :] == 2, 1.0, 0.0).astype(F32)
            square = density * density
            cube = square * density
            nu_design = 1.0 / (1.0 + MU_GAIN * cube)
            gz_i = gz * D + z
            norm_z = norm_of(rz[gz_i], gz_i, total["gz"]).astype(F32)
            inverse = SENS_GAIN / (norm_yx * norm_z)
            nu_slope = -3.0 * MU_GAIN * design * square * nu_design * nu_design
            kk[plane(z), :] = -0.5 * nu_slope * inverse
            qq[plane(z), :] = 3.0 * KAPPA_GAIN * design * square * inverse
            return 0

        each(D, material, 0, WIDTH['material'])

        sum_start("gz", sum_finish("gy"))
        arrive(gotf)
        xf = [pair(xrf, 0), pair(xrf, 1)]

        def across_x(z, _):
            outside = unpack(xf[0], z, 4) + unpack(xf[1], z, 2)
            for c in range(6):
                at = plane(c * D + z)
                near_x[at, :] = jnp.where(outer_x, f[at, :] - outside[c], 0.0)
            return 0

        each(D, across_x, 0, WIDTH['across_x'])
        arrive(got1)
        add_outer(zr1, yr1, 8)
        x1 = [pair(xr1, 0), pair(xr1, 1)]

        def shares(answers, near):
            main = None
            for c in range(6):
                term = answers[c] * near[c]
                main = term if c == 0 else main + term if c < 3 else main - term
            return [main, answers[6] * near[2] - answers[7] * near[5], -(answers[7] * near[2]) - answers[6] * near[5]]

        def sweep2(z, tile):
            out = finish(z, a1, x1, 8)
            for c in range(8):
                a2[plane(c * D + z), :] = out[c]
            share = shares(out, [near_x[plane(c * D + z), :] for c in range(6)])
            for k in range(3):
                t[plane(k * D + z), :] = share[k]
            return pack(z, (tile,), share)[0]

        xs2[0] = each(D, sweep2, zero, WIDTH['sweep2'])
        hz2 = []
        hy2 = []
        for side, z in ((0, 0), (1, D - 1)):
            at = [pl.ds((c * D + z) * H, H) for c in range(8)]
            near = [f[at[c], :] - zrf[side, pl.ds(c * H, H), :] for c in range(6)]
            share = shares([a2[where, :] for where in at], near)
            for k in range(3):
                zs2[side, pl.ds(k * H, H), :] = share[k]
            hz2.append(share)
            at = [pl.ds(c * D * H + side * (H - 1), D, stride=H) for c in range(8)]
            near = [f[at[c], :] - yrf[side, pl.ds(c * D, D), :] for c in range(6)]
            share = shares([a2[where, :] for where in at], near)
            for k in range(3):
                ys2[side, pl.ds(k * D, D), :] = share[k]
            hy2.append(share)
        got2 = exchange(18, zs2, zr2, ys2, yr2, xs2, xr2)

        def sens(z, last):
            zp = clamp(z + 1)
            av = [a2[plane(c * D + z), :] for c in range(8)]
            fv = [f[plane(c * D + z), :] for c in range(6)]
            above = [a2[plane(c * D + zp), :] for c in range(8)], [f[plane(c * D + zp), :] for c in range(6)]
            ez = shares([v - w for v, w in zip(av, above[0])], [v - w for v, w in zip(fv, above[1])])
            ey = shares([v - pltpu.roll(v, H - 1, 0) for v in av], [v - pltpu.roll(v, H - 1, 0) for v in fv])
            ex = shares([v - pltpu.roll(v, L - 1, 1) for v in av], [v - pltpu.roll(v, L - 1, 1) for v in fv])
            more = [zero, av[6] * fv[5] + av[7] * fv[2], av[6] * fv[2] - av[7] * fv[5]]
            for c in range(6):
                more[0] = more[0] + fv[c] * (fv[c] + av[(c + 3) % 6])
            for k in range(3):
                along_y = jnp.where(row < H - 1, ey[k], 0.0)
                along_x = jnp.where(lane < L - 1, ex[k], 0.0)
                energy = ez[k] + last[k] + along_y + pltpu.roll(along_y, 1, 0)
                energy = energy + along_x + pltpu.roll(along_x, 1, 1) + t[plane(k * D + z), :]
                s[plane(k * D + z), :] = kk[plane(z), :] * energy + qq[plane(z), :] * more[k]
            return ez

        each(D, sens, [zero] * 3, WIDTH['sens'])
        total_ports = sum_finish("gz")
        link_re = scale * jnp.sum(total_ports[0:1])
        link_im = scale * jnp.sum(total_ports[1:2])
        imp_o[0] = link_re
        imp_o[1] = link_im
        coef_re = 2.0 * (link_re - zt[0])
        coef_im = -2.0 * (link_im - zt[1])

        def joined(parts):
            return parts[0] + (coef_re * parts[1] + coef_im * parts[2])

        def join(z, _):
            s[plane(z), :] = joined([s[plane(k * D + z), :] for k in range(3)])
            return 0

        each(D, join, 0, WIDTH['join'])
        for side, z in ((0, 0), (1, D - 1)):
            at = pl.ds(z * H, H)
            s[at, :] += kk[at, :] * joined(hz2[side])
            at = pl.ds(side * (H - 1), D, stride=H)
            s[at, :] = s[at, :] + kk[at, :] * joined(hy2[side])
        arrive(got2)
        for side, z in ((0, 0), (1, D - 1)):
            at = pl.ds(z * H, H)
            s[at, :] += kk[at, :] * joined([zr2[side, pl.ds(k * H, H), :] for k in range(3)])
            at = pl.ds(side * (H - 1), D, stride=H)
            s[at, :] = s[at, :] + kk[at, :] * joined([yr2[side, pl.ds(k * D, D), :] for k in range(3)])
        tile2 = pair(xr2, 0)
        tile2 = joined([tile2, pltpu.roll(tile2, L - 2, 1), pltpu.roll(tile2, L - 4, 1)])

        def add_x(z, _):
            outside = unpack(tile2, z, 1)[0]
            s[plane(z), :] += kk[plane(z), :] * jnp.where(outer_x, outside, 0.0)
            return 0

        each(D, add_x, 0, WIDTH['add_x'])

        lane8 = lax.broadcasted_iota(jnp.int32, (8, L), 1)
        left = lane < L // 2
        left8 = lane8 < L // 2

        def turn(v):
            return pltpu.roll(v, L // 2, 1)

        def split(v):
            high = v.astype(BF16)
            return high, (v - high.astype(F32)).astype(BF16)

        def keep(ref, k, v):
            high, low = split(v)
            ref[pl.ds(k * H, H), pl.ds(0, L)] = high
            ref[pl.ds(k * H, H), pl.ds(L, L)] = low

        def stack(a, b):
            return jnp.concatenate([a, b], axis=0)

        def band(matrix, value, n, dst):
            both = jnp.dot(matrix[pl.ds(n * L, L), :], value[...], preferred_element_type=F32)
            dst[...] = both[:, :L] + both[:, L:]

        def band_out(matrix, value, axis, src, dst, own, slot):
            band(matrix, value, 0, src.at[0])
            band(matrix, value, 2, src.at[1])
            got = [beside(axis, d, src.at[side], dst.at[1 - side], slot + side) for side, d in ((0, -1), (1, 1))]
            band(matrix, value, 1, own)
            return got

        for p in range(8):
            keep(vbA, p, jnp.where(left, s[plane(p), :], turn(s[plane(p + 8), :])))
        gotY = band_out(ky, vbA, "gy", ysF, yrF, oyF, 24)
        for k in range(8):
            tiles = []
            for z in (2 * k, 2 * k + 1):
                v = s[plane(z), :]
                tiles.append(jnp.where(left8, turn(v[:8]), v[8:]))
            keep(vbB, k, stack(*tiles))
        gotZ = band_out(kz, vbB, "gz", zsF, zrF, ozF, 26)

        def answer(z, _):
            re, im = a2[plane(6 * D + z), :], a2[plane(7 * D + z), :]
            added = {2: coef_re * re - coef_im * im, 5: coef_re * im + coef_im * re}
            for c in added:
                a2[plane(c * D + z), :] += added[c]
            return 0

        each(D, answer, 0, WIDTH['answer'])
        adj_copy = pltpu.make_async_copy(a2.at[pl.ds(0, 6 * D * H), :], adj_o, out_sem)
        adj_copy.start()

        def eight(ref, k):
            return ref[pl.ds(8 * k, 8), :]

        arrive(gotZ)
        vz = [eight(ozF, z) + eight(zrF.at[0], z) + eight(zrF.at[1], z) for z in range(D)]
        for p in range(8):
            low, high = vz[p], vz[p + 8]
            keep(vbB, p, stack(jnp.where(left8, low, turn(high)), jnp.where(left8, turn(low), high)))
        gotY2 = band_out(ky, vbB, "gy", ysG, yrG, oyG, 30)
        def columns(dst, src, count, rows_, offset, lanes):
            for g in range(count // 4):
                tile = None
                for q in range(4):
                    moved = pltpu.roll(src[pl.ds((4 * g + q) * rows_, rows_), :], (16 * q - offset) % L, 1)
                    tile = moved if q == 0 else jnp.where(lax.rem(lanes // REACH, 4) == q, moved, tile)
                dst[pl.ds(g * rows_, rows_), :] = tile

        def send_columns(axis, dx, st, sr, src, slot):
            got = []
            for n, d in ((0, 0), (1, -1), (2, 1)):
                if axis == "gz":
                    columns(st.at[n], src[n], D, 8, 0, lane8)
                else:
                    columns(st.at[n], src[n], 8, H, 48, lane)
                if d == 0:
                    got.append(beside("gx", dx, st.at[0], sr.at[0], slot))
                    continue
                go = jnp.logical_and(inside("gx", dx), inside(axis, d))
                come = jnp.logical_and(inside("gx", -dx), inside(axis, -d))
                copy = remote(st.at[n], sr.at[3 - n], slot + n, {axis: pos[axis] + d, "gx": gx + dx})
                pl.when(go)(copy.start)
                sent.append((go, copy))
                got.append((come, copy))
            return got

        gotX = send_columns("gy", 1, stB, srB, (oyG, ysG.at[0], ysG.at[1]), 35)
        arrive(gotY)
        vy = [oyF[plane(p), :] + yrF[0, plane(p), :] + yrF[1, plane(p), :] for p in range(8)]
        for k in range(4):
            near, far = [], []
            for p in (2 * k, 2 * k + 1):
                top, bottom = vy[p][:8], vy[p][8:]
                near.append(jnp.where(left8, top, turn(bottom)))
                far.append(jnp.where(left8, turn(top), bottom))
            keep(vbA, k, stack(*near))
            keep(vbA, k + 4, stack(*far))
        gotZ2 = band_out(kz, vbA, "gz", zsG, zrG, ozG, 28)

        gotX += send_columns("gz", -1, stA, srA, (ozG, zsG.at[0], zsG.at[1]), 32)
        arrive(gotZ2)
        vz = [eight(ozG, z) + eight(zrG.at[0], z) + eight(zrG.at[1], z) for z in range(D)]
        arrive(gotY2)
        arrive(gotX)
        ga = [sum(srA[n, pl.ds(8 * g, 8), :] for n in range(3)) for g in range(4)]
        gb = [sum(srB[n, plane(g), :] for n in range(3)) for g in range(2)]
        vy = [oyG[plane(p), :] + yrG[0, plane(p), :] + yrG[1, plane(p), :] for p in range(8)]
        for z in range(D):
            v = vz[z]
            own = jnp.where(left, stack(v, turn(v)), turn(vy[z]) if z < 8 else vy[z - 8])
            group = ga[z // 4]
            above = stack(*(pltpu.roll(group, (-16 * (z % 4) - 64 * h) % L, 1) for h in range(2)))
            below = pltpu.roll(gb[z % 8 // 4], (112 - 64 * (z // 8) - 16 * (z % 4)) % L, 1)
            for k, part in enumerate((own, jnp.where(left, above, below))):
                big, small = split(part)
                xin[plane(z), pl.ds(k * L, L)] = big
                xin[plane(z + D), pl.ds(k * L, L)] = small
        both = lax.dot_general(xin[...], bx[...], (((1,), (1,)), ((), ())), preferred_element_type=F32)
        grad_o[...] = both[:D * H] + both[D * H:]

        for cond, copy in sent:
            pl.when(cond)(copy.wait_send)
        for stage in stages:
            for d in range(1, stages[stage][0]):
                sum_copy(stage, d, False).wait_send()
        adj_copy.wait()

    return kernel


def solution(mesh):
    sizes = dict(mesh.shape)
    nz, ny, nx = (sizes[a] for a in AXES)
    rows = D * H
    vm = lambda *shape: pltpu.VMEM(shape, F32)
    field = vm(rows, L)

    def halo(planes, tiles):
        y = vm(2, planes * D, L)
        z = vm(2, planes * H, L)
        return [z, y, vm(tiles, H, L), z, y, vm(2, tiles, H, L)]

    scratch = [
        vm(6 * rows, L), pltpu.SMEM((2,), F32), pltpu.SMEM((nz * D,), jnp.int32), pltpu.SMEM((ny * H,), jnp.int32),
        pltpu.VMEM((nx, L), jnp.int32),
        vm(6 * rows, L), vm(6 * rows, L), field, pltpu.VMEM((rows, L), jnp.int32), pltpu.VMEM((rows, L), jnp.int32),
        vm(8 * rows, L), vm(8 * rows, L), vm(8 * rows, L),
    ] + [field] * 13 + [vm(3 * rows, L)] + halo(7, 2) + halo(6, 2) + halo(8, 2) + [
        vm(2, 3 * H, L), vm(2, 3 * D, L), vm(1, H, L), vm(2, 3 * H, L), vm(2, 3 * D, L), vm(2, 1, H, L),
        pltpu.VMEM((3 * L, L), BF16), pltpu.VMEM((3 * L, L), BF16), pltpu.VMEM((L, 2 * L), BF16),
    ] + [vm(2, L, L)] * 8 + [vm(L, L)] * 4 + [vm(3, 32, L)] * 4 + [
        pltpu.VMEM((L, 2 * L), BF16), pltpu.VMEM((L, 2 * L), BF16), pltpu.VMEM((2 * rows, 2 * L), BF16),
    ] + [vm(n, 2, L) for n in (CORES, nx, ny, nz // CORES)] + [
        pltpu.SemaphoreType.DMA((9,)), pltpu.SemaphoreType.DMA,
        pltpu.SemaphoreType.DMA((38,)), pltpu.SemaphoreType.DMA((38,)),
    ] + [pltpu.SemaphoreType.DMA((n,)) for n in (CORES, nx, ny, nz // CORES) for _ in range(2)]
    hbm = pl.BlockSpec(memory_space=pl.ANY)
    smem = pl.BlockSpec(memory_space=pltpu.SMEM)
    vmem = pl.BlockSpec(memory_space=pltpu.VMEM)
    call = pl.pallas_call(
        make_kernel(sizes),
        out_shape=(
            pltpu.VMEM((6 * rows, L), F32),
            pltpu.VMEM((rows, L), F32),
            jax.ShapeDtypeStruct((2,), F32),
        ),
        in_specs=[hbm] * 9,
        out_specs=(hbm, vmem, smem),
        scratch_shapes=scratch,
        compiler_params=pltpu.CompilerParams(
            collective_id=0, has_side_effects=True, vmem_limit_bytes=32 * 2**20),
    )

    def hand_over(adj_i, grad_i, imp_i, adj_o, grad_o, imp_o, imp, sem, imp_sem):
        first = pltpu.make_async_copy(imp_i, imp, imp_sem)
        copies = [
            pltpu.make_async_copy(src, dst, sem.at[k])
            for k, (src, dst) in enumerate(((adj_i, adj_o), (grad_i, grad_o), (imp, imp_o)))
        ]
        first.start()
        copies[0].start()
        copies[1].start()
        first.wait()
        copies[2].start()
        for copy in copies:
            copy.wait()

    results = pl.pallas_call(
        hand_over,
        out_shape=(
            jax.ShapeDtypeStruct((6 * rows, L), F32),
            jax.ShapeDtypeStruct((rows, L), F32),
            jax.ShapeDtypeStruct((2,), F32),
        ),
        in_specs=[hbm] * 3,
        out_specs=(hbm,) * 3,
        scratch_shapes=[pltpu.SMEM((2,), F32), pltpu.SemaphoreType.DMA((3,)), pltpu.SemaphoreType.DMA],
        compiler_params=pltpu.CompilerParams(vmem_limit_bytes=16 * 2**20))

    def body(forward, adjoint_prev, density, labels, ports, z_target, radius_z, radius_y, radius_x):
        arrays = (
            forward.reshape(6 * rows, L), adjoint_prev.reshape(6 * rows, L), density.reshape(rows, L),
            labels.reshape(rows, L), ports.reshape(rows, L), z_target, radius_z, radius_y,
            radius_x.reshape(nx, L))
        place = pltpu.with_memory_space_constraint
        made = call(*(place(v, pltpu.HBM) for v in arrays))
        adjoint, gradient, impedance = results(place(made[0], pltpu.VMEM), place(made[1], pltpu.VMEM), made[2])
        return adjoint.reshape(6, D, H, L), gradient.reshape(D, H, L), impedance

    in_specs = (P(None, *AXES),) * 2 + (P(*AXES),) * 3 + (P(),) * 4
    out_specs = (P(None, *AXES), P(*AXES), P())
    return jax.shard_map(body, mesh=mesh, in_specs=in_specs, out_specs=out_specs, check_vma=False)
```

```python
import jax
import jax.numpy as jnp
from jax import lax
from jax.experimental import pallas as pl
from jax.experimental.pallas import tpu as pltpu
from jax.sharding import PartitionSpec as P

MU_GAIN = 19.0
KAPPA_GAIN = 2.0
RELAX = 0.8
SENS_GAIN = 0.1
REACH = 16
CORES = 2
WIDTH = dict(add_x=16, add_y=16, add_z=8, build=4, build_x=4, faces=16, inner1=16, inner2=16, material=16, pack0=16, packf=16, sens=16, step=8, sweep1=16, sweep2=16, across_x=16, reluctivity=16, join=16, answer=16)
MESH = pl.DeviceIdType.MESH
AXES = ("gz", "gy", "gx")
F32 = jnp.float32
BF16 = jnp.bfloat16
D = 16
H = 16
L = 128


def plane(index):
    if isinstance(index, int):
        return pl.ds(index * H, H)
    return pl.ds(pl.multiple_of(index * H, H), H)


def each(count, step, carry, width):
    if width == count:
        for k in range(count):
            carry = step(k, carry)
        return carry

    def group(g, carry):
        for k in range(width):
            carry = step(g * width + k, carry)
        return carry

    return lax.fori_loop(0, count // width, group, carry)


def mod(a, b):
    return a % b if isinstance(a, int) else lax.rem(a, b)


def clamp(value):
    if isinstance(value, int):
        return min(max(value, 0), D - 1)
    return jnp.clip(value, 0, D - 1)


def tri(value):
    value = jnp.maximum(value, 0)
    return value * (value + 1) // 2


def norm_of(radius, position, length):
    whole = (radius + 1) * (radius + 1)
    return whole - tri(radius - position) - tri(radius - (length - 1 - position))


def make_kernel(sizes):
    nz, ny, nx = sizes["gz"], sizes["gy"], sizes["gx"]
    total = {"gz": nz * D, "gy": ny * H, "gx": nx * L}
    scale = 4.0 / (total["gz"] * total["gy"] * total["gx"])

    def kernel(fwd_h, adj_h, den_h, lab_h, prt_h, zt_h, rz_h, ry_h, rx_h,
               adj_o, grad_o, imp_o,
               near_x, zt, rz, ry, rx, f, a0, den, lab, prt, a1, a2, t,
               nu, kap, wzm, wzp, wym, wyp, wxm, wxp, al, be, hx, kk, qq, s,
               zs0, ys0, xs0, zr0, yr0, xr0,
               zsf, ysf, xsf, zrf, yrf, xrf,
               zs1, ys1, xs1, zr1, yr1, xr1,
               zs2, ys2, xs2, zr2, yr2, xr2,
               ky, kz, bx, ysF, yrF, zsF, zrF, ysG, yrG, zsG, zrG, oyF, ozF, oyG, ozG,
               stA, srA, stB, srB, vbA, vbB, xin,
               sum_core, sum_x, sum_y, sum_z, in_sem, out_sem, ss, rs,
               ss_core, rs_core, ss_x, rs_x, ss_y, rs_y, ss_z, rs_z):
        sums = {"core": sum_core, "gx": sum_x, "gy": sum_y, "gz": sum_z}
        sum_ss = {"core": ss_core, "gx": ss_x, "gy": ss_y, "gz": ss_z}
        sum_rs = {"core": rs_core, "gx": rs_x, "gy": rs_y, "gz": rs_z}
        gz, gy, gx = (lax.axis_index(a) for a in AXES)
        pos = {"gz": gz, "gy": gy, "gx": gx}
        core = lax.rem(gz, CORES)

        def inside(axis, d):
            size = {"gz": nz, "gy": ny, "gx": nx}[axis]
            return pos[axis] < size - 1 if d > 0 else pos[axis] > 0

        stages = {
            "core": (CORES, lambda d: {"gz": gz - core + lax.rem(core + d, CORES)}, core),
            "gx": (nx, lambda d: {"gx": lax.rem(gx + d, nx)}, gx),
            "gy": (ny, lambda d: {"gy": lax.rem(gy + d, ny)}, gy),
            "gz": (nz // CORES, lambda d: {"gz": lax.rem(gz + CORES * d, nz)}, gz // CORES),
        }
        barrier = pltpu.get_barrier_semaphore()
        others = []
        for axis, dx in (("gz", 1), ("gy", -1)):
            for d in (-1, 1):
                others.append(({axis: pos[axis] + d, "gx": gx + dx},
                               jnp.logical_and(inside(axis, d), inside("gx", dx)),
                               jnp.logical_and(inside(axis, -d), inside("gx", -dx))))
        for d in (-1, 1):
            near = jnp.logical_and(inside("gz", d), (core == 0) if d < 0 else (core == CORES - 1))
            others.append(({"gz": gz + d}, near, near))
        expected = 0
        for members, peer, _ in reversed(stages.values()):
            for d in sorted(range(1, members), key=lambda d: abs(d - members / 2)):
                pl.semaphore_signal(barrier, inc=1, device_id=peer(d), device_id_type=MESH)
                expected += 1
        for where, comes, goes in others:
            @pl.when(comes)
            def _():
                pl.semaphore_signal(barrier, inc=1, device_id=where, device_id_type=MESH)
            expected = expected + goes.astype(jnp.int32)

        loads = [
            pltpu.make_async_copy(src, dst, in_sem.at[k])
            for k, (src, dst) in enumerate((
                (den_h, den), (lab_h, lab), (adj_h, a0.at[pl.ds(0, 6 * D * H), :]),
                (fwd_h, f.at[pl.ds(0, 6 * D * H), :]), (prt_h, prt),
                (rx_h, rx), (ry_h, ry), (rz_h, rz), (zt_h, zt)))
        ]
        for load in loads[5:] + loads[:5]:
            load.start()

        def remote(src, dst, slot, where):
            return pltpu.make_async_remote_copy(
                src_ref=src, dst_ref=dst, send_sem=ss.at[slot], recv_sem=rs.at[slot],
                device_id=where, device_id_type=MESH)

        sent = []

        def beside(axis, d, src, dst, slot):
            copy = remote(src, dst, slot, {axis: pos[axis] + d})
            pl.when(inside(axis, d))(copy.start)
            sent.append((inside(axis, d), copy))
            return (inside(axis, -d), copy)

        def arrive(copies):
            for cond, copy in copies:
                pl.when(cond)(copy.wait_recv)

        def exchange(base, zs, zr, ys, yr, xs, xr):
            copies = []
            for axis, src, dst, k in (("gy", ys, yr, 2), ("gz", zs, zr, 0), ("gx", xs, xr, 4)):
                for d in (-1, 1):
                    side = 0 if d < 0 else 1
                    piece = src if axis == "gx" else src.at[side]
                    copies.append(beside(axis, d, piece, dst.at[1 - side], base + k + side))
            return copies

        edges = {axis: (pos[axis] == 0, pos[axis] == {"gz": nz, "gy": ny, "gx": nx}[axis] - 1) for axis in AXES}
        for axis, bufs in (("gz", (zr0, zrf, zr1, zr2, zrF, zrG)), ("gy", (yr0, yrf, yr1, yr2, yrF, yrG)),
                           ("gx", (xr0, xrf, xr1, xr2))):
            for side in (0, 1):
                @pl.when(edges[axis][side])
                def _():
                    for buf in bufs:
                        buf[side] = jnp.zeros(buf.shape[1:], F32)
                    if axis == "gx":
                        column = lax.rem(lax.broadcasted_iota(jnp.int32, (H, L), 1), 8)
                        xr0[side, 1] = jnp.where(column // 2 == 2, 1.0, 0.0).astype(F32)
                    else:
                        buf = zr0 if axis == "gz" else yr0
                        buf[side, pl.ds(6 * H, H), :] = jnp.ones((H, L), F32)
        for strip, axis, side in ((srA, "gz", 1), (srB, "gy", 0)):
            for cond, slots in ((edges["gx"][side], (0, 1, 2)), (edges[axis][0], (1,)), (edges[axis][1], (2,))):
                @pl.when(cond)
                def _():
                    for slot in slots:
                        strip[slot] = jnp.zeros(strip.shape[1:], F32)

        lane = lax.broadcasted_iota(jnp.int32, (H, L), 1)
        row = lax.broadcasted_iota(jnp.int32, (H, L), 0)

        loads[0].wait()
        loads[1].wait()

        def reluctivity(z, _):
            density = den[plane(z), :]
            design = jnp.where(lab[plane(z), :] == 2, 1.0, 0.0).astype(F32)
            cube = density * density * density
            nu_design = 1.0 / (1.0 + MU_GAIN * cube)
            nu[plane(z), :] = 1.0 - design + design * nu_design
            kap[plane(z), :] = design * KAPPA_GAIN * cube
            return 0

        each(D, reluctivity, 0, WIDTH['reluctivity'])

        def pack(z, tiles, values):
            out = list(tiles)
            for c, v in enumerate(values):
                moved = pltpu.roll(v, (z * 8 + 2 * (c % 4) + 1) % L, 1)
                out[c // 4] = jnp.where(lane // 2 == z * 4 + c % 4, moved, out[c // 4])
            return tuple(out)

        def pair(xr, n):
            below = pltpu.roll(xr[0, n], 1, 1)
            above = pltpu.roll(xr[1, n], L - 1, 1)
            return jnp.where(lax.rem(lane, 2) == 0, above, below)

        def unpack(tile, z, count, first=0):
            return [pltpu.roll(tile, (-z * 8 - 2 * c - 1) % L, 1) for c in range(first, first + count)]

        zero = jnp.zeros((H, L), F32)

        def cell_rows(ref, count, first):
            return ref[pl.ds(first, count * D, stride=H), :]

        loads[2].wait()
        for side, z in ((0, 0), (1, D - 1)):
            for c in range(6):
                zs0[side, pl.ds(c * H, H), :] = a0[pl.ds((c * D + z) * H, H), :]
            zs0[side, pl.ds(6 * H, H), :] = nu[pl.ds(z * H, H), :]
            ys0[side, pl.ds(0, 6 * D), :] = cell_rows(a0, 6, side * (H - 1))
            ys0[side, pl.ds(6 * D, D), :] = cell_rows(nu, 1, side * (H - 1))

        def pack0(z, tiles):
            return pack(z, tiles, [a0[plane(c * D + z), :] for c in range(6)] + [nu[plane(z), :]])

        tiles = each(D, pack0, (zero, zero), WIDTH['pack0'])
        xs0[0] = tiles[0]
        xs0[1] = tiles[1]

        pl.semaphore_wait(barrier, expected)
        got0 = exchange(0, zs0, zr0, ys0, yr0, xs0, xr0)

        def sum_copy(stage, d, arriving):
            members, peer, slot = stages[stage]
            at = lax.rem(slot + d, members) if arriving else slot
            ref = sums[stage].at[at]
            return pltpu.make_async_remote_copy(
                src_ref=ref, dst_ref=ref, send_sem=sum_ss[stage].at[d], recv_sem=sum_rs[stage].at[at],
                device_id=peer(d), device_id_type=MESH)

        def sum_start(stage, value):
            members, _, slot = stages[stage]
            sums[stage][slot] = value
            for d in range(1, members):
                sum_copy(stage, d, False).start()

        def sum_finish(stage):
            members = stages[stage][0]
            for d in range(1, members):
                sum_copy(stage, d, True).wait_recv()
            value = sums[stage][0]
            for q in range(1, members):
                value = value + sums[stage][q]
            return value

        loads[3].wait()
        loads[4].wait()
        for side, z in ((0, 0), (1, D - 1)):
            for c in range(6):
                zsf[side, pl.ds(c * H, H), :] = f[pl.ds((c * D + z) * H, H), :]
            ysf[side] = cell_rows(f, 6, side * (H - 1))

        def packf(z, carry):
            tiles, re, im = carry
            values = [f[plane(c * D + z), :] for c in range(6)]
            mask = prt[plane(z), :].astype(F32)
            return (pack(z, tiles, values), re + mask * values[2], im + mask * values[5])

        tiles, port_re, port_im = each(D, packf, ((zero, zero), zero, zero), WIDTH['packf'])
        xsf[0] = tiles[0]
        xsf[1] = tiles[1]
        port_sum = jnp.concatenate(
            [jnp.sum(port_re, axis=0, keepdims=True), jnp.sum(port_im, axis=0, keepdims=True)], axis=0)

        sum_start("core", port_sum)

        def faces(z, _):
            v = nu[plane(z), :]
            below = nu[plane(clamp(z - 1)), :]
            above = nu[plane(clamp(z + 1)), :]
            wzm[plane(z), :] = jnp.where(z > 0, 0.5 * (v + below), 0.0)
            wzp[plane(z), :] = jnp.where(z < D - 1, 0.5 * (v + above), 0.0)
            wym[plane(z), :] = jnp.where(row > 0, 0.5 * (v + pltpu.roll(v, 1, 0)), 0.0)
            wyp[plane(z), :] = jnp.where(row < H - 1, 0.5 * (v + pltpu.roll(v, H - 1, 0)), 0.0)
            wxm[plane(z), :] = jnp.where(lane > 0, 0.5 * (v + pltpu.roll(v, 1, 1)), 0.0)
            wxp[plane(z), :] = jnp.where(lane < L - 1, 0.5 * (v + pltpu.roll(v, L - 1, 1)), 0.0)
            inner_sum = wzm[plane(z), :] + wzp[plane(z), :] + wym[plane(z), :] + wyp[plane(z), :]
            al[plane(z), :] = inner_sum + wxm[plane(z), :] + wxp[plane(z), :]
            return 0

        each(D, faces, 0, WIDTH['faces'])

        def inner(a, count, z, begin):
            zm = clamp(z - 1)
            zp = clamp(z + 1)
            w = [ref[plane(z), :] for ref in (wzm, wzp, wym, wyp, wxm, wxp)]
            for c in range(count):
                v = a[plane(c * D + z), :]
                total_ = w[0] * a[plane(c * D + zm), :] + w[1] * a[plane(c * D + zp), :]
                total_ += w[2] * pltpu.roll(v, 1, 0) + w[3] * pltpu.roll(v, H - 1, 0)
                total_ += w[4] * pltpu.roll(v, 1, 1) + w[5] * pltpu.roll(v, L - 1, 1)
                first = begin(c)
                t[plane(c * D + z), :] = total_ if first is None else total_ + first

        def inner1(z, _):
            kappa = kap[plane(z), :]
            inner(a0, 6, z, lambda c: kappa * f[plane(c * D + z), :])
            return 0

        each(D, inner1, 0, WIDTH['inner1'])
        sum_start("gx", sum_finish("core"))
        gotf = exchange(6, zsf, zrf, ysf, yrf, xsf, xrf)

        arrive(got0)
        x0 = [pair(xr0, 0), pair(xr0, 1)]
        outer_x = jnp.logical_or(lane == 0, lane == L - 1)

        hz = []
        hy = []
        for side, z in ((0, 0), (1, D - 1)):
            hz.append(0.5 * (nu[pl.ds(z * H, H), :] + zr0[side, pl.ds(6 * H, H), :]))
            hy.append(0.5 * (cell_rows(nu, 1, side * (H - 1)) + yr0[side, pl.ds(6 * D, D), :]))

        def add_outer(zr, yr, count):
            for side, z in ((0, 0), (1, D - 1)):
                for c in range(count):
                    t[pl.ds((c * D + z) * H, H), :] += hz[side] * zr[side, pl.ds(c * H, H), :]
                for c in range(count):
                    at = pl.ds(c * D * H + side * (H - 1), D, stride=H)
                    t[at, :] = t[at, :] + hy[side] * yr[side, pl.ds(c * D, D), :]

        add_outer(zr0, yr0, 6)
        for side, z in ((0, 0), (1, D - 1)):
            al[pl.ds(z * H, H), :] += hz[side]
            at = pl.ds(side * (H - 1), D, stride=H)
            al[at, :] = al[at, :] + hy[side]

        def finish(z, a, tiles_in, count):
            alpha = al[plane(z), :]
            beta = be[plane(z), :]
            face = hx[plane(z), :]
            outside = unpack(tiles_in[0], z, 4) + unpack(tiles_in[1], z, count - 4)
            tt = [t[plane(c * D + z), :] + face * outside[c] for c in range(count)]
            out = [None] * count
            pairs = [(0, 3), (1, 4), (2, 5)] + ([(6, 7)] if count == 8 else [])
            for re, im in pairs:
                out[re] = (1.0 - RELAX) * a[plane(re * D + z), :] + (tt[re] * alpha + tt[im] * beta)
                out[im] = (1.0 - RELAX) * a[plane(im * D + z), :] + (tt[im] * alpha - tt[re] * beta)
            return out

        def sweep1(z, tiles):
            if z == 13:
                sum_start("gy", sum_finish("gx"))
            face = jnp.where(outer_x, 0.5 * (nu[plane(z), :] + unpack(x0[1], z, 1, 2)[0]), 0.0)
            hx[plane(z), :] = face
            d = al[plane(z), :] + face
            kappa = kap[plane(z), :]
            weight = RELAX / (d * d + kappa * kappa)
            al[plane(z), :] = d * weight
            be[plane(z), :] = kappa * weight
            out = finish(z, a0, x0, 6)
            mask = prt[plane(z), :].astype(F32)
            out.append(mask * (d * weight))
            out.append(-mask * (kappa * weight))
            for c in range(8):
                a1[plane(c * D + z), :] = out[c]
            return pack(z, tiles, out)

        tiles = each(D, sweep1, (zero, zero), WIDTH['sweep1'])
        xs1[0] = tiles[0]
        xs1[1] = tiles[1]
        for side, z in ((0, 0), (1, D - 1)):
            for c in range(8):
                zs1[side, pl.ds(c * H, H), :] = a1[pl.ds((c * D + z) * H, H), :]
            ys1[side] = cell_rows(a1, 8, side * (H - 1))
        got1 = exchange(12, zs1, zr1, ys1, yr1, xs1, xr1)

        def inner2(z, _):
            kappa = kap[plane(z), :]

            def begin(c):
                if c < 6:
                    return kappa * f[plane(c * D + z), :]
                return prt[plane(z), :].astype(F32) if c == 6 else None

            inner(a1, 8, z, begin)
            return 0

        each(D, inner2, 0, WIDTH['inner2'])
        for load in loads[5:]:
            load.wait()
        ry_l = jnp.zeros((H, L), jnp.int32)
        rz_l = jnp.zeros((H, L), jnp.int32)
        ry_r = jnp.zeros((H, L), jnp.int32)
        for b in range(H):
            ry_b = ry[gy * H + b]
            rz_b = rz[gz * D + b]
            ry_l = jnp.where(lax.rem(lane, H) == b, ry_b, ry_l)
            rz_l = jnp.where(lane // 8 == b, rz_b, rz_l)
            ry_r = jnp.where(row == b, ry_b, ry_r)

        def build(k, _):
            n = k // 8
            q = mod(k, 8)
            band_y = jnp.maximum(ry_l + 1 - jnp.abs(lax.rem(lane, H) - (row + (n - 1) * H)), 0)
            ky[plane(k), :] = jnp.where(lane // H == q, band_y, 0).astype(F32).astype(BF16)
            band_z = jnp.maximum(rz_l + 1 - jnp.abs(lane // 8 - (2 * q + row // 8 + (n - 1) * D)), 0)
            kz[plane(k), :] = jnp.where(lax.rem(lane, 8) == lax.rem(row, 8), band_z, 0).astype(F32).astype(BF16)
            return 0

        each(24, build, 0, WIDTH['build'])
        rx_own = jnp.broadcast_to(rx[pl.ds(gx, 1), :], (H, L))
        rx_low = jnp.broadcast_to(rx[pl.ds(jnp.maximum(gx - 1, 0), 1), :], (H, L))
        rx_high = jnp.broadcast_to(rx[pl.ds(jnp.minimum(gx + 1, nx - 1), 1), :], (H, L))

        def build_x(k, _):
            target = row + k * H
            own = jnp.maximum(rx_own + 1 - jnp.abs(lane - target), 0)
            low = jnp.maximum(rx_low + 1 - jnp.abs(lane - L - target), 0)
            high = jnp.maximum(rx_high + 1 - jnp.abs(lane + L - target), 0)
            bx[plane(k), pl.ds(0, L)] = own.astype(F32).astype(BF16)
            bx[plane(k), pl.ds(L, L)] = jnp.where(lane < L // 2, high, low).astype(F32).astype(BF16)
            return 0

        each(L // H, build_x, 0, WIDTH['build_x'])
        norm_yx = (norm_of(ry_r, gy * H + row, total["gy"]) * norm_of(rx_own, gx * L + lane, total["gx"])).astype(F32)

        def material(z, _):
            density = den[plane(z), :]
            design = jnp.where(lab[plane(z), :] == 2, 1.0, 0.0).astype(F32)
            square = density * density
            cube = square * density
            nu_design = 1.0 / (1.0 + MU_GAIN * cube)
            gz_i = gz * D + z
            norm_z = norm_of(rz[gz_i], gz_i, total["gz"]).astype(F32)
            inverse = SENS_GAIN / (norm_yx * norm_z)
            nu_slope = -3.0 * MU_GAIN * design * square * nu_design * nu_design
            kk[plane(z), :] = -0.5 * nu_slope * inverse
            qq[plane(z), :] = 3.0 * KAPPA_GAIN * design * square * inverse
            return 0

        each(D, material, 0, WIDTH['material'])

        sum_start("gz", sum_finish("gy"))
        arrive(gotf)
        xf = [pair(xrf, 0), pair(xrf, 1)]

        def across_x(z, _):
            outside = unpack(xf[0], z, 4) + unpack(xf[1], z, 2)
            for c in range(6):
                at = plane(c * D + z)
                near_x[at, :] = jnp.where(outer_x, f[at, :] - outside[c], 0.0)
            return 0

        each(D, across_x, 0, WIDTH['across_x'])
        arrive(got1)
        add_outer(zr1, yr1, 8)
        x1 = [pair(xr1, 0), pair(xr1, 1)]

        def shares(answers, near):
            main = None
            for c in range(6):
                term = answers[c] * near[c]
                main = term if c == 0 else main + term if c < 3 else main - term
            return [main, answers[6] * near[2] - answers[7] * near[5], -(answers[7] * near[2]) - answers[6] * near[5]]

        def sweep2(z, tile):
            out = finish(z, a1, x1, 8)
            for c in range(8):
                a2[plane(c * D + z), :] = out[c]
            share = shares(out, [near_x[plane(c * D + z), :] for c in range(6)])
            for k in range(3):
                t[plane(k * D + z), :] = share[k]
            return pack(z, (tile,), share)[0]

        xs2[0] = each(D, sweep2, zero, WIDTH['sweep2'])
        hz2 = []
        hy2 = []
        for side, z in ((0, 0), (1, D - 1)):
            at = [pl.ds((c * D + z) * H, H) for c in range(8)]
            near = [f[at[c], :] - zrf[side, pl.ds(c * H, H), :] for c in range(6)]
            share = shares([a2[where, :] for where in at], near)
            for k in range(3):
                zs2[side, pl.ds(k * H, H), :] = share[k]
            hz2.append(share)
            at = [pl.ds(c * D * H + side * (H - 1), D, stride=H) for c in range(8)]
            near = [f[at[c], :] - yrf[side, pl.ds(c * D, D), :] for c in range(6)]
            share = shares([a2[where, :] for where in at], near)
            for k in range(3):
                ys2[side, pl.ds(k * D, D), :] = share[k]
            hy2.append(share)
        got2 = exchange(18, zs2, zr2, ys2, yr2, xs2, xr2)

        def sens(z, last):
            zp = clamp(z + 1)
            av = [a2[plane(c * D + z), :] for c in range(8)]
            fv = [f[plane(c * D + z), :] for c in range(6)]
            above = [a2[plane(c * D + zp), :] for c in range(8)], [f[plane(c * D + zp), :] for c in range(6)]
            ez = shares([v - w for v, w in zip(av, above[0])], [v - w for v, w in zip(fv, above[1])])
            ey = shares([v - pltpu.roll(v, H - 1, 0) for v in av], [v - pltpu.roll(v, H - 1, 0) for v in fv])
            ex = shares([v - pltpu.roll(v, L - 1, 1) for v in av], [v - pltpu.roll(v, L - 1, 1) for v in fv])
            more = [zero, av[6] * fv[5] + av[7] * fv[2], av[6] * fv[2] - av[7] * fv[5]]
            for c in range(6):
                more[0] = more[0] + fv[c] * (fv[c] + av[(c + 3) % 6])
            for k in range(3):
                along_y = jnp.where(row < H - 1, ey[k], 0.0)
                along_x = jnp.where(lane < L - 1, ex[k], 0.0)
                energy = ez[k] + last[k] + along_y + pltpu.roll(along_y, 1, 0)
                energy = energy + along_x + pltpu.roll(along_x, 1, 1) + t[plane(k * D + z), :]
                s[plane(k * D + z), :] = kk[plane(z), :] * energy + qq[plane(z), :] * more[k]
            return ez

        each(D, sens, [zero] * 3, WIDTH['sens'])
        total_ports = sum_finish("gz")
        link_re = scale * jnp.sum(total_ports[0:1])
        link_im = scale * jnp.sum(total_ports[1:2])
        imp_o[0] = link_re
        imp_o[1] = link_im
        coef_re = 2.0 * (link_re - zt[0])
        coef_im = -2.0 * (link_im - zt[1])

        def joined(parts):
            return parts[0] + (coef_re * parts[1] + coef_im * parts[2])

        def join(z, _):
            s[plane(z), :] = joined([s[plane(k * D + z), :] for k in range(3)])
            return 0

        each(D, join, 0, WIDTH['join'])
        for side, z in ((0, 0), (1, D - 1)):
            at = pl.ds(z * H, H)
            s[at, :] += kk[at, :] * joined(hz2[side])
            at = pl.ds(side * (H - 1), D, stride=H)
            s[at, :] = s[at, :] + kk[at, :] * joined(hy2[side])
        arrive(got2)
        for side, z in ((0, 0), (1, D - 1)):
            at = pl.ds(z * H, H)
            s[at, :] += kk[at, :] * joined([zr2[side, pl.ds(k * H, H), :] for k in range(3)])
            at = pl.ds(side * (H - 1), D, stride=H)
            s[at, :] = s[at, :] + kk[at, :] * joined([yr2[side, pl.ds(k * D, D), :] for k in range(3)])
        tile2 = pair(xr2, 0)
        tile2 = joined([tile2, pltpu.roll(tile2, L - 2, 1), pltpu.roll(tile2, L - 4, 1)])

        def add_x(z, _):
            outside = unpack(tile2, z, 1)[0]
            s[plane(z), :] += kk[plane(z), :] * jnp.where(outer_x, outside, 0.0)
            return 0

        each(D, add_x, 0, WIDTH['add_x'])

        lane8 = lax.broadcasted_iota(jnp.int32, (8, L), 1)
        left = lane < L // 2
        left8 = lane8 < L // 2

        def turn(v):
            return pltpu.roll(v, L // 2, 1)

        def split(v):
            high = v.astype(BF16)
            return high, (v - high.astype(F32)).astype(BF16)

        def keep(ref, k, v):
            high, low = split(v)
            ref[pl.ds(k * H, H), pl.ds(0, L)] = high
            ref[pl.ds(k * H, H), pl.ds(L, L)] = low

        def stack(a, b):
            return jnp.concatenate([a, b], axis=0)

        def band(matrix, value, n, dst):
            both = jnp.dot(matrix[pl.ds(n * L, L), :], value[...], preferred_element_type=F32)
            dst[...] = both[:, :L] + both[:, L:]

        def band_out(matrix, value, axis, src, dst, own, slot):
            band(matrix, value, 0, src.at[0])
            band(matrix, value, 2, src.at[1])
            got = [beside(axis, d, src.at[side], dst.at[1 - side], slot + side) for side, d in ((0, -1), (1, 1))]
            band(matrix, value, 1, own)
            return got

        for p in range(8):
            keep(vbA, p, jnp.where(left, s[plane(p), :], turn(s[plane(p + 8), :])))
        gotY = band_out(ky, vbA, "gy", ysF, yrF, oyF, 24)
        for k in range(8):
            tiles = []
            for z in (2 * k, 2 * k + 1):
                v = s[plane(z), :]
                tiles.append(jnp.where(left8, turn(v[:8]), v[8:]))
            keep(vbB, k, stack(*tiles))
        gotZ = band_out(kz, vbB, "gz", zsF, zrF, ozF, 26)

        def answer(z, _):
            re, im = a2[plane(6 * D + z), :], a2[plane(7 * D + z), :]
            added = {2: coef_re * re - coef_im * im, 5: coef_re * im + coef_im * re}
            for c in added:
                a2[plane(c * D + z), :] += added[c]
            return 0

        each(D, answer, 0, WIDTH['answer'])
        adj_copy = pltpu.make_async_copy(a2.at[pl.ds(0, 6 * D * H), :], adj_o, out_sem)
        adj_copy.start()

        def eight(ref, k):
            return ref[pl.ds(8 * k, 8), :]

        arrive(gotZ)
        vz = [eight(ozF, z) + eight(zrF.at[0], z) + eight(zrF.at[1], z) for z in range(D)]
        for p in range(8):
            low, high = vz[p], vz[p + 8]
            keep(vbB, p, stack(jnp.where(left8, low, turn(high)), jnp.where(left8, turn(low), high)))
        gotY2 = band_out(ky, vbB, "gy", ysG, yrG, oyG, 30)
        def columns(dst, src, count, rows_, offset, lanes):
            for g in range(count // 4):
                tile = None
                for q in range(4):
                    moved = pltpu.roll(src[pl.ds((4 * g + q) * rows_, rows_), :], (16 * q - offset) % L, 1)
                    tile = moved if q == 0 else jnp.where(lax.rem(lanes // REACH, 4) == q, moved, tile)
                dst[pl.ds(g * rows_, rows_), :] = tile

        def send_columns(axis, dx, st, sr, src, slot):
            got = []
            for n, d in ((0, 0), (1, -1), (2, 1)):
                if axis == "gz":
                    columns(st.at[n], src[n], D, 8, 0, lane8)
                else:
                    columns(st.at[n], src[n], 8, H, 48, lane)
                if d == 0:
                    got.append(beside("gx", dx, st.at[0], sr.at[0], slot))
                    continue
                go = jnp.logical_and(inside("gx", dx), inside(axis, d))
                come = jnp.logical_and(inside("gx", -dx), inside(axis, -d))
                copy = remote(st.at[n], sr.at[3 - n], slot + n, {axis: pos[axis] + d, "gx": gx + dx})
                pl.when(go)(copy.start)
                sent.append((go, copy))
                got.append((come, copy))
            return got

        gotX = send_columns("gy", 1, stB, srB, (oyG, ysG.at[0], ysG.at[1]), 35)
        arrive(gotY)
        vy = [oyF[plane(p), :] + yrF[0, plane(p), :] + yrF[1, plane(p), :] for p in range(8)]
        for k in range(4):
            near, far = [], []
            for p in (2 * k, 2 * k + 1):
                top, bottom = vy[p][:8], vy[p][8:]
                near.append(jnp.where(left8, top, turn(bottom)))
                far.append(jnp.where(left8, turn(top), bottom))
            keep(vbA, k, stack(*near))
            keep(vbA, k + 4, stack(*far))
        gotZ2 = band_out(kz, vbA, "gz", zsG, zrG, ozG, 28)

        gotX += send_columns("gz", -1, stA, srA, (ozG, zsG.at[0], zsG.at[1]), 32)
        arrive(gotZ2)
        vz = [eight(ozG, z) + eight(zrG.at[0], z) + eight(zrG.at[1], z) for z in range(D)]
        arrive(gotY2)
        arrive(gotX)
        ga = [sum(srA[n, pl.ds(8 * g, 8), :] for n in range(3)) for g in range(4)]
        gb = [sum(srB[n, plane(g), :] for n in range(3)) for g in range(2)]
        vy = [oyG[plane(p), :] + yrG[0, plane(p), :] + yrG[1, plane(p), :] for p in range(8)]
        for z in range(D):
            v = vz[z]
            own = jnp.where(left, stack(v, turn(v)), turn(vy[z]) if z < 8 else vy[z - 8])
            group = ga[z // 4]
            above = stack(*(pltpu.roll(group, (-16 * (z % 4) - 64 * h) % L, 1) for h in range(2)))
            below = pltpu.roll(gb[z % 8 // 4], (112 - 64 * (z // 8) - 16 * (z % 4)) % L, 1)
            for k, part in enumerate((own, jnp.where(left, above, below))):
                big, small = split(part)
                xin[plane(z), pl.ds(k * L, L)] = big
                xin[plane(z + D), pl.ds(k * L, L)] = small
        both = lax.dot_general(xin[...], bx[...], (((1,), (1,)), ((), ())), preferred_element_type=F32)
        grad_o[...] = both[:D * H] + both[D * H:]

        for cond, copy in sent:
            pl.when(cond)(copy.wait_send)
        for stage in stages:
            for d in range(1, stages[stage][0]):
                sum_copy(stage, d, False).wait_send()
        adj_copy.wait()

    return kernel


def solution(mesh):
    sizes = dict(mesh.shape)
    nz, ny, nx = (sizes[a] for a in AXES)
    rows = D * H
    vm = lambda *shape: pltpu.VMEM(shape, F32)
    field = vm(rows, L)

    def halo(planes, tiles):
        y = vm(2, planes * D, L)
        z = vm(2, planes * H, L)
        return [z, y, vm(tiles, H, L), z, y, vm(2, tiles, H, L)]

    scratch = [
        vm(6 * rows, L), pltpu.SMEM((2,), F32), pltpu.SMEM((nz * D,), jnp.int32), pltpu.SMEM((ny * H,), jnp.int32),
        pltpu.VMEM((nx, L), jnp.int32),
        vm(6 * rows + H, L), vm(6 * rows + H, L), field, pltpu.VMEM((rows, L), jnp.int32), pltpu.VMEM((rows, L), jnp.int32),
        vm(8 * rows + H, L), vm(8 * rows + H, L), vm(8 * rows + H, L),
    ] + [vm(rows + H, L)] * 13 + [vm(3 * rows + H, L)] + halo(7, 2) + halo(6, 2) + halo(8, 2) + [
        vm(2, 3 * H, L), vm(2, 3 * D, L), vm(1, H, L), vm(2, 3 * H, L), vm(2, 3 * D, L), vm(2, 1, H, L),
        pltpu.VMEM((3 * L, L), BF16), pltpu.VMEM((3 * L, L), BF16), pltpu.VMEM((L, 2 * L), BF16),
    ] + [vm(2, L, L)] * 8 + [vm(L, L)] * 4 + [vm(3, 32, L)] * 4 + [
        pltpu.VMEM((L, 2 * L), BF16), pltpu.VMEM((L, 2 * L), BF16), pltpu.VMEM((2 * rows, 2 * L), BF16),
    ] + [vm(n, 2, L) for n in (CORES, nx, ny, nz // CORES)] + [
        pltpu.SemaphoreType.DMA((9,)), pltpu.SemaphoreType.DMA,
        pltpu.SemaphoreType.DMA((38,)), pltpu.SemaphoreType.DMA((38,)),
    ] + [pltpu.SemaphoreType.DMA((n,)) for n in (CORES, nx, ny, nz // CORES) for _ in range(2)]
    hbm = pl.BlockSpec(memory_space=pl.ANY)
    smem = pl.BlockSpec(memory_space=pltpu.SMEM)
    vmem = pl.BlockSpec(memory_space=pltpu.VMEM)
    call = pl.pallas_call(
        make_kernel(sizes),
        out_shape=(
            pltpu.VMEM((6 * rows, L), F32),
            pltpu.VMEM((rows, L), F32),
            jax.ShapeDtypeStruct((2,), F32),
        ),
        in_specs=[hbm] * 9,
        out_specs=(hbm, vmem, smem),
        scratch_shapes=scratch,
        compiler_params=pltpu.CompilerParams(
            collective_id=0, has_side_effects=True, vmem_limit_bytes=32 * 2**20),
    )

    def hand_over(adj_i, grad_i, imp_i, adj_o, grad_o, imp_o, imp, sem, imp_sem):
        first = pltpu.make_async_copy(imp_i, imp, imp_sem)
        copies = [
            pltpu.make_async_copy(src, dst, sem.at[k])
            for k, (src, dst) in enumerate(((adj_i, adj_o), (grad_i, grad_o), (imp, imp_o)))
        ]
        first.start()
        copies[0].start()
        copies[1].start()
        first.wait()
        copies[2].start()
        for copy in copies:
            copy.wait()

    results = pl.pallas_call(
        hand_over,
        out_shape=(
            jax.ShapeDtypeStruct((6 * rows, L), F32),
            jax.ShapeDtypeStruct((rows, L), F32),
            jax.ShapeDtypeStruct((2,), F32),
        ),
        in_specs=[hbm] * 3,
        out_specs=(hbm,) * 3,
        scratch_shapes=[pltpu.SMEM((2,), F32), pltpu.SemaphoreType.DMA((3,)), pltpu.SemaphoreType.DMA],
        compiler_params=pltpu.CompilerParams(vmem_limit_bytes=16 * 2**20))

    def body(forward, adjoint_prev, density, labels, ports, z_target, radius_z, radius_y, radius_x):
        arrays = (
            forward.reshape(6 * rows, L), adjoint_prev.reshape(6 * rows, L), density.reshape(rows, L),
            labels.reshape(rows, L), ports.reshape(rows, L), z_target, radius_z, radius_y,
            radius_x.reshape(nx, L))
        place = pltpu.with_memory_space_constraint
        made = call(*(place(v, pltpu.HBM) for v in arrays))
        adjoint, gradient, impedance = results(place(made[0], pltpu.VMEM), place(made[1], pltpu.VMEM), made[2])
        return adjoint.reshape(6, D, H, L), gradient.reshape(D, H, L), impedance

    in_specs = (P(None, *AXES),) * 2 + (P(*AXES),) * 3 + (P(),) * 4
    out_specs = (P(None, *AXES), P(*AXES), P())
    return jax.shard_map(body, mesh=mesh, in_specs=in_specs, out_specs=out_specs, check_vma=False)
```

```python
import jax
import jax.numpy as jnp
from jax import lax
from jax.experimental import pallas as pl
from jax.experimental.pallas import tpu as pltpu
from jax.sharding import PartitionSpec as P

MU_GAIN = 19.0
KAPPA_GAIN = 2.0
RELAX = 0.8
SENS_GAIN = 0.1
REACH = 16
CORES = 2
WIDTH = dict(add_x=16, add_y=16, add_z=8, build=4, build_x=4, faces=16, inner1=16, inner2=16, material=16, pack0=16, packf=16, sens=16, step=8, sweep1=16, sweep2=16, across_x=16, reluctivity=16, join=16, answer=16)
MESH = pl.DeviceIdType.MESH
AXES = ("gz", "gy", "gx")
F32 = jnp.float32
BF16 = jnp.bfloat16
D = 16
H = 16
L = 128


def plane(index):
    if isinstance(index, int):
        return pl.ds(index * H, H)
    return pl.ds(pl.multiple_of(index * H, H), H)


def each(count, step, carry, width):
    if width == count:
        for k in range(count):
            carry = step(k, carry)
        return carry

    def group(g, carry):
        for k in range(width):
            carry = step(g * width + k, carry)
        return carry

    return lax.fori_loop(0, count // width, group, carry)


def mod(a, b):
    return a % b if isinstance(a, int) else lax.rem(a, b)


def clamp(value):
    if isinstance(value, int):
        return min(max(value, 0), D - 1)
    return jnp.clip(value, 0, D - 1)


def tri(value):
    value = jnp.maximum(value, 0)
    return value * (value + 1) // 2


def norm_of(radius, position, length):
    whole = (radius + 1) * (radius + 1)
    return whole - tri(radius - position) - tri(radius - (length - 1 - position))


def make_kernel(sizes):
    nz, ny, nx = sizes["gz"], sizes["gy"], sizes["gx"]
    total = {"gz": nz * D, "gy": ny * H, "gx": nx * L}
    scale = 4.0 / (total["gz"] * total["gy"] * total["gx"])

    def kernel(fwd_h, adj_h, den_h, lab_h, prt_h, zt_h, rz_h, ry_h, rx_h,
               adj_o, grad_o, imp_o,
               near_x, zt, rz, ry, rx, f, a0, den, lab, prt, a1, a2, t,
               nu, kap, wzm, wzp, wym, wyp, wxm, wxp, al, be, hx, kk, qq, s,
               zs0, ys0, xs0, zr0, yr0, xr0,
               zsf, ysf, xsf, zrf, yrf, xrf,
               zs1, ys1, xs1, zr1, yr1, xr1,
               zs2, ys2, xs2, zr2, yr2, xr2,
               ky, kz, bx, ysF, yrF, zsF, zrF, ysG, yrG, zsG, zrG, oyF, ozF, oyG, ozG,
               stA, srA, stB, srB, vbA, vbB, xin,
               sum_core, sum_x, sum_y, sum_z, in_sem, out_sem, ss, rs,
               ss_core, rs_core, ss_x, rs_x, ss_y, rs_y, ss_z, rs_z):
        sums = {"core": sum_core, "gx": sum_x, "gy": sum_y, "gz": sum_z}
        sum_ss = {"core": ss_core, "gx": ss_x, "gy": ss_y, "gz": ss_z}
        sum_rs = {"core": rs_core, "gx": rs_x, "gy": rs_y, "gz": rs_z}
        gz, gy, gx = (lax.axis_index(a) for a in AXES)
        pos = {"gz": gz, "gy": gy, "gx": gx}
        core = lax.rem(gz, CORES)

        def inside(axis, d):
            size = {"gz": nz, "gy": ny, "gx": nx}[axis]
            return pos[axis] < size - 1 if d > 0 else pos[axis] > 0

        stages = {
            "core": (CORES, lambda d: {"gz": gz - core + lax.rem(core + d, CORES)}, core),
            "gx": (nx, lambda d: {"gx": lax.rem(gx + d, nx)}, gx),
            "gy": (ny, lambda d: {"gy": lax.rem(gy + d, ny)}, gy),
            "gz": (nz // CORES, lambda d: {"gz": lax.rem(gz + CORES * d, nz)}, gz // CORES),
        }
        barrier = pltpu.get_barrier_semaphore()
        others = []
        for axis, dx in (("gz", 1), ("gy", -1)):
            for d in (-1, 1):
                others.append(({axis: pos[axis] + d, "gx": gx + dx},
                               jnp.logical_and(inside(axis, d), inside("gx", dx)),
                               jnp.logical_and(inside(axis, -d), inside("gx", -dx))))
        for d in (-1, 1):
            near = jnp.logical_and(inside("gz", d), (core == 0) if d < 0 else (core == CORES - 1))
            others.append(({"gz": gz + d}, near, near))
        expected = 0
        for members, peer, _ in reversed(stages.values()):
            for d in sorted(range(1, members), key=lambda d: abs(d - members / 2)):
                pl.semaphore_signal(barrier, inc=1, device_id=peer(d), device_id_type=MESH)
                expected += 1
        for where, comes, goes in others:
            @pl.when(comes)
            def _():
                pl.semaphore_signal(barrier, inc=1, device_id=where, device_id_type=MESH)
            expected = expected + goes.astype(jnp.int32)

        loads = [
            pltpu.make_async_copy(src, dst, in_sem.at[k])
            for k, (src, dst) in enumerate((
                (den_h, den), (lab_h, lab), (adj_h, a0.at[pl.ds(0, 6 * D * H), :]),
                (fwd_h, f.at[pl.ds(0, 6 * D * H), :]), (prt_h, prt),
                (rx_h, rx), (ry_h, ry), (rz_h, rz), (zt_h, zt)))
        ]
        for load in loads[5:] + loads[:5]:
            load.start()

        def remote(src, dst, slot, where):
            return pltpu.make_async_remote_copy(
                src_ref=src, dst_ref=dst, send_sem=ss.at[slot], recv_sem=rs.at[slot],
                device_id=where, device_id_type=MESH)

        sent = []

        def beside(axis, d, src, dst, slot):
            copy = remote(src, dst, slot, {axis: pos[axis] + d})
            pl.when(inside(axis, d))(copy.start)
            sent.append((inside(axis, d), copy))
            return (inside(axis, -d), copy)

        def arrive(copies):
            for cond, copy in copies:
                pl.when(cond)(copy.wait_recv)

        def exchange(base, zs, zr, ys, yr, xs, xr):
            copies = []
            for axis, src, dst, k in (("gy", ys, yr, 2), ("gz", zs, zr, 0), ("gx", xs, xr, 4)):
                for d in (-1, 1):
                    side = 0 if d < 0 else 1
                    piece = src if axis == "gx" else src.at[side]
                    copies.append(beside(axis, d, piece, dst.at[1 - side], base + k + side))
            return copies

        edges = {axis: (pos[axis] == 0, pos[axis] == {"gz": nz, "gy": ny, "gx": nx}[axis] - 1) for axis in AXES}
        for axis, bufs in (("gz", (zr0, zrf, zr1, zr2, zrF, zrG)), ("gy", (yr0, yrf, yr1, yr2, yrF, yrG)),
                           ("gx", (xr0, xrf, xr1, xr2))):
            for side in (0, 1):
                @pl.when(edges[axis][side])
                def _():
                    for buf in bufs:
                        buf[side] = jnp.zeros(buf.shape[1:], F32)
                    if axis == "gx":
                        column = lax.rem(lax.broadcasted_iota(jnp.int32, (H, L), 1), 8)
                        xr0[side, 1] = jnp.where(column // 2 == 2, 1.0, 0.0).astype(F32)
                    else:
                        buf = zr0 if axis == "gz" else yr0
                        buf[side, pl.ds(6 * H, H), :] = jnp.ones((H, L), F32)
        for strip, axis, side in ((srA, "gz", 1), (srB, "gy", 0)):
            for cond, slots in ((edges["gx"][side], (0, 1, 2)), (edges[axis][0], (1,)), (edges[axis][1], (2,))):
                @pl.when(cond)
                def _():
                    for slot in slots:
                        strip[slot] = jnp.zeros(strip.shape[1:], F32)

        lane = lax.broadcasted_iota(jnp.int32, (H, L), 1)
        row = lax.broadcasted_iota(jnp.int32, (H, L), 0)

        loads[0].wait()
        loads[1].wait()

        def reluctivity(z, _):
            density = den[plane(z), :]
            design = jnp.where(lab[plane(z), :] == 2, 1.0, 0.0).astype(F32)
            cube = density * density * density
            nu_design = 1.0 / (1.0 + MU_GAIN * cube)
            nu[plane(z), :] = 1.0 - design + design * nu_design
            kap[plane(z), :] = design * KAPPA_GAIN * cube
            return 0

        each(D, reluctivity, 0, WIDTH['reluctivity'])

        def pack(z, tiles, values):
            out = list(tiles)
            for c, v in enumerate(values):
                moved = pltpu.roll(v, (z * 8 + 2 * (c % 4) + 1) % L, 1)
                out[c // 4] = jnp.where(lane // 2 == z * 4 + c % 4, moved, out[c // 4])
            return tuple(out)

        def pair(xr, n):
            below = pltpu.roll(xr[0, n], 1, 1)
            above = pltpu.roll(xr[1, n], L - 1, 1)
            return jnp.where(lax.rem(lane, 2) == 0, above, below)

        def unpack(tile, z, count, first=0):
            return [pltpu.roll(tile, (-z * 8 - 2 * c - 1) % L, 1) for c in range(first, first + count)]

        zero = jnp.zeros((H, L), F32)

        def cell_rows(ref, count, first):
            return ref[pl.ds(first, count * D, stride=H), :]

        loads[2].wait()
        for side, z in ((0, 0), (1, D - 1)):
            for c in range(6):
                zs0[side, pl.ds(c * H, H), :] = a0[pl.ds((c * D + z) * H, H), :]
            zs0[side, pl.ds(6 * H, H), :] = nu[pl.ds(z * H, H), :]
            ys0[side, pl.ds(0, 6 * D), :] = cell_rows(a0, 6, side * (H - 1))
            ys0[side, pl.ds(6 * D, D), :] = cell_rows(nu, 1, side * (H - 1))

        def pack0(z, tiles):
            return pack(z, tiles, [a0[plane(c * D + z), :] for c in range(6)] + [nu[plane(z), :]])

        tiles = each(D, pack0, (zero, zero), WIDTH['pack0'])
        xs0[0] = tiles[0]
        xs0[1] = tiles[1]

        pl.semaphore_wait(barrier, expected)
        got0 = exchange(0, zs0, zr0, ys0, yr0, xs0, xr0)

        def sum_copy(stage, d, arriving):
            members, peer, slot = stages[stage]
            at = lax.rem(slot + d, members) if arriving else slot
            ref = sums[stage].at[at]
            return pltpu.make_async_remote_copy(
                src_ref=ref, dst_ref=ref, send_sem=sum_ss[stage].at[d], recv_sem=sum_rs[stage].at[at],
                device_id=peer(d), device_id_type=MESH)

        def sum_start(stage, value):
            members, _, slot = stages[stage]
            sums[stage][slot] = value
            for d in range(1, members):
                sum_copy(stage, d, False).start()

        def sum_finish(stage):
            members = stages[stage][0]
            for d in range(1, members):
                sum_copy(stage, d, True).wait_recv()
            value = sums[stage][0]
            for q in range(1, members):
                value = value + sums[stage][q]
            return value

        loads[3].wait()
        loads[4].wait()
        for side, z in ((0, 0), (1, D - 1)):
            for c in range(6):
                zsf[side, pl.ds(c * H, H), :] = f[pl.ds((c * D + z) * H, H), :]
            ysf[side] = cell_rows(f, 6, side * (H - 1))

        def packf(z, carry):
            tiles, re, im = carry
            values = [f[plane(c * D + z), :] for c in range(6)]
            mask = prt[plane(z), :].astype(F32)
            return (pack(z, tiles, values), re + mask * values[2], im + mask * values[5])

        tiles, port_re, port_im = each(D, packf, ((zero, zero), zero, zero), WIDTH['packf'])
        xsf[0] = tiles[0]
        xsf[1] = tiles[1]
        port_sum = jnp.concatenate(
            [jnp.sum(port_re, axis=0, keepdims=True), jnp.sum(port_im, axis=0, keepdims=True)], axis=0)

        sum_start("core", port_sum)

        def faces(z, _):
            v = nu[plane(z), :]
            below = nu[plane(clamp(z - 1)), :]
            above = nu[plane(clamp(z + 1)), :]
            wzm[plane(z), :] = jnp.where(z > 0, 0.5 * (v + below), 0.0)
            wzp[plane(z), :] = jnp.where(z < D - 1, 0.5 * (v + above), 0.0)
            wym[plane(z), :] = jnp.where(row > 0, 0.5 * (v + pltpu.roll(v, 1, 0)), 0.0)
            wyp[plane(z), :] = jnp.where(row < H - 1, 0.5 * (v + pltpu.roll(v, H - 1, 0)), 0.0)
            wxm[plane(z), :] = jnp.where(lane > 0, 0.5 * (v + pltpu.roll(v, 1, 1)), 0.0)
            wxp[plane(z), :] = jnp.where(lane < L - 1, 0.5 * (v + pltpu.roll(v, L - 1, 1)), 0.0)
            inner_sum = wzm[plane(z), :] + wzp[plane(z), :] + wym[plane(z), :] + wyp[plane(z), :]
            al[plane(z), :] = inner_sum + wxm[plane(z), :] + wxp[plane(z), :]
            return 0

        each(D, faces, 0, WIDTH['faces'])

        def inner(a, count, z, begin):
            zm = clamp(z - 1)
            zp = clamp(z + 1)
            w = [ref[plane(z), :] for ref in (wzm, wzp, wym, wyp, wxm, wxp)]
            for c in range(count):
                v = a[plane(c * D + z), :]
                total_ = w[0] * a[plane(c * D + zm), :] + w[1] * a[plane(c * D + zp), :]
                total_ += w[2] * pltpu.roll(v, 1, 0) + w[3] * pltpu.roll(v, H - 1, 0)
                total_ += w[4] * pltpu.roll(v, 1, 1) + w[5] * pltpu.roll(v, L - 1, 1)
                first = begin(c)
                t[plane(c * D + z), :] = total_ if first is None else total_ + first

        def inner1(z, _):
            kappa = kap[plane(z), :]
            inner(a0, 6, z, lambda c: kappa * f[plane(c * D + z), :])
            return 0

        each(D, inner1, 0, WIDTH['inner1'])
        sum_start("gx", sum_finish("core"))
        gotf = exchange(6, zsf, zrf, ysf, yrf, xsf, xrf)

        arrive(got0)
        x0 = [pair(xr0, 0), pair(xr0, 1)]
        outer_x = jnp.logical_or(lane == 0, lane == L - 1)

        hz = []
        hy = []
        for side, z in ((0, 0), (1, D - 1)):
            hz.append(0.5 * (nu[pl.ds(z * H, H), :] + zr0[side, pl.ds(6 * H, H), :]))
            hy.append(0.5 * (cell_rows(nu, 1, side * (H - 1)) + yr0[side, pl.ds(6 * D, D), :]))

        def add_outer(zr, yr, count):
            for side, z in ((0, 0), (1, D - 1)):
                for c in range(count):
                    t[pl.ds((c * D + z) * H, H), :] += hz[side] * zr[side, pl.ds(c * H, H), :]
                for c in range(count):
                    at = pl.ds(c * D * H + side * (H - 1), D, stride=H)
                    t[at, :] = t[at, :] + hy[side] * yr[side, pl.ds(c * D, D), :]

        add_outer(zr0, yr0, 6)
        for side, z in ((0, 0), (1, D - 1)):
            al[pl.ds(z * H, H), :] += hz[side]
            at = pl.ds(side * (H - 1), D, stride=H)
            al[at, :] = al[at, :] + hy[side]

        def finish(z, a, tiles_in, count):
            alpha = al[plane(z), :]
            beta = be[plane(z), :]
            face = hx[plane(z), :]
            outside = unpack(tiles_in[0], z, 4) + unpack(tiles_in[1], z, count - 4)
            tt = [t[plane(c * D + z), :] + face * outside[c] for c in range(count)]
            out = [None] * count
            pairs = [(0, 3), (1, 4), (2, 5)] + ([(6, 7)] if count == 8 else [])
            for re, im in pairs:
                out[re] = (1.0 - RELAX) * a[plane(re * D + z), :] + (tt[re] * alpha + tt[im] * beta)
                out[im] = (1.0 - RELAX) * a[plane(im * D + z), :] + (tt[im] * alpha - tt[re] * beta)
            return out

        def sweep1(z, tiles):
            if z == 13:
                sum_start("gy", sum_finish("gx"))
            face = jnp.where(outer_x, 0.5 * (nu[plane(z), :] + unpack(x0[1], z, 1, 2)[0]), 0.0)
            hx[plane(z), :] = face
            d = al[plane(z), :] + face
            kappa = kap[plane(z), :]
            weight = RELAX / (d * d + kappa * kappa)
            al[plane(z), :] = d * weight
            be[plane(z), :] = kappa * weight
            out = finish(z, a0, x0, 6)
            mask = prt[plane(z), :].astype(F32)
            out.append(mask * (d * weight))
            out.append(-mask * (kappa * weight))
            for c in range(8):
                a1[plane(c * D + z), :] = out[c]
            return pack(z, tiles, out)

        tiles = each(D, sweep1, (zero, zero), WIDTH['sweep1'])
        xs1[0] = tiles[0]
        xs1[1] = tiles[1]
        for side, z in ((0, 0), (1, D - 1)):
            for c in range(8):
                zs1[side, pl.ds(c * H, H), :] = a1[pl.ds((c * D + z) * H, H), :]
            ys1[side] = cell_rows(a1, 8, side * (H - 1))
        got1 = exchange(12, zs1, zr1, ys1, yr1, xs1, xr1)

        def inner2(z, _):
            kappa = kap[plane(z), :]

            def begin(c):
                if c < 6:
                    return kappa * f[plane(c * D + z), :]
                return prt[plane(z), :].astype(F32) if c == 6 else None

            inner(a1, 8, z, begin)
            return 0

        each(D, inner2, 0, WIDTH['inner2'])
        for load in loads[5:]:
            load.wait()
        ry_l = jnp.zeros((H, L), jnp.int32)
        rz_l = jnp.zeros((H, L), jnp.int32)
        ry_r = jnp.zeros((H, L), jnp.int32)
        for b in range(H):
            ry_b = ry[gy * H + b]
            rz_b = rz[gz * D + b]
            ry_l = jnp.where(lax.rem(lane, H) == b, ry_b, ry_l)
            rz_l = jnp.where(lane // 8 == b, rz_b, rz_l)
            ry_r = jnp.where(row == b, ry_b, ry_r)

        def build(k, _):
            n = k // 8
            q = mod(k, 8)
            band_y = jnp.maximum(ry_l + 1 - jnp.abs(lax.rem(lane, H) - (row + (n - 1) * H)), 0)
            ky[plane(k), :] = jnp.where(lane // H == q, band_y, 0).astype(F32).astype(BF16)
            band_z = jnp.maximum(rz_l + 1 - jnp.abs(lane // 8 - (2 * q + row // 8 + (n - 1) * D)), 0)
            kz[plane(k), :] = jnp.where(lax.rem(lane, 8) == lax.rem(row, 8), band_z, 0).astype(F32).astype(BF16)
            return 0

        each(24, build, 0, WIDTH['build'])
        rx_own = jnp.broadcast_to(rx[pl.ds(gx, 1), :], (H, L))
        rx_low = jnp.broadcast_to(rx[pl.ds(jnp.maximum(gx - 1, 0), 1), :], (H, L))
        rx_high = jnp.broadcast_to(rx[pl.ds(jnp.minimum(gx + 1, nx - 1), 1), :], (H, L))

        def build_x(k, _):
            target = row + k * H
            own = jnp.maximum(rx_own + 1 - jnp.abs(lane - target), 0)
            low = jnp.maximum(rx_low + 1 - jnp.abs(lane - L - target), 0)
            high = jnp.maximum(rx_high + 1 - jnp.abs(lane + L - target), 0)
            bx[plane(k), pl.ds(0, L)] = own.astype(F32).astype(BF16)
            bx[plane(k), pl.ds(L, L)] = jnp.where(lane < L // 2, high, low).astype(F32).astype(BF16)
            return 0

        each(L // H, build_x, 0, WIDTH['build_x'])
        norm_yx = (norm_of(ry_r, gy * H + row, total["gy"]) * norm_of(rx_own, gx * L + lane, total["gx"])).astype(F32)

        def material(z, _):
            density = den[plane(z), :]
            design = jnp.where(lab[plane(z), :] == 2, 1.0, 0.0).astype(F32)
            square = density * density
            cube = square * density
            nu_design = 1.0 / (1.0 + MU_GAIN * cube)
            gz_i = gz * D + z
            norm_z = norm_of(rz[gz_i], gz_i, total["gz"]).astype(F32)
            inverse = SENS_GAIN / (norm_yx * norm_z)
            nu_slope = -3.0 * MU_GAIN * design * square * nu_design * nu_design
            kk[plane(z), :] = -0.5 * nu_slope * inverse
            qq[plane(z), :] = 3.0 * KAPPA_GAIN * design * square * inverse
            return 0

        each(D, material, 0, WIDTH['material'])

        arrive(gotf)
        xf = [pair(xrf, 0), pair(xrf, 1)]

        def across_x(z, _):
            outside = unpack(xf[0], z, 4) + unpack(xf[1], z, 2)
            for c in range(6):
                at = plane(c * D + z)
                near_x[at, :] = jnp.where(outer_x, f[at, :] - outside[c], 0.0)
            return 0

        each(D, across_x, 0, WIDTH['across_x'])
        sum_start("gz", sum_finish("gy"))
        arrive(got1)
        add_outer(zr1, yr1, 8)
        x1 = [pair(xr1, 0), pair(xr1, 1)]

        def shares(answers, near):
            main = None
            for c in range(6):
                term = answers[c] * near[c]
                main = term if c == 0 else main + term if c < 3 else main - term
            return [main, answers[6] * near[2] - answers[7] * near[5], -(answers[7] * near[2]) - answers[6] * near[5]]

        def sweep2(z, tile):
            out = finish(z, a1, x1, 8)
            for c in range(8):
                a2[plane(c * D + z), :] = out[c]
            share = shares(out, [near_x[plane(c * D + z), :] for c in range(6)])
            for k in range(3):
                t[plane(k * D + z), :] = share[k]
            return pack(z, (tile,), share)[0]

        xs2[0] = each(D, sweep2, zero, WIDTH['sweep2'])
        hz2 = []
        hy2 = []
        for side, z in ((0, 0), (1, D - 1)):
            at = [pl.ds((c * D + z) * H, H) for c in range(8)]
            near = [f[at[c], :] - zrf[side, pl.ds(c * H, H), :] for c in range(6)]
            share = shares([a2[where, :] for where in at], near)
            for k in range(3):
                zs2[side, pl.ds(k * H, H), :] = share[k]
            hz2.append(share)
            at = [pl.ds(c * D * H + side * (H - 1), D, stride=H) for c in range(8)]
            near = [f[at[c], :] - yrf[side, pl.ds(c * D, D), :] for c in range(6)]
            share = shares([a2[where, :] for where in at], near)
            for k in range(3):
                ys2[side, pl.ds(k * D, D), :] = share[k]
            hy2.append(share)
        got2 = exchange(18, zs2, zr2, ys2, yr2, xs2, xr2)

        def sens(z, last):
            zp = clamp(z + 1)
            av = [a2[plane(c * D + z), :] for c in range(8)]
            fv = [f[plane(c * D + z), :] for c in range(6)]
            above = [a2[plane(c * D + zp), :] for c in range(8)], [f[plane(c * D + zp), :] for c in range(6)]
            ez = shares([v - w for v, w in zip(av, above[0])], [v - w for v, w in zip(fv, above[1])])
            ey = shares([v - pltpu.roll(v, H - 1, 0) for v in av], [v - pltpu.roll(v, H - 1, 0) for v in fv])
            ex = shares([v - pltpu.roll(v, L - 1, 1) for v in av], [v - pltpu.roll(v, L - 1, 1) for v in fv])
            more = [zero, av[6] * fv[5] + av[7] * fv[2], av[6] * fv[2] - av[7] * fv[5]]
            for c in range(6):
                more[0] = more[0] + fv[c] * (fv[c] + av[(c + 3) % 6])
            for k in range(3):
                along_y = jnp.where(row < H - 1, ey[k], 0.0)
                along_x = jnp.where(lane < L - 1, ex[k], 0.0)
                energy = ez[k] + last[k] + along_y + pltpu.roll(along_y, 1, 0)
                energy = energy + along_x + pltpu.roll(along_x, 1, 1) + t[plane(k * D + z), :]
                s[plane(k * D + z), :] = kk[plane(z), :] * energy + qq[plane(z), :] * more[k]
            return ez

        each(D, sens, [zero] * 3, WIDTH['sens'])
        total_ports = sum_finish("gz")
        link_re = scale * jnp.sum(total_ports[0:1])
        link_im = scale * jnp.sum(total_ports[1:2])
        imp_o[0] = link_re
        imp_o[1] = link_im
        coef_re = 2.0 * (link_re - zt[0])
        coef_im = -2.0 * (link_im - zt[1])

        def joined(parts):
            return parts[0] + (coef_re * parts[1] + coef_im * parts[2])

        def join(z, _):
            s[plane(z), :] = joined([s[plane(k * D + z), :] for k in range(3)])
            return 0

        each(D, join, 0, WIDTH['join'])
        for side, z in ((0, 0), (1, D - 1)):
            at = pl.ds(z * H, H)
            s[at, :] += kk[at, :] * joined(hz2[side])
            at = pl.ds(side * (H - 1), D, stride=H)
            s[at, :] = s[at, :] + kk[at, :] * joined(hy2[side])
        arrive(got2)
        for side, z in ((0, 0), (1, D - 1)):
            at = pl.ds(z * H, H)
            s[at, :] += kk[at, :] * joined([zr2[side, pl.ds(k * H, H), :] for k in range(3)])
            at = pl.ds(side * (H - 1), D, stride=H)
            s[at, :] = s[at, :] + kk[at, :] * joined([yr2[side, pl.ds(k * D, D), :] for k in range(3)])
        tile2 = pair(xr2, 0)
        tile2 = joined([tile2, pltpu.roll(tile2, L - 2, 1), pltpu.roll(tile2, L - 4, 1)])

        def add_x(z, _):
            outside = unpack(tile2, z, 1)[0]
            s[plane(z), :] += kk[plane(z), :] * jnp.where(outer_x, outside, 0.0)
            return 0

        each(D, add_x, 0, WIDTH['add_x'])

        lane8 = lax.broadcasted_iota(jnp.int32, (8, L), 1)
        left = lane < L // 2
        left8 = lane8 < L // 2

        def turn(v):
            return pltpu.roll(v, L // 2, 1)

        def split(v):
            high = v.astype(BF16)
            return high, (v - high.astype(F32)).astype(BF16)

        def keep(ref, k, v):
            high, low = split(v)
            ref[pl.ds(k * H, H), pl.ds(0, L)] = high
            ref[pl.ds(k * H, H), pl.ds(L, L)] = low

        def stack(a, b):
            return jnp.concatenate([a, b], axis=0)

        def band(matrix, value, n, dst):
            both = jnp.dot(matrix[pl.ds(n * L, L), :], value[...], preferred_element_type=F32)
            dst[...] = both[:, :L] + both[:, L:]

        def band_out(matrix, value, axis, src, dst, own, slot):
            band(matrix, value, 0, src.at[0])
            band(matrix, value, 2, src.at[1])
            got = [beside(axis, d, src.at[side], dst.at[1 - side], slot + side) for side, d in ((0, -1), (1, 1))]
            band(matrix, value, 1, own)
            return got

        for p in range(8):
            keep(vbA, p, jnp.where(left, s[plane(p), :], turn(s[plane(p + 8), :])))
        gotY = band_out(ky, vbA, "gy", ysF, yrF, oyF, 24)
        for k in range(8):
            tiles = []
            for z in (2 * k, 2 * k + 1):
                v = s[plane(z), :]
                tiles.append(jnp.where(left8, turn(v[:8]), v[8:]))
            keep(vbB, k, stack(*tiles))
        gotZ = band_out(kz, vbB, "gz", zsF, zrF, ozF, 26)

        def answer(z, _):
            re, im = a2[plane(6 * D + z), :], a2[plane(7 * D + z), :]
            added = {2: coef_re * re - coef_im * im, 5: coef_re * im + coef_im * re}
            for c in added:
                a2[plane(c * D + z), :] += added[c]
            return 0

        each(D, answer, 0, WIDTH['answer'])
        adj_copy = pltpu.make_async_copy(a2.at[pl.ds(0, 6 * D * H), :], adj_o, out_sem)
        adj_copy.start()

        def eight(ref, k):
            return ref[pl.ds(8 * k, 8), :]

        arrive(gotZ)
        vz = [eight(ozF, z) + eight(zrF.at[0], z) + eight(zrF.at[1], z) for z in range(D)]
        for p in range(8):
            low, high = vz[p], vz[p + 8]
            keep(vbB, p, stack(jnp.where(left8, low, turn(high)), jnp.where(left8, turn(low), high)))
        gotY2 = band_out(ky, vbB, "gy", ysG, yrG, oyG, 30)
        def columns(dst, src, count, rows_, offset, lanes):
            for g in range(count // 4):
                tile = None
                for q in range(4):
                    moved = pltpu.roll(src[pl.ds((4 * g + q) * rows_, rows_), :], (16 * q - offset) % L, 1)
                    tile = moved if q == 0 else jnp.where(lax.rem(lanes // REACH, 4) == q, moved, tile)
                dst[pl.ds(g * rows_, rows_), :] = tile

        def send_columns(axis, dx, st, sr, src, slot):
            got = []
            for n, d in ((0, 0), (1, -1), (2, 1)):
                if axis == "gz":
                    columns(st.at[n], src[n], D, 8, 0, lane8)
                else:
                    columns(st.at[n], src[n], 8, H, 48, lane)
                if d == 0:
                    got.append(beside("gx", dx, st.at[0], sr.at[0], slot))
                    continue
                go = jnp.logical_and(inside("gx", dx), inside(axis, d))
                come = jnp.logical_and(inside("gx", -dx), inside(axis, -d))
                copy = remote(st.at[n], sr.at[3 - n], slot + n, {axis: pos[axis] + d, "gx": gx + dx})
                pl.when(go)(copy.start)
                sent.append((go, copy))
                got.append((come, copy))
            return got

        gotX = send_columns("gy", 1, stB, srB, (oyG, ysG.at[0], ysG.at[1]), 35)
        arrive(gotY)
        vy = [oyF[plane(p), :] + yrF[0, plane(p), :] + yrF[1, plane(p), :] for p in range(8)]
        for k in range(4):
            near, far = [], []
            for p in (2 * k, 2 * k + 1):
                top, bottom = vy[p][:8], vy[p][8:]
                near.append(jnp.where(left8, top, turn(bottom)))
                far.append(jnp.where(left8, turn(top), bottom))
            keep(vbA, k, stack(*near))
            keep(vbA, k + 4, stack(*far))
        gotZ2 = band_out(kz, vbA, "gz", zsG, zrG, ozG, 28)

        gotX += send_columns("gz", -1, stA, srA, (ozG, zsG.at[0], zsG.at[1]), 32)
        arrive(gotZ2)
        vz = [eight(ozG, z) + eight(zrG.at[0], z) + eight(zrG.at[1], z) for z in range(D)]
        arrive(gotY2)
        arrive(gotX)
        ga = [sum(srA[n, pl.ds(8 * g, 8), :] for n in range(3)) for g in range(4)]
        gb = [sum(srB[n, plane(g), :] for n in range(3)) for g in range(2)]
        vy = [oyG[plane(p), :] + yrG[0, plane(p), :] + yrG[1, plane(p), :] for p in range(8)]
        for z in range(D):
            v = vz[z]
            own = jnp.where(left, stack(v, turn(v)), turn(vy[z]) if z < 8 else vy[z - 8])
            group = ga[z // 4]
            above = stack(*(pltpu.roll(group, (-16 * (z % 4) - 64 * h) % L, 1) for h in range(2)))
            below = pltpu.roll(gb[z % 8 // 4], (112 - 64 * (z // 8) - 16 * (z % 4)) % L, 1)
            for k, part in enumerate((own, jnp.where(left, above, below))):
                big, small = split(part)
                xin[plane(z), pl.ds(k * L, L)] = big
                xin[plane(z + D), pl.ds(k * L, L)] = small
        both = lax.dot_general(xin[...], bx[...], (((1,), (1,)), ((), ())), preferred_element_type=F32)
        grad_o[...] = both[:D * H] + both[D * H:]

        for cond, copy in sent:
            pl.when(cond)(copy.wait_send)
        for stage in stages:
            for d in range(1, stages[stage][0]):
                sum_copy(stage, d, False).wait_send()
        adj_copy.wait()

    return kernel


def solution(mesh):
    sizes = dict(mesh.shape)
    nz, ny, nx = (sizes[a] for a in AXES)
    rows = D * H
    vm = lambda *shape: pltpu.VMEM(shape, F32)
    field = vm(rows, L)

    def halo(planes, tiles):
        y = vm(2, planes * D, L)
        z = vm(2, planes * H, L)
        return [z, y, vm(tiles, H, L), z, y, vm(2, tiles, H, L)]

    scratch = [
        vm(6 * rows, L), pltpu.SMEM((2,), F32), pltpu.SMEM((nz * D,), jnp.int32), pltpu.SMEM((ny * H,), jnp.int32),
        pltpu.VMEM((nx, L), jnp.int32),
        vm(6 * rows + H, L), vm(6 * rows + H, L), field, pltpu.VMEM((rows, L), jnp.int32), pltpu.VMEM((rows, L), jnp.int32),
        vm(8 * rows + H, L), vm(8 * rows + H, L), vm(8 * rows + H, L),
    ] + [vm(rows + H, L)] * 13 + [vm(3 * rows + H, L)] + halo(7, 2) + halo(6, 2) + halo(8, 2) + [
        vm(2, 3 * H, L), vm(2, 3 * D, L), vm(1, H, L), vm(2, 3 * H, L), vm(2, 3 * D, L), vm(2, 1, H, L),
        pltpu.VMEM((3 * L, L), BF16), pltpu.VMEM((3 * L, L), BF16), pltpu.VMEM((L, 2 * L), BF16),
    ] + [vm(2, L, L)] * 8 + [vm(L, L)] * 4 + [vm(3, 32, L)] * 4 + [
        pltpu.VMEM((L, 2 * L), BF16), pltpu.VMEM((L, 2 * L), BF16), pltpu.VMEM((2 * rows, 2 * L), BF16),
    ] + [vm(n, 2, L) for n in (CORES, nx, ny, nz // CORES)] + [
        pltpu.SemaphoreType.DMA((9,)), pltpu.SemaphoreType.DMA,
        pltpu.SemaphoreType.DMA((38,)), pltpu.SemaphoreType.DMA((38,)),
    ] + [pltpu.SemaphoreType.DMA((n,)) for n in (CORES, nx, ny, nz // CORES) for _ in range(2)]
    hbm = pl.BlockSpec(memory_space=pl.ANY)
    smem = pl.BlockSpec(memory_space=pltpu.SMEM)
    vmem = pl.BlockSpec(memory_space=pltpu.VMEM)
    call = pl.pallas_call(
        make_kernel(sizes),
        out_shape=(
            pltpu.VMEM((6 * rows, L), F32),
            pltpu.VMEM((rows, L), F32),
            jax.ShapeDtypeStruct((2,), F32),
        ),
        in_specs=[hbm] * 9,
        out_specs=(hbm, vmem, smem),
        scratch_shapes=scratch,
        compiler_params=pltpu.CompilerParams(
            collective_id=0, has_side_effects=True, vmem_limit_bytes=32 * 2**20),
    )

    def hand_over(adj_i, grad_i, imp_i, adj_o, grad_o, imp_o, imp, sem, imp_sem):
        first = pltpu.make_async_copy(imp_i, imp, imp_sem)
        copies = [
            pltpu.make_async_copy(src, dst, sem.at[k])
            for k, (src, dst) in enumerate(((adj_i, adj_o), (grad_i, grad_o), (imp, imp_o)))
        ]
        first.start()
        copies[0].start()
        copies[1].start()
        first.wait()
        copies[2].start()
        for copy in copies:
            copy.wait()

    results = pl.pallas_call(
        hand_over,
        out_shape=(
            jax.ShapeDtypeStruct((6 * rows, L), F32),
            jax.ShapeDtypeStruct((rows, L), F32),
            jax.ShapeDtypeStruct((2,), F32),
        ),
        in_specs=[hbm] * 3,
        out_specs=(hbm,) * 3,
        scratch_shapes=[pltpu.SMEM((2,), F32), pltpu.SemaphoreType.DMA((3,)), pltpu.SemaphoreType.DMA],
        compiler_params=pltpu.CompilerParams(vmem_limit_bytes=16 * 2**20))

    def body(forward, adjoint_prev, density, labels, ports, z_target, radius_z, radius_y, radius_x):
        arrays = (
            forward.reshape(6 * rows, L), adjoint_prev.reshape(6 * rows, L), density.reshape(rows, L),
            labels.reshape(rows, L), ports.reshape(rows, L), z_target, radius_z, radius_y,
            radius_x.reshape(nx, L))
        place = pltpu.with_memory_space_constraint
        made = call(*(place(v, pltpu.HBM) for v in arrays))
        adjoint, gradient, impedance = results(place(made[0], pltpu.VMEM), place(made[1], pltpu.VMEM), made[2])
        return adjoint.reshape(6, D, H, L), gradient.reshape(D, H, L), impedance

    in_specs = (P(None, *AXES),) * 2 + (P(*AXES),) * 3 + (P(),) * 4
    out_specs = (P(None, *AXES), P(*AXES), P())
    return jax.shard_map(body, mesh=mesh, in_specs=in_specs, out_specs=out_specs, check_vma=False)
```
